32 devices in a mesh: dp: 16 (over z, x, core), fsdp: 2 (over y).
Axes of the slice: x: 2, y: 2, z: 4, core: 2. Of those that a mesh axis runs over, the one named last changes fastest.
Arguments:
- image_maps: bfloat16 [64, 8, 8, 3072], P(('dp', 'fsdp')), may hold values from -6 to 6
- dw_kernel: bfloat16 [49, 3072], P(None, 'fsdp'), may hold values from -0.5 to 0.55
- channel_terms: bfloat16 [4, 3072], P(None, 'fsdp'), may hold values from 0.099609375 to 1.8984375
- head_weight: bfloat16 [3072, 1152], P('fsdp'), may hold values from -0.5 to 0.5
- text_feats: bfloat16 [64, 1152], P(('dp', 'fsdp')), may hold values from -6 to 6
Outputs:
- image_grads: bfloat16 [64, 8, 8, 3072], P(('dp', 'fsdp'))
- kernel_grads: float32 [49, 3072], P(None, 'fsdp')
- term_grads: float32 [4, 3072], P(None, 'fsdp')
- head_grads: float32 [3072, 1152], P('fsdp')
- text_grads: float32 [64, 1152], P(('dp', 'fsdp'))
The draws below stay inside these ranges and needn't reach their ends.
All inputs are finite; a program needn't handle non-finite values.
Results may differ from the reference program's by a relative error of at most 0.017.
Values may be sent and summed in bfloat16 or wider, within the bound.
No kernel may reach another device: no remote copies, remote signals or barrier semaphores. Data moves between devices by JAX's collectives and lax.ppermute only.
A program may use at most 192 MiB of HBM per device.

```python
import math
import jax
import jax.numpy as jnp
from jax import lax

C = 3072
E = 1152
SIDE = 8
KER = 7
IMG_DEV = 2
IMAGES = 64
N_FSDP = 2


def shared_signs(key):
    picks = jax.random.bernoulli(jax.random.fold_in(key, 101), 0.5, (C,))
    return jnp.where(picks, 1.0, -1.0).astype(jnp.float32)


def draw_image_maps(key, part):
    channel_signs = shared_signs(key)
    key = jax.random.fold_in(key, 3)
    noise_key, flip_key = jax.random.split(key)
    noise = jnp.clip(jax.random.normal(noise_key, (IMAGES, SIDE, SIDE, C), jnp.float32), -3.5, 3.5)
    strength = 2.0
    image_signs = jnp.where(jax.random.bernoulli(flip_key, 0.5, (IMAGES,)), 1.0, -1.0).astype(jnp.float32)
    row_index = jnp.arange(SIDE)
    halves = jnp.where(row_index < SIDE // 2, 1.0, -1.0).astype(jnp.float32)
    pattern = strength * image_signs[:, None, None, None] * halves[None, :, None, None] * channel_signs[None, None, None, :]
    return (noise + pattern).astype(jnp.bfloat16)


def draw_dw_kernel(key, part):
    key = jax.random.fold_in(key, 5)
    taps = jnp.clip(jax.random.normal(key, (KER * KER, C), jnp.float32), -3.0, 3.0)
    offset = 0.08
    return (taps / KER + offset).astype(jnp.bfloat16)


def draw_head_weight(key, part):
    channel_signs = shared_signs(key)
    key = jax.random.fold_in(key, 7)
    random_key, along_key = jax.random.split(key)
    base = jnp.clip(jax.random.normal(random_key, (C, E), jnp.float32), -3.0, 3.0)
    tilt = 0.03
    along = jax.random.uniform(along_key, (E,), jnp.float32, -1.5, 1.5)
    return (base / math.sqrt(C) + tilt * channel_signs[:, None] * along[None, :]).astype(jnp.bfloat16)


def levels(stream_key, shape, cuts, low, top_value):
    level, own = 1.0, jax.random.fold_in(stream_key, 6)
    for dim, blocks in cuts:
        draws = jnp.exp(jax.random.uniform(jax.random.fold_in(own, dim), (blocks,), jnp.float32, low / len(cuts), top_value / len(cuts)))
        level = level * jnp.repeat(draws, shape[dim] // blocks).reshape([-1 if axis == dim else 1 for axis in range(len(shape))])
    return level


def normal_values(own_key, dims, deviation, most, shards=(), held_as=jnp.bfloat16):
    array = deviation * jax.random.normal(own_key, dims, jnp.float32)
    if shards:
        array = array * levels(own_key, dims, shards, -0.22, 0.18)
    return jnp.clip(array, -most, most).astype(held_as)


def setup_inputs(seed: int = 0) -> dict:
    key_list = jax.random.split(jax.random.key(seed), 6)
    image_maps = draw_image_maps(jax.random.fold_in(key_list[5], 71), 0)
    dw_kernel = draw_dw_kernel(jax.random.fold_in(key_list[5], 71), 0)
    channel_terms = jnp.clip(1.0 + 0.18 * jax.random.normal(key_list[2], (4, C), jnp.float32), 0.099609375, 1.8984375).astype(jnp.bfloat16)
    head_weight = draw_head_weight(jax.random.fold_in(key_list[5], 71), 0)
    text_feats = normal_values(key_list[4], (IMAGES, E), 1.0, 6.0, ((0, 32),))
    return dict(image_maps=image_maps, dw_kernel=dw_kernel, channel_terms=channel_terms, head_weight=head_weight, text_feats=text_feats)


EPS = 1e-06
LOGIT_SCALE = 10.0
LOGIT_BIAS = -2.0

def depthwise(inputs, kernel):
    ker_side = 7
    reach = ker_side // 2
    height = inputs.shape[1]
    width = inputs.shape[2]
    padded = jnp.pad(inputs, ((0, 0), (reach, reach), (reach, reach), (0, 0)))
    mixed = jnp.zeros_like(inputs)
    for row_tap in range(ker_side):
        for col_tap in range(ker_side):
            mixed = mixed + padded[:, row_tap:row_tap + height, col_tap:col_tap + width, :] * kernel[row_tap * ker_side + col_tap]
    return mixed

def block_pool(inputs, kernel, conv_bias, norm_gain, layer_scale):
    mixed = depthwise(inputs, kernel) + conv_bias
    row_mean = lax.optimization_barrier(jnp.mean(mixed, axis=3, keepdims=True))
    centered = mixed - row_mean
    row_var = lax.optimization_barrier(jnp.mean(centered * centered, axis=3, keepdims=True))
    output = inputs + layer_scale * (centered * lax.rsqrt(row_var + EPS) * norm_gain)
    return lax.optimization_barrier(jnp.mean(output, axis=(1, 2)))

def head_norm(pooled, head_gain):
    row_mean = lax.optimization_barrier(jnp.mean(pooled, axis=1, keepdims=True))
    centered = pooled - row_mean
    row_var = lax.optimization_barrier(jnp.mean(centered * centered, axis=1, keepdims=True))
    return centered * lax.rsqrt(row_var + EPS) * head_gain

def to_unit(vectors):
    return vectors * lax.rsqrt(lax.optimization_barrier(jnp.sum(vectors * vectors, axis=1, keepdims=True)) + EPS)

def reference(image_maps, dw_kernel, channel_terms, head_weight, text_feats):
    group_size = IMG_DEV * N_FSDP
    group_count = IMAGES // group_size
    kernel = dw_kernel.astype(jnp.float32)
    terms_all = channel_terms.astype(jnp.float32)
    image_groups = image_maps.reshape(group_count, group_size, SIDE, SIDE, C)

    def pool_group(images):
        return block_pool(images.astype(jnp.float32), kernel, terms_all[0], terms_all[1], terms_all[2])
    pooled = lax.map(pool_group, image_groups).reshape(IMAGES, C)
    normed, head_back = jax.vjp(head_norm, pooled, terms_all[3])
    pooled_bf = normed.astype(jnp.bfloat16)
    embed = jnp.dot(pooled_bf, head_weight, preferred_element_type=jnp.float32)
    unit_vec, unit_back = jax.vjp(to_unit, embed)
    unit_bf = unit_vec.astype(jnp.bfloat16)
    text_unit, text_back = jax.vjp(to_unit, text_feats.astype(jnp.float32))
    text_bf = text_unit.astype(jnp.bfloat16)
    logits = LOGIT_SCALE * lax.dot_general(unit_bf, text_bf, (((1,), (1,)), ((), ())), preferred_element_type=jnp.float32) + LOGIT_BIAS
    rows_here = lax.broadcasted_iota(jnp.int32, logits.shape, 0)
    cols_here = lax.broadcasted_iota(jnp.int32, logits.shape, 1)
    positive = jnp.where(rows_here == cols_here, 1.0, 0.0).astype(jnp.float32)
    weights = (jax.nn.sigmoid(logits) - positive).astype(jnp.bfloat16)
    unit_grad = LOGIT_SCALE * jnp.dot(weights, text_bf, preferred_element_type=jnp.float32)
    text_unit_grad = LOGIT_SCALE * lax.dot_general(weights, unit_bf, (((0,), (0,)), ((), ())), preferred_element_type=jnp.float32)
    text_grads = text_back(text_unit_grad)[0]
    embed_grad = unit_back(unit_grad)[0].astype(jnp.bfloat16)
    pooled_grad = lax.dot_general(embed_grad, head_weight, (((1,), (1,)), ((), ())), preferred_element_type=jnp.float32)
    head_grads = lax.dot_general(pooled_bf, embed_grad, (((0,), (0,)), ((), ())), preferred_element_type=jnp.float32)
    pool_grad, gain_grad = head_back(pooled_grad)
    pool_grads = pool_grad.reshape(group_count, group_size, C)

    def back_group(carry_sums, packed):
        images, cotangent = packed
        primal, pull_back = jax.vjp(block_pool, images.astype(jnp.float32), kernel, terms_all[0], terms_all[1], terms_all[2])
        image_grad, kernel_grad, bias_grad, norm_grad, scale_grad = pull_back(cotangent)
        sums = (carry_sums[0] + kernel_grad, carry_sums[1] + bias_grad, carry_sums[2] + norm_grad, carry_sums[3] + scale_grad)
        return (sums, image_grad.astype(jnp.bfloat16))
    start_sums = (jnp.zeros((KER * KER, C), jnp.float32), jnp.zeros((C,), jnp.float32), jnp.zeros((C,), jnp.float32), jnp.zeros((C,), jnp.float32))
    totals, image_grads = lax.scan(back_group, start_sums, (image_groups, pool_grads))
    kernel_grads = totals[0]
    term_grads = jnp.stack([totals[1], totals[2], totals[3], gain_grad])
    image_grads = image_grads.reshape(IMAGES, SIDE, SIDE, C)
    return (image_grads, kernel_grads, term_grads, head_grads, text_grads)
```

```python
import jax
import jax.numpy as jnp
from jax import lax
from jax.sharding import PartitionSpec as P

EPS = 1e-06
LOGIT_SCALE = 10.0
LOGIT_BIAS = -2.0
KER = 7
BF = jnp.bfloat16
F32 = jnp.float32


def swap(value, axis, mask):
    count = lax.axis_size(axis)
    return lax.ppermute(value, axis, [(source, source ^ mask) for source in range(count)])


def tree_gather(value, axis, masks):
    for mask in masks:
        value = jnp.concatenate([value, swap(value, axis, mask)], axis=0)
    return value


def bits_up(count):
    masks = []
    mask = 1
    while mask < count:
        masks.append(mask)
        mask *= 2
    return masks


def depthwise(inputs, kernel):
    reach = KER // 2
    height = inputs.shape[1]
    width = inputs.shape[2]
    padded = jnp.pad(inputs, ((0, 0), (reach, reach), (reach, reach), (0, 0)))
    mixed = jnp.zeros_like(inputs)
    for row_tap in range(KER):
        for col_tap in range(KER):
            mixed = (
                mixed
                + padded[:, row_tap : row_tap + height, col_tap : col_tap + width, :]
                * kernel[row_tap * KER + col_tap]
            )
    return mixed


def block_pool(inputs, kernel, conv_bias, norm_gain, layer_scale):
    mixed = depthwise(inputs, kernel) + conv_bias
    row_mean = jnp.mean(mixed, axis=3, keepdims=True)
    centered = mixed - row_mean
    row_var = jnp.mean(centered * centered, axis=3, keepdims=True)
    output = inputs + layer_scale * (centered * lax.rsqrt(row_var + EPS) * norm_gain)
    return jnp.mean(output, axis=(1, 2))


def head_norm(pooled, head_gain):
    row_mean = jnp.mean(pooled, axis=1, keepdims=True)
    centered = pooled - row_mean
    row_var = jnp.mean(centered * centered, axis=1, keepdims=True)
    return centered * lax.rsqrt(row_var + EPS) * head_gain


def to_unit(vectors):
    return vectors * lax.rsqrt(jnp.sum(vectors * vectors, axis=1, keepdims=True) + EPS)


def pick(value, index, width):
    return lax.dynamic_slice_in_dim(value, index * width, width, axis=value.ndim - 1)


def join_slices(pieces, member):
    count = len(pieces)
    if count == 1:
        return pieces[0]
    if count == 2:
        low = jnp.where(member == 0, pieces[0], pieces[1])
        high = jnp.where(member == 0, pieces[1], pieces[0])
        return jnp.concatenate([low, high], axis=-1)
    stacked = jnp.stack(pieces)
    return jnp.concatenate(
        [lax.dynamic_index_in_dim(stacked, member ^ s, keepdims=False) for s in range(count)], axis=-1
    )


def reduce_terms(value, member, core, members, dp_masks):
    rows, channels = value.shape
    share = channels // members
    half = share // 2
    split = value.reshape(rows, members, 2, half)
    keep = lax.dynamic_index_in_dim(split, core, axis=2, keepdims=False)
    give = lax.dynamic_index_in_dim(split, 1 - core, axis=2, keepdims=False).astype(BF)
    chip = keep.astype(BF).astype(F32) + swap(give, "dp", 1).astype(F32)
    total = lax.dynamic_index_in_dim(chip, member, axis=1, keepdims=False).astype(BF).astype(F32)
    for m in range(1, members):
        part = lax.dynamic_index_in_dim(chip, member ^ m, axis=1, keepdims=False).astype(BF)
        total = total + swap(part, "fsdp", m).astype(F32)
    for mask in dp_masks:
        sent = total.astype(BF)
        total = sent.astype(F32) + swap(sent, "dp", mask).astype(F32)
    sent = total.astype(BF)
    other = swap(sent, "dp", 1)
    low = jnp.where(core == 0, sent, other)
    high = jnp.where(core == 0, other, sent)
    return jnp.concatenate([low, high], axis=1).astype(F32)


def per_device(image_maps, dw_kernel, channel_terms, head_weight, text_feats):
    rows = image_maps.shape[0]
    members = lax.axis_size("fsdp")
    member = lax.axis_index("fsdp")
    core = lax.axis_index("dp") % 2
    pair_masks = bits_up(members)
    dp_masks = bits_up(lax.axis_size("dp"))
    down = dp_masks[::-1]
    share = head_weight.shape[0]

    weights = jnp.concatenate([dw_kernel, channel_terms], axis=0)
    weights = join_slices([weights] + [swap(weights, "fsdp", m) for m in range(1, members)], member)
    kernel = weights[: KER * KER].astype(F32)
    terms = weights[KER * KER :].astype(F32)

    text_unit, text_back = jax.vjp(to_unit, text_feats.astype(F32))
    own_text = text_unit.astype(BF)
    text_all = tree_gather(tree_gather(own_text, "fsdp", pair_masks), "dp", down)

    inputs = image_maps.astype(F32)
    pooled, block_back = jax.vjp(block_pool, inputs, kernel, terms[0], terms[1], terms[2])
    normed, head_back = jax.vjp(head_norm, pooled, terms[3])
    pooled_bf = normed.astype(BF)

    group = jnp.concatenate(
        [pick(pooled_bf, member, share)]
        + [swap(pick(pooled_bf, member ^ m, share), "fsdp", m) for m in range(1, members)],
        axis=0,
    )
    partial = jnp.dot(group, head_weight, preferred_element_type=F32)
    embed = partial
    for m in range(1, members):
        other = swap(partial, "fsdp", m)
        embed = embed + jnp.concatenate(
            [other[(k ^ m) * rows : (k ^ m) * rows + rows] for k in range(members)], axis=0
        )
    unit_vec, unit_back = jax.vjp(to_unit, embed)
    unit_bf = unit_vec.astype(BF)

    def pair_weights(images, texts):
        logits = (
            LOGIT_SCALE
            * lax.dot_general(images, texts, (((1,), (1,)), ((), ())), preferred_element_type=F32)
            + LOGIT_BIAS
        )
        here = lax.broadcasted_iota(jnp.int32, logits.shape, 0)
        there = lax.broadcasted_iota(jnp.int32, logits.shape, 1)
        positive = jnp.where(here == there, 1.0, 0.0).astype(F32)
        return (jax.nn.sigmoid(logits) - positive).astype(BF)

    unit_sum = LOGIT_SCALE * jnp.dot(
        pair_weights(unit_bf, text_all), text_all, preferred_element_type=F32
    )
    embed_grad = unit_back(unit_sum)[0].astype(BF)
    grad_part = lax.dot_general(
        embed_grad, head_weight, (((1,), (1,)), ((), ())), preferred_element_type=F32
    )
    pooled_grad = join_slices(
        [grad_part[:rows]]
        + [swap(grad_part[m * rows : m * rows + rows], "fsdp", m) for m in range(1, members)],
        member,
    )

    packed = tree_gather(jnp.concatenate([group, embed_grad, unit_bf], axis=1), "dp", down)
    group_all = packed[:, :share]
    width = embed_grad.shape[1]
    grad_all = packed[:, share : share + width]
    unit_all = packed[:, share + width :]

    pool_grad, gain_grad = head_back(pooled_grad)
    image_grad, kernel_grad, bias_grad, norm_grad, scale_grad = block_back(pool_grad)
    sums = jnp.concatenate(
        [kernel_grad, jnp.stack([bias_grad, norm_grad, scale_grad, gain_grad])], axis=0
    )
    sums = reduce_terms(sums, member, core, members, dp_masks[1:])

    head_grads = lax.dot_general(
        group_all, grad_all, (((0,), (0,)), ((), ())), preferred_element_type=F32
    )
    text_sum = LOGIT_SCALE * lax.dot_general(
        pair_weights(unit_all, own_text),
        unit_all,
        (((0,), (0,)), ((), ())),
        preferred_element_type=F32,
    )
    text_grads = text_back(text_sum)[0]
    return (
        image_grad.astype(BF),
        sums[: KER * KER],
        sums[KER * KER :],
        head_grads,
        text_grads,
    )


def solution(mesh):
    in_specs = (
        P(("dp", "fsdp"), None, None, None),
        P(None, "fsdp"),
        P(None, "fsdp"),
        P("fsdp", None),
        P(("dp", "fsdp"), None),
    )
    out_specs = (
        P(("dp", "fsdp"), None, None, None),
        P(None, "fsdp"),
        P(None, "fsdp"),
        P("fsdp", None),
        P(("dp", "fsdp"), None),
    )
    return jax.shard_map(
        per_device, mesh=mesh, in_specs=in_specs, out_specs=out_specs, check_vma=False
    )
```

```python
import jax
import jax.numpy as jnp
from jax import lax
from jax.experimental import pallas as pl
from jax.experimental.pallas import tpu as pltpu
from jax.sharding import PartitionSpec as P

EPS = 1e-06
LOGIT_SCALE = 10.0
LOGIT_BIAS = -2.0
KER = 7
REACH = KER // 2
TAPS = KER * KER
LANES = 128
ROWS_PAD = 64
BF = jnp.bfloat16
F32 = jnp.float32


def swap(value, axis, mask):
    count = lax.axis_size(axis)
    return lax.ppermute(value, axis, [(source, source ^ mask) for source in range(count)])


def tree_gather(value, axis, masks):
    for mask in masks:
        value = jnp.concatenate([value, swap(value, axis, mask)], axis=0)
    return value


def bits_up(count):
    masks = []
    mask = 1
    while mask < count:
        masks.append(mask)
        mask *= 2
    return masks


def params(mebibytes):
    return pltpu.CompilerParams(vmem_limit_bytes=mebibytes * 1024 * 1024)


VM = pl.BlockSpec(memory_space=pltpu.VMEM)
SM = pl.BlockSpec(memory_space=pltpu.SMEM)


def lane_block(index, width):
    return pl.ds(pl.multiple_of(index * width, LANES), width)


def shift_cols(value, step):
    if step == 0:
        return value
    width = value.shape[0]
    rolled = pltpu.roll(value, (-step) % width, 0)
    col = lax.broadcasted_iota(jnp.int32, value.shape, 0)
    inside = (col < width - step) if step > 0 else (col >= -step)
    return jnp.where(inside, rolled, 0.0)


def conv_rows(rows, tap_row, flip):
    height = len(rows)
    sums = [None] * height
    for b in range(KER):
        moved = [shift_cols(row, b - REACH) for row in rows]
        for a in range(KER):
            tap = (KER - 1 - a) * KER + (KER - 1 - b) if flip else a * KER + b
            weight = tap_row(tap)
            for h in range(max(0, REACH - a), min(height, height + REACH - a)):
                term = moved[h + a - REACH] * weight
                sums[h] = term if sums[h] is None else sums[h] + term
    return sums


def forward_kernel(members, member_ref, x_ref, *refs):
    kernel_refs, refs = refs[:members], refs[members:]
    term_refs, refs = refs[:members], refs[members:]
    piece_refs, refs = refs[:members], refs[members:]
    weight_ref, mixed_ref, mean_ref, rstd_ref, hatsum_ref, hat_ref, hrstd_ref, sum_ref, pool_ref = refs
    images, height, width, channels = x_ref.shape
    share = channels // members
    tiles = channels // LANES
    cells = height * width
    member = member_ref[0]
    for m in range(members):
        lanes = lane_block(member ^ m, share)
        weight_ref[0:TAPS, lanes] = kernel_refs[m][...].astype(F32)
        weight_ref[TAPS : TAPS + 4, lanes] = term_refs[m][...].astype(F32)
    sum_ref[...] = jnp.zeros_like(sum_ref)

    @pl.loop(0, tiles)
    def _(t):
        lanes = lane_block(t, LANES)
        bias = weight_ref[TAPS : TAPS + 1, lanes]
        for i in range(images):
            rows = [x_ref[i, h, :, lanes].astype(F32) for h in range(height)]
            sums = conv_rows(rows, lambda tap: weight_ref[tap : tap + 1, lanes], False)
            for h in range(height):
                value = sums[h] + bias
                mixed_ref[i, h, :, lanes] = value
                sum_ref[i, h] += value

    mean = jnp.sum(sum_ref[...], axis=-1, keepdims=True) * (1.0 / channels)
    mean_ref[...] = jnp.broadcast_to(mean, mean_ref.shape)
    sum_ref[...] = jnp.zeros_like(sum_ref)

    @pl.loop(0, tiles)
    def _(t):
        lanes = lane_block(t, LANES)
        for i in range(images):
            for h in range(height):
                value = mixed_ref[i, h, :, lanes] - mean_ref[i, h]
                sum_ref[i, h] += value * value

    var = jnp.sum(sum_ref[...], axis=-1, keepdims=True) * (1.0 / channels)
    rstd_ref[...] = jnp.broadcast_to(lax.rsqrt(var + EPS), rstd_ref.shape)

    @pl.loop(0, tiles)
    def _(t):
        lanes = lane_block(t, LANES)
        scale = weight_ref[TAPS + 1 : TAPS + 2, lanes] * weight_ref[TAPS + 2 : TAPS + 3, lanes]
        for i in range(images):
            hats = jnp.zeros((width, LANES), F32)
            plain = jnp.zeros((width, LANES), F32)
            for h in range(height):
                hats = hats + (mixed_ref[i, h, :, lanes] - mean_ref[i, h]) * rstd_ref[i, h]
                plain = plain + x_ref[i, h, :, lanes].astype(F32)
            hat_row = jnp.sum(hats, axis=0, keepdims=True)
            hatsum_ref[i : i + 1, lanes] = hat_row
            pool_ref[i : i + 1, lanes] = (
                jnp.sum(plain, axis=0, keepdims=True) + scale * hat_row
            ) * (1.0 / cells)

    pooled = pool_ref[...]
    centered = pooled - jnp.mean(pooled, axis=1, keepdims=True)
    head_rstd = lax.rsqrt(jnp.mean(centered * centered, axis=1, keepdims=True) + EPS)
    hat = centered * head_rstd
    hat_ref[...] = hat
    hrstd_ref[...] = jnp.broadcast_to(head_rstd, hrstd_ref.shape)
    pool_ref[...] = hat * weight_ref[TAPS + 3 : TAPS + 4, :]
    for m in range(members):
        piece_refs[m][...] = pool_ref[:, lane_block(member ^ m, share)].astype(BF)


def forward_block(member, image_maps, kernels, terms):
    images, height, width, channels = image_maps.shape
    members = len(kernels)
    share = channels // members
    shape = jax.ShapeDtypeStruct
    cell = (images, height, width, LANES)
    outs = [shape((images, share), BF)] * members + [
        shape((TAPS + 7, channels), F32),
        shape(image_maps.shape, F32),
        shape(cell, F32),
        shape(cell, F32),
        shape((images, channels), F32),
        shape((images, channels), F32),
        shape((images, LANES), F32),
    ]
    result = pl.pallas_call(
        lambda *refs: forward_kernel(members, *refs),
        out_shape=outs,
        in_specs=[SM, VM] + [VM] * (2 * members),
        out_specs=[VM] * len(outs),
        scratch_shapes=[pltpu.VMEM(cell, F32), pltpu.VMEM((images, channels), F32)],
        compiler_params=params(24),
        name="forward_block",
    )(member, image_maps, *kernels, *terms)
    return result[:members], result[members:]


def head_kernel(members, *refs):
    group = jnp.concatenate([ref[...].astype(F32) for ref in refs[:members]], axis=0).astype(BF)
    weight_ref, group_ref, out_ref = refs[members:]
    group_ref[...] = group
    out_ref[...] = jnp.dot(group, weight_ref[...], preferred_element_type=F32)


def head_project(pieces, head_weight):
    members = len(pieces)
    share, embed_width = head_weight.shape
    rows = members * pieces[0].shape[0]
    return pl.pallas_call(
        lambda *refs: head_kernel(members, *refs),
        out_shape=[
            jax.ShapeDtypeStruct((rows, share), BF),
            jax.ShapeDtypeStruct((rows, embed_width), F32),
        ],
        in_specs=[VM] * (members + 1),
        out_specs=[VM, VM],
        compiler_params=params(24),
        name="head_project",
    )(*pieces, head_weight)


def pair_weights(images, texts):
    logits = (
        LOGIT_SCALE
        * lax.dot_general(images, texts, (((1,), (1,)), ((), ())), preferred_element_type=F32)
        + LOGIT_BIAS
    )
    here = lax.broadcasted_iota(jnp.int32, logits.shape, 0)
    there = lax.broadcasted_iota(jnp.int32, logits.shape, 1)
    positive = jnp.where(here == there, 1.0, 0.0).astype(F32)
    return (jax.nn.sigmoid(logits) - positive).astype(BF)


def loss_kernel(members, *refs):
    partials, refs = refs[:members], refs[members:]
    text_ref, weight_ref, unit_ref, grad_ref = refs[:4]
    piece_refs = refs[4:]
    total_rows = partials[0].shape[0]
    rows = total_rows // members
    embed = partials[0][...]
    for m in range(1, members):
        embed = embed + jnp.concatenate(
            [partials[m][(k ^ m) * rows : (k ^ m) * rows + rows, :] for k in range(members)], axis=0
        )
    inv = lax.rsqrt(jnp.sum(embed * embed, axis=1, keepdims=True) + EPS)
    unit = embed * inv
    unit_bf = unit.astype(BF)
    unit_ref[...] = unit_bf
    texts = text_ref[...]
    unit_grad = LOGIT_SCALE * jnp.dot(
        pair_weights(unit_bf, texts), texts, preferred_element_type=F32
    )
    along = jnp.sum(unit * unit_grad, axis=1, keepdims=True)
    embed_grad = (inv * (unit_grad - unit * along)).astype(BF)
    grad_ref[...] = embed_grad
    part = lax.dot_general(
        embed_grad, weight_ref[...], (((1,), (1,)), ((), ())), preferred_element_type=F32
    )
    for m in range(members):
        piece_refs[m][...] = part[m * rows : m * rows + rows]


def loss_block(partials, text_all, head_weight):
    members = len(partials)
    total_rows, embed_width = partials[0].shape
    share = head_weight.shape[0]
    shape = jax.ShapeDtypeStruct
    result = pl.pallas_call(
        lambda *refs: loss_kernel(members, *refs),
        out_shape=[
            shape((total_rows, embed_width), BF),
            shape((total_rows, embed_width), BF),
        ]
        + [shape((total_rows // members, share), F32)] * members,
        in_specs=[VM] * (members + 2),
        out_specs=[VM] * (members + 2),
        compiler_params=params(24),
        name="loss_block",
    )(*partials, text_all, head_weight)
    return result[0], result[1], result[2:]


def terms_kernel(members, place_ref, *refs):
    grad_refs, refs = refs[:members], refs[members:]
    x_ref, weight_ref, mixed_ref, mean_ref, rstd_ref, hatsum_ref, hat_ref, hrstd_ref = refs[:8]
    keep_ref, give_ref, flow_ref, shared_ref, full_ref, scaled_ref, dot_ref, sums_ref, taps_ref = refs[8:]
    images, height, width, channels = x_ref.shape
    share = channels // members
    tiles = channels // LANES
    cells = height * width
    member = place_ref[0]
    core = place_ref[1]
    for m in range(members):
        full_ref[:, lane_block(member ^ m, share)] = grad_refs[m][...]
    grad = full_ref[...]
    hat = hat_ref[...]
    sums_ref[...] = jnp.zeros_like(sums_ref)
    sums_ref[TAPS + 3 : TAPS + 4, :] = jnp.sum(grad * hat, axis=0, keepdims=True)
    inner = grad * weight_ref[TAPS + 3 : TAPS + 4, :]
    shared = (
        hrstd_ref[:, 0:1]
        * (
            inner
            - jnp.mean(inner, axis=1, keepdims=True)
            - hat * jnp.mean(inner * hat, axis=1, keepdims=True)
        )
        * (1.0 / cells)
    )
    shared_ref[...] = shared
    gain = weight_ref[TAPS + 1 : TAPS + 2, :]
    scale = weight_ref[TAPS + 2 : TAPS + 3, :]
    hat_grad = shared * hatsum_ref[...]
    hat_total = jnp.sum(hat_grad, axis=0, keepdims=True)
    sums_ref[TAPS + 1 : TAPS + 2, :] = hat_total * scale
    sums_ref[TAPS + 2 : TAPS + 3, :] = hat_total * gain
    scaled = shared * (gain * scale)
    scaled_mean = jnp.mean(scaled, axis=1, keepdims=True)
    scaled_ref[...] = scaled - scaled_mean
    dot_ref[...] = jnp.zeros_like(dot_ref)

    @pl.loop(0, tiles)
    def _(t):
        lanes = lane_block(t, LANES)
        for i in range(images):
            factor = scaled_ref[i : i + 1, lanes]
            for h in range(height):
                dot_ref[i, h] += factor * (mixed_ref[i, h, :, lanes] - mean_ref[i, h])

    dots = jnp.sum(dot_ref[...], axis=-1, keepdims=True) * (1.0 / channels)
    dot_ref[...] = jnp.broadcast_to(dots, dot_ref.shape) * rstd_ref[...] * rstd_ref[...]

    @pl.loop(0, tiles)
    def _(t):
        lanes = lane_block(t, LANES)
        flows = []
        for i in range(images):
            factor = scaled_ref[i : i + 1, lanes]
            flow_rows = []
            for h in range(height):
                centered = mixed_ref[i, h, :, lanes] - mean_ref[i, h]
                flow = rstd_ref[i, h] * (factor - centered * dot_ref[i, h])
                flow_ref[i, h, :, lanes] = flow
                flow_rows.append(flow)
            flows.append(flow_rows)
        bias = flows[0][0]
        for i in range(images):
            for h in range(height):
                if i or h:
                    bias = bias + flows[i][h]
        taps_ref[TAPS * width : TAPS * width + width, :] = bias
        for b in range(KER):
            totals = [None] * KER
            for i in range(images):
                moved = [shift_cols(x_ref[i, h, :, lanes].astype(F32), b - REACH) for h in range(height)]
                for a in range(KER):
                    for h in range(max(0, REACH - a), min(height, height + REACH - a)):
                        term = flows[i][h] * moved[h + a - REACH]
                        totals[a] = term if totals[a] is None else totals[a] + term
            for a in range(KER):
                tap = a * KER + b
                taps_ref[tap * width : tap * width + width, :] = totals[a]
        rows = TAPS + 1
        total = taps_ref[pl.ds(0, rows, stride=width), :]
        for s in range(1, width):
            total = total + taps_ref[pl.ds(s, rows, stride=width), :]
        sums_ref[0:rows, lanes] = total

    half = ROWS_PAD // 2
    for m in range(members):
        lanes = lane_block(member ^ m, share)
        keep_ref[m] = sums_ref[pl.ds(pl.multiple_of(core * half, half), half), lanes].astype(BF)
        give_ref[m] = sums_ref[pl.ds(pl.multiple_of((1 - core) * half, half), half), lanes].astype(BF)


def terms_block(place, grads, image_maps, weights, mixed, mean, rstd, hatsum, hat, hrstd):
    images, height, width, channels = image_maps.shape
    members = len(grads)
    share = channels // members
    shape = jax.ShapeDtypeStruct
    half = shape((members, ROWS_PAD // 2, share), BF)
    return pl.pallas_call(
        lambda *refs: terms_kernel(members, *refs),
        out_shape=[half, half, shape(image_maps.shape, F32), shape((images, channels), F32)],
        in_specs=[SM] + [VM] * (members + 8),
        out_specs=[VM] * 4,
        scratch_shapes=[
            pltpu.VMEM((images, channels), F32),
            pltpu.VMEM((images, channels), F32),
            pltpu.VMEM((images, height, width, LANES), F32),
            pltpu.VMEM((ROWS_PAD, channels), F32),
            pltpu.VMEM(((TAPS + 1) * width, LANES), F32),
        ],
        compiler_params=params(24),
        name="terms_block",
    )(place, *grads, image_maps, weights, mixed, mean, rstd, hatsum, hat, hrstd)


def images_kernel(flow_ref, weight_ref, shared_ref, out_ref):
    images, height, width, channels = flow_ref.shape

    @pl.loop(0, channels // LANES)
    def _(t):
        lanes = lane_block(t, LANES)
        for i in range(images):
            rows = [flow_ref[i, h, :, lanes] for h in range(height)]
            sums = conv_rows(rows, lambda tap: weight_ref[tap : tap + 1, lanes], True)
            for h in range(height):
                out_ref[i, h, :, lanes] = (sums[h] + shared_ref[i : i + 1, lanes]).astype(BF)


def images_block(flow, weights, shared):
    return pl.pallas_call(
        images_kernel,
        out_shape=jax.ShapeDtypeStruct(flow.shape, BF),
        in_specs=[VM] * 3,
        out_specs=VM,
        compiler_params=params(24),
        cost_estimate=pl.CostEstimate(
            flops=2 * TAPS * flow.size, bytes_accessed=6 * flow.size, transcendentals=0
        ),
        name="images_block",
    )(flow, weights, shared)


def to_unit(vectors):
    return vectors * lax.rsqrt(jnp.sum(vectors * vectors, axis=1, keepdims=True) + EPS)


def reduce_terms(keep, give, core, members, dp_masks):
    chip = keep.astype(F32) + swap(give, "dp", 1).astype(F32)
    sent = chip.astype(BF)
    total = sent[0].astype(F32)
    for m in range(1, members):
        total = total + swap(sent[m], "fsdp", m).astype(F32)
    for mask in dp_masks:
        sent = total.astype(BF)
        total = sent.astype(F32) + swap(sent, "dp", mask).astype(F32)
    sent = total.astype(BF)
    other = swap(sent, "dp", 1)
    low = jnp.where(core == 0, sent, other)
    high = jnp.where(core == 0, other, sent)
    return jnp.concatenate([low, high], axis=0).astype(F32)


def per_device(image_maps, dw_kernel, channel_terms, head_weight, text_feats):
    rows = image_maps.shape[0]
    members = lax.axis_size("fsdp")
    member = lax.axis_index("fsdp")
    core = lax.axis_index("dp") % 2
    place = jnp.stack([member, core]).astype(jnp.int32)
    others = range(1, members)
    pair_masks = bits_up(members)
    dp_masks = bits_up(lax.axis_size("dp"))
    down = dp_masks[::-1]
    share, width = head_weight.shape

    kernels = [dw_kernel] + [swap(dw_kernel, "fsdp", m) for m in others]
    terms = [channel_terms] + [swap(channel_terms, "fsdp", m) for m in others]

    text_unit, text_back = jax.vjp(to_unit, text_feats.astype(F32))
    own_text = text_unit.astype(BF)
    text_all = tree_gather(tree_gather(own_text, "fsdp", pair_masks), "dp", down)

    pieces, saved = forward_block(place, image_maps, kernels, terms)
    weights = saved[0]
    pieces = [pieces[0]] + [swap(pieces[m], "fsdp", m) for m in others]
    group, partial = head_project(pieces, head_weight)
    partials = [partial] + [swap(partial, "fsdp", m) for m in others]
    unit_bf, embed_grad, grads = loss_block(partials, text_all, head_weight)
    grads = [grads[0]] + [swap(grads[m], "fsdp", m) for m in others]

    keep, give, flow, shared = terms_block(place, grads, image_maps, *saved)
    image_grads = images_block(flow, weights, shared)

    packed = tree_gather(jnp.concatenate([group, embed_grad, unit_bf], axis=1), "dp", down)
    group_all = packed[:, :share]
    grad_all = packed[:, share : share + width]
    unit_all = packed[:, share + width :]

    sums = reduce_terms(keep, give, core, members, dp_masks[1:])

    head_grads = lax.dot_general(
        group_all, grad_all, (((0,), (0,)), ((), ())), preferred_element_type=F32
    )
    text_sum = LOGIT_SCALE * lax.dot_general(
        pair_weights(unit_all, own_text),
        unit_all,
        (((0,), (0,)), ((), ())),
        preferred_element_type=F32,
    )
    text_grads = text_back(text_sum)[0]
    return (image_grads, sums[:TAPS], sums[TAPS : TAPS + 4], head_grads, text_grads)


def solution(mesh):
    in_specs = (
        P(("dp", "fsdp"), None, None, None),
        P(None, "fsdp"),
        P(None, "fsdp"),
        P("fsdp", None),
        P(("dp", "fsdp"), None),
    )
    out_specs = (
        P(("dp", "fsdp"), None, None, None),
        P(None, "fsdp"),
        P(None, "fsdp"),
        P("fsdp", None),
        P(("dp", "fsdp"), None),
    )
    return jax.shard_map(
        per_device, mesh=mesh, in_specs=in_specs, out_specs=out_specs, check_vma=False
    )
```

```python
import jax
import jax.numpy as jnp
from jax import lax
from jax.experimental import pallas as pl
from jax.experimental.pallas import tpu as pltpu
from jax.sharding import PartitionSpec as P

EPS = 1e-06
LOGIT_SCALE = 10.0
LOGIT_BIAS = -2.0
KER = 7
REACH = KER // 2
TAPS = KER * KER
LANES = 128
ROWS_PAD = 64
HALF_PAD = ROWS_PAD // 2
TERM_ROW = 56
BF = jnp.bfloat16
F32 = jnp.float32


def swap(value, axis, mask):
    count = lax.axis_size(axis)
    return lax.ppermute(value, axis, [(source, source ^ mask) for source in range(count)])


def tree_gather(value, axis, masks):
    for mask in masks:
        value = jnp.concatenate([value, swap(value, axis, mask)], axis=0)
    return value


def bits_up(count):
    masks = []
    mask = 1
    while mask < count:
        masks.append(mask)
        mask *= 2
    return masks


def params(mebibytes):
    return pltpu.CompilerParams(vmem_limit_bytes=mebibytes * 1024 * 1024)


def far(arrays):
    return [pltpu.with_memory_space_constraint(value, pltpu.HBM) for value in arrays]


def near(arrays):
    return [pltpu.with_memory_space_constraint(value, pltpu.VMEM) for value in arrays]


VM = pl.BlockSpec(memory_space=pltpu.VMEM)
SM = pl.BlockSpec(memory_space=pltpu.SMEM)
HB = pl.BlockSpec(memory_space=pltpu.HBM)
ANY = pl.BlockSpec(memory_space=pl.ANY)
SHAPE = jax.ShapeDtypeStruct


def lane_block(index, width):
    return pl.ds(pl.multiple_of(index * width, LANES), width)


def shift_cols(value, step):
    if step == 0:
        return value
    width = value.shape[0]
    rolled = pltpu.roll(value, (-step) % width, 0)
    col = lax.broadcasted_iota(jnp.int32, value.shape, 0)
    inside = (col < width - step) if step > 0 else (col >= -step)
    return jnp.where(inside, rolled, 0.0)


def conv_rows(rows, tap_row, flip):
    height = len(rows)
    sums = [None] * height
    for b in range(KER):
        moved = [shift_cols(row, b - REACH) for row in rows]
        for a in range(KER):
            tap = (KER - 1 - a) * KER + (KER - 1 - b) if flip else a * KER + b
            weight = tap_row(tap)
            for h in range(max(0, REACH - a), min(height, height + REACH - a)):
                term = moved[h + a - REACH] * weight
                sums[h] = term if sums[h] is None else sums[h] + term
    return sums


def stack_rows(low, high, order):
    def kernel(low_ref, high_ref, order_ref, out_ref):
        both = jnp.concatenate([low_ref[...].astype(F32), high_ref[...].astype(F32)], axis=0)
        out_ref[...] = both.astype(out_ref.dtype)

    rows, width = low.shape
    return pl.pallas_call(
        kernel,
        out_shape=SHAPE((2 * rows, width), low.dtype),
        in_specs=[VM, VM, ANY],
        out_specs=VM,
        compiler_params=params(24),
        name="stack_rows",
    )(low, high, order)


def add_all(values, order):
    def kernel(*refs):
        total = refs[0][...].astype(F32)
        for ref in refs[1:-2]:
            total = total + ref[...].astype(F32)
        refs[-1][...] = total.astype(BF)

    return pl.pallas_call(
        kernel,
        out_shape=SHAPE(values[0].shape, BF),
        in_specs=[VM] * len(values) + [ANY],
        out_specs=VM,
        compiler_params=params(24),
        name="add_all",
    )(*values, order)


def chip_sums(keep, give):
    members = keep.shape[0]

    def kernel(keep_ref, give_ref, *out_refs):
        for m in range(members):
            out_refs[m][...] = (keep_ref[m].astype(F32) + give_ref[m].astype(F32)).astype(BF)

    return pl.pallas_call(
        kernel,
        out_shape=[SHAPE(keep.shape[1:], BF)] * members,
        in_specs=[VM, VM],
        out_specs=[VM] * members,
        compiler_params=params(24),
        name="chip_sums",
    )(keep, give)


def tile_of(base_piece, t, member, share):
    per_piece = share // LANES
    piece = base_piece + t // per_piece
    return lane_block((member ^ piece) * per_piece + t % per_piece, LANES)


def conv_tiles(tiles, base_piece, member, share, x_ref, weight_ref, mixed_ref, sum_ref):
    images, height = x_ref.shape[:2]

    @pl.loop(0, tiles)
    def _(t):
        lanes = lane_block(t, LANES)
        source = tile_of(base_piece, t, member, share)
        bias = weight_ref[TERM_ROW : TERM_ROW + 1, lanes]
        for i in range(images):
            rows = [x_ref[i, h, :, source].astype(F32) for h in range(height)]
            sums = conv_rows(rows, lambda tap: weight_ref[tap : tap + 1, lanes], False)
            for h in range(height):
                value = sums[h] + bias
                mixed_ref[i, h, :, lanes] = value
                sum_ref[i, h] += value


def own_kernel(
    members, place_ref, x_hbm, kernel_hbm, term_hbm, mixed_ref, sum_ref, weight_ref, x_ref, kernel_ref, term_ref, sems
):
    share = kernel_hbm.shape[1]
    member = place_ref[0]
    copies = [
        pltpu.make_async_copy(kernel_hbm, kernel_ref, sems.at[0]),
        pltpu.make_async_copy(term_hbm, term_ref, sems.at[1]),
    ]
    for m in range(members):
        lanes = lane_block(member ^ m, share)
        copies.append(
            pltpu.make_async_copy(
                x_hbm.at[:, :, :, lanes], x_ref.at[:, :, :, lanes], sems.at[2 + m]
            )
        )
    for copy in copies:
        copy.start()
    sum_ref[...] = jnp.zeros_like(sum_ref)
    for copy in copies[:3]:
        copy.wait()
    weight_ref[0:TAPS, :] = kernel_ref[...].astype(F32)
    weight_ref[TERM_ROW : TERM_ROW + 4, :] = term_ref[...].astype(F32)
    conv_tiles(share // LANES, 0, member, share, x_ref, weight_ref, mixed_ref, sum_ref)
    for copy in copies[3:]:
        copy.wait()


def own_block(place, image_maps, dw_kernel, channel_terms):
    images, height, width, channels = image_maps.shape
    share = dw_kernel.shape[1]
    members = channels // share
    return pl.pallas_call(
        lambda *refs: own_kernel(members, *refs),
        out_shape=[
            SHAPE((images, height, width, share), F32),
            SHAPE((images, height, width, LANES), F32),
            SHAPE((ROWS_PAD, share), F32),
            SHAPE(image_maps.shape, BF),
        ],
        in_specs=[SM, HB, HB, HB],
        out_specs=[VM] * 4,
        scratch_shapes=[
            pltpu.VMEM(dw_kernel.shape, BF),
            pltpu.VMEM(channel_terms.shape, BF),
            pltpu.SemaphoreType.DMA((2 + members,)),
        ],
        compiler_params=params(24),
        name="own_block",
    )(place, *far([image_maps, dw_kernel, channel_terms]))


def forward_kernel(members, place_ref, head_hbm, x_ref, mixed_own, sum_own, weight_own, order_ref, *refs):
    kernel_refs, refs = refs[: members - 1], refs[members - 1 :]
    term_refs, refs = refs[: members - 1], refs[members - 1 :]
    piece_refs, refs = refs[:members], refs[members:]
    head_ref, weight_rest, mixed_rest, mean_ref, rstd_ref, hatsum_ref, hat_ref, hrstd_ref, sum_ref, pool_ref, sem = refs
    images, height, width, channels = x_ref.shape
    share = channels // members
    cells = height * width
    member = place_ref[0]
    head_copy = pltpu.make_async_copy(head_hbm, head_ref, sem)
    head_copy.start()
    for m in range(1, members):
        lanes = slice((m - 1) * share, m * share)
        weight_rest[0:TAPS, lanes] = kernel_refs[m - 1][...].astype(F32)
        weight_rest[TERM_ROW : TERM_ROW + 4, lanes] = term_refs[m - 1][...].astype(F32)
    sum_ref[...] = sum_own[...]
    own_tiles = share // LANES
    rest_tiles = (members - 1) * own_tiles
    conv_tiles(rest_tiles, 1, member, share, x_ref, weight_rest, mixed_rest, sum_ref)
    parts = [(0, own_tiles, mixed_own, weight_own), (1, rest_tiles, mixed_rest, weight_rest)]

    mean = jnp.sum(sum_ref[...], axis=-1, keepdims=True) * (1.0 / channels)
    mean_ref[...] = jnp.broadcast_to(mean, mean_ref.shape)
    sum_ref[...] = jnp.zeros_like(sum_ref)
    for base, tiles, mixed_ref, weight_ref in parts:

        @pl.loop(0, tiles)
        def _(t):
            lanes = lane_block(t, LANES)
            for i in range(images):
                for h in range(height):
                    value = mixed_ref[i, h, :, lanes] - mean_ref[i, h]
                    sum_ref[i, h] += value * value

    var = jnp.sum(sum_ref[...], axis=-1, keepdims=True) * (1.0 / channels)
    rstd_ref[...] = jnp.broadcast_to(lax.rsqrt(var + EPS), rstd_ref.shape)
    for base, tiles, mixed_ref, weight_ref in parts:

        @pl.loop(0, tiles)
        def _(t):
            lanes = lane_block(t, LANES)
            wide = lane_block(t + base * own_tiles, LANES)
            source = tile_of(base, t, member, share)
            scale = (
                weight_ref[TERM_ROW + 1 : TERM_ROW + 2, lanes]
                * weight_ref[TERM_ROW + 2 : TERM_ROW + 3, lanes]
            )
            for i in range(images):
                hats = jnp.zeros((width, LANES), F32)
                plain = jnp.zeros((width, LANES), F32)
                for h in range(height):
                    hats = hats + (mixed_ref[i, h, :, lanes] - mean_ref[i, h]) * rstd_ref[i, h]
                    plain = plain + x_ref[i, h, :, source].astype(F32)
                hat_row = jnp.sum(hats, axis=0, keepdims=True)
                hatsum_ref[i : i + 1, wide] = hat_row
                pool_ref[i : i + 1, wide] = (
                    jnp.sum(plain, axis=0, keepdims=True) + scale * hat_row
                ) * (1.0 / cells)

    pooled = pool_ref[...]
    centered = pooled - jnp.mean(pooled, axis=1, keepdims=True)
    head_rstd = lax.rsqrt(jnp.mean(centered * centered, axis=1, keepdims=True) + EPS)
    hat = centered * head_rstd
    hat_ref[...] = hat
    hrstd_ref[...] = jnp.broadcast_to(head_rstd, hrstd_ref.shape)
    for m in range(members):
        gain = (
            weight_own[TERM_ROW + 3 : TERM_ROW + 4, :]
            if m == 0
            else weight_rest[TERM_ROW + 3 : TERM_ROW + 4, (m - 1) * share : m * share]
        )
        piece_refs[m][...] = (hat[:, m * share : (m + 1) * share] * gain).astype(BF)
    head_copy.wait()


def forward_block(place, head_weight, x_here, own, order, kernels, terms):
    images, height, width, channels = x_here.shape
    members = len(kernels) + 1
    share = channels // members
    cell = (images, height, width, LANES)
    outs = [SHAPE((images, share), BF)] * members + [
        SHAPE(head_weight.shape, BF),
        SHAPE((ROWS_PAD, channels - share), F32),
        SHAPE((images, height, width, channels - share), F32),
        SHAPE(cell, F32),
        SHAPE(cell, F32),
        SHAPE((images, channels), F32),
        SHAPE((images, channels), F32),
        SHAPE((images, LANES), F32),
    ]
    result = pl.pallas_call(
        lambda *refs: forward_kernel(members, *refs),
        out_shape=outs,
        in_specs=[SM, HB, VM, VM, VM, VM, ANY] + [VM] * (2 * (members - 1)),
        out_specs=[VM] * len(outs),
        scratch_shapes=[
            pltpu.VMEM(cell, F32),
            pltpu.VMEM((images, channels), F32),
            pltpu.SemaphoreType.DMA,
        ],
        compiler_params=params(24),
        name="forward_block",
    )(place, *far([head_weight]), *near([x_here, *own]), order, *near([*kernels, *terms]))
    return result[:members], result[members], result[members + 1], result[members + 2], result[members + 3 :]


def head_kernel(members, *refs):
    group = jnp.concatenate([ref[...].astype(F32) for ref in refs[:members]], axis=0).astype(BF)
    weight_ref, group_ref, out_ref = refs[members:]
    group_ref[...] = group
    out_ref[...] = jnp.dot(group, weight_ref[...], preferred_element_type=F32)


def head_project(pieces, head_weight):
    members = len(pieces)
    share, embed_width = head_weight.shape
    rows = members * pieces[0].shape[0]
    return pl.pallas_call(
        lambda *refs: head_kernel(members, *refs),
        out_shape=[SHAPE((rows, share), BF), SHAPE((rows, embed_width), F32)],
        in_specs=[VM] * (members + 1),
        out_specs=[VM, VM],
        compiler_params=params(24),
        name="head_project",
    )(*near([*pieces, head_weight]))


def inverse_norm(vectors):
    return lax.rsqrt(jnp.sum(vectors * vectors, axis=1, keepdims=True) + EPS)


def pair_weights(images, texts):
    logits = (
        LOGIT_SCALE
        * lax.dot_general(images, texts, (((1,), (1,)), ((), ())), preferred_element_type=F32)
        + LOGIT_BIAS
    )
    here = lax.broadcasted_iota(jnp.int32, logits.shape, 0)
    there = lax.broadcasted_iota(jnp.int32, logits.shape, 1)
    positive = jnp.where(here == there, 1.0, 0.0).astype(F32)
    return (jax.nn.sigmoid(logits) - positive).astype(BF)


def unit_back(unit, inverse, grad):
    return inverse * (grad - unit * jnp.sum(unit * grad, axis=1, keepdims=True))


def loss_kernel(members, *refs):
    partials, refs = refs[:members], refs[members:]
    text_low, text_high, group_ref, weight_ref, packed_ref = refs[:5]
    piece_refs = refs[5:]
    total_rows, width = partials[0].shape
    rows = total_rows // members
    share = group_ref.shape[1]
    embed = partials[0][...]
    for m in range(1, members):
        embed = embed + jnp.concatenate(
            [partials[m][(k ^ m) * rows : (k ^ m) * rows + rows, :] for k in range(members)], axis=0
        )
    inverse = inverse_norm(embed)
    unit = embed * inverse
    unit_bf = unit.astype(BF)
    raw = jnp.concatenate([text_low[...], text_high[...]], axis=0).astype(F32)
    texts = (raw * inverse_norm(raw)).astype(BF)
    unit_grad = LOGIT_SCALE * jnp.dot(
        pair_weights(unit_bf, texts), texts, preferred_element_type=F32
    )
    embed_grad = unit_back(unit, inverse, unit_grad).astype(BF)
    packed_ref[:, 0:share] = group_ref[...]
    packed_ref[:, share : share + width] = embed_grad
    packed_ref[:, share + width : share + 2 * width] = unit_bf
    part = lax.dot_general(
        embed_grad, weight_ref[...], (((1,), (1,)), ((), ())), preferred_element_type=F32
    )
    for m in range(members):
        piece_refs[m][...] = part[m * rows : m * rows + rows]


def loss_block(partials, texts, group, head_weight):
    members = len(partials)
    total_rows, embed_width = partials[0].shape
    share = head_weight.shape[0]
    result = pl.pallas_call(
        lambda *refs: loss_kernel(members, *refs),
        out_shape=[SHAPE((total_rows, share + 2 * embed_width), BF)]
        + [SHAPE((total_rows // members, share), F32)] * members,
        in_specs=[VM] * (members + 4),
        out_specs=[VM] * (members + 1),
        compiler_params=params(24),
        name="loss_block",
    )(*near([*partials, *texts, group, head_weight]))
    return result[0], result[1:]


def terms_kernel(members, place_ref, *refs):
    grad_refs, refs = refs[:members], refs[members:]
    order_ref, x_ref, weight_own, weight_rest, mixed_own, mixed_rest, mean_ref, rstd_ref, hatsum_ref, hat_ref, hrstd_ref = refs[:11]
    keep_ref, give_ref, flow_ref, shared_ref, scaled_ref, dot_ref, sums_ref, taps_ref = refs[11:]
    images, height, width, channels = x_ref.shape
    share = channels // members
    own_tiles = share // LANES
    rest_tiles = (members - 1) * own_tiles
    cells = height * width
    member = place_ref[0]
    core = place_ref[1]
    parts = [(0, own_tiles, mixed_own), (1, rest_tiles, mixed_rest)]

    def term_row(row):
        return jnp.concatenate(
            [weight_own[TERM_ROW + row : TERM_ROW + row + 1, :], weight_rest[TERM_ROW + row : TERM_ROW + row + 1, :]],
            axis=1,
        )

    grad = jnp.concatenate([ref[...] for ref in grad_refs], axis=1)
    hat = hat_ref[...]
    sums_ref[...] = jnp.zeros_like(sums_ref)
    sums_ref[TERM_ROW + 3 : TERM_ROW + 4, :] = jnp.sum(grad * hat, axis=0, keepdims=True)
    inner = grad * term_row(3)
    shared = (
        hrstd_ref[:, 0:1]
        * (
            inner
            - jnp.mean(inner, axis=1, keepdims=True)
            - hat * jnp.mean(inner * hat, axis=1, keepdims=True)
        )
        * (1.0 / cells)
    )
    shared_ref[...] = shared
    gain = term_row(1)
    scale = term_row(2)
    hat_total = jnp.sum(shared * hatsum_ref[...], axis=0, keepdims=True)
    sums_ref[TERM_ROW + 1 : TERM_ROW + 2, :] = hat_total * scale
    sums_ref[TERM_ROW + 2 : TERM_ROW + 3, :] = hat_total * gain
    scaled = shared * (gain * scale)
    scaled_ref[...] = scaled - jnp.mean(scaled, axis=1, keepdims=True)
    dot_ref[...] = jnp.zeros_like(dot_ref)
    for base, tiles, mixed_ref in parts:

        @pl.loop(0, tiles)
        def _(t):
            lanes = lane_block(t, LANES)
            wide = lane_block(t + base * own_tiles, LANES)
            for i in range(images):
                factor = scaled_ref[i : i + 1, wide]
                for h in range(height):
                    dot_ref[i, h] += factor * (mixed_ref[i, h, :, lanes] - mean_ref[i, h])

    dots = jnp.sum(dot_ref[...], axis=-1, keepdims=True) * (1.0 / channels)
    dot_ref[...] = jnp.broadcast_to(dots, dot_ref.shape) * rstd_ref[...] * rstd_ref[...]
    for base, tiles, mixed_ref in parts:

        @pl.loop(0, tiles)
        def _(t):
            lanes = lane_block(t, LANES)
            wide = lane_block(t + base * own_tiles, LANES)
            source = tile_of(base, t, member, share)
            flows = []
            for i in range(images):
                factor = scaled_ref[i : i + 1, wide]
                flow_rows = []
                for h in range(height):
                    centered = mixed_ref[i, h, :, lanes] - mean_ref[i, h]
                    flow = rstd_ref[i, h] * (factor - centered * dot_ref[i, h])
                    flow_ref[i, h, :, wide] = flow
                    flow_rows.append(flow)
                flows.append(flow_rows)
            bias = flows[0][0]
            for i in range(images):
                for h in range(height):
                    if i or h:
                        bias = bias + flows[i][h]
            taps_ref[TAPS * width : TAPS * width + width, :] = bias
            for b in range(KER):
                totals = [None] * KER
                for i in range(images):
                    moved = [
                        shift_cols(x_ref[i, h, :, source].astype(F32), b - REACH)
                        for h in range(height)
                    ]
                    for a in range(KER):
                        for h in range(max(0, REACH - a), min(height, height + REACH - a)):
                            term = flows[i][h] * moved[h + a - REACH]
                            totals[a] = term if totals[a] is None else totals[a] + term
                for a in range(KER):
                    tap = a * KER + b
                    taps_ref[tap * width : tap * width + width, :] = totals[a]
            rows = TAPS + 1
            total = taps_ref[pl.ds(0, rows, stride=width), :]
            for s in range(1, width):
                total = total + taps_ref[pl.ds(s, rows, stride=width), :]
            sums_ref[0:TAPS, wide] = total[0:TAPS]
            sums_ref[TERM_ROW : TERM_ROW + 1, wide] = total[TAPS : TAPS + 1]

    for m in range(members):
        lanes = slice(m * share, (m + 1) * share)
        keep_ref[m] = sums_ref[pl.ds(pl.multiple_of(core * HALF_PAD, HALF_PAD), HALF_PAD), lanes].astype(BF)
        give_ref[m] = sums_ref[pl.ds(pl.multiple_of((1 - core) * HALF_PAD, HALF_PAD), HALF_PAD), lanes].astype(BF)


def terms_block(place, grads, order, x_here, weights, mixed, saved):
    images, height, width, channels = x_here.shape
    members = len(grads)
    share = channels // members
    half = SHAPE((members, HALF_PAD, share), BF)
    return pl.pallas_call(
        lambda *refs: terms_kernel(members, *refs),
        out_shape=[half, half, SHAPE(x_here.shape, F32), SHAPE((images, channels), F32)],
        in_specs=[SM] + [VM] * members + [ANY] + [VM] * 10,
        out_specs=[VM] * 4,
        scratch_shapes=[
            pltpu.VMEM((images, channels), F32),
            pltpu.VMEM((images, height, width, LANES), F32),
            pltpu.VMEM((ROWS_PAD, channels), F32),
            pltpu.VMEM(((TAPS + 1) * width, LANES), F32),
        ],
        compiler_params=params(24),
        name="terms_block",
    )(place, *near(grads), order, *near([x_here, *weights, *mixed, *saved]))


def images_kernel(image, place_ref, flow_ref, weight_own, weight_rest, shared_ref, out_ref, token_ref):
    height, width, channels = flow_ref.shape[1:]
    share = weight_own.shape[1]
    own_tiles = share // LANES
    step = pl.program_id(0)
    token_ref[...] = jnp.zeros_like(token_ref)

    def piece(weight_ref, first):
        @pl.loop(0, own_tiles)
        def _(t):
            lanes = lane_block(t, LANES)
            wide = lane_block(t + step * own_tiles, LANES)
            near_lanes = lane_block(t + (step - first) * own_tiles, LANES)
            rows = [flow_ref[image, h, :, wide] for h in range(height)]
            sums = conv_rows(rows, lambda tap: weight_ref[tap : tap + 1, near_lanes], True)
            for h in range(height):
                out_ref[0, h, :, lanes] = (sums[h] + shared_ref[image : image + 1, wide]).astype(BF)

    @pl.when(step == 0)
    def _():
        piece(weight_own, 0)

    @pl.when(step != 0)
    def _():
        piece(weight_rest, 1)


def image_block(image, place, flow, weights, shared, order, out):
    first = out is None
    share = weights[0].shape[1]
    members = flow.shape[3] // share
    operands = [place, *near([flow, *weights, shared]), order] + ([] if first else [out])

    def kernel(*refs):
        images_kernel(image, *refs[:5], refs[-2], refs[-1])

    return pl.pallas_call(
        kernel,
        grid_spec=pltpu.PrefetchScalarGridSpec(
            num_scalar_prefetch=1,
            grid=(members,),
            in_specs=[VM, VM, VM, VM, ANY] + ([] if first else [HB]),
            out_specs=[
                pl.BlockSpec(
                    (1,) + flow.shape[1:3] + (share,),
                    lambda step, place_ref: (image, 0, 0, place_ref[0] ^ step),
                ),
                pl.BlockSpec((8, LANES), lambda step, place_ref: (0, 0)),
            ],
        ),
        out_shape=[SHAPE(flow.shape, BF), SHAPE((8, LANES), F32)],
        input_output_aliases={} if first else {6: 0},
        compiler_params=params(24),
        name="image_block",
    )(*operands)


def head_grads_kernel(block, packed_low, packed_high, text_ref, order_ref, head_ref, text_grad_ref):
    share = packed_low.shape[1] - 2 * text_ref.shape[1]
    width = text_ref.shape[1]
    step = pl.program_id(0)
    lanes = lane_block(step, block)
    grads = slice(share, share + width)
    images = jnp.concatenate([packed_low[:, lanes], packed_high[:, lanes]], axis=0)
    grad = jnp.concatenate([packed_low[:, grads], packed_high[:, grads]], axis=0)
    head_ref[...] = lax.dot_general(
        images, grad, (((0,), (0,)), ((), ())), preferred_element_type=F32
    )

    @pl.when(step == 0)
    def _():
        units = slice(share + width, share + 2 * width)
        unit_all = jnp.concatenate([packed_low[:, units], packed_high[:, units]], axis=0)
        raw = text_ref[...].astype(F32)
        inverse = inverse_norm(raw)
        unit = raw * inverse
        pairs = pair_weights(unit_all, unit.astype(BF))
        text_sum = LOGIT_SCALE * lax.dot_general(
            pairs, unit_all, (((0,), (0,)), ((), ())), preferred_element_type=F32
        )
        text_grad_ref[...] = unit_back(unit, inverse, text_sum)


def head_grads_block(packed, text_feats, share, order):
    rows, width = text_feats.shape
    block = 256 if share % 256 == 0 else LANES
    return pl.pallas_call(
        lambda *refs: head_grads_kernel(block, *refs),
        grid=(share // block,),
        out_shape=[SHAPE((share, width), F32), SHAPE((rows, width), F32)],
        in_specs=[VM, VM, VM, ANY],
        out_specs=[
            pl.BlockSpec((block, width), lambda step: (step, 0)),
            pl.BlockSpec((rows, width), lambda step: (0, 0)),
        ],
        compiler_params=params(24),
        name="head_grads_block",
    )(*near(packed), text_feats, order)


def split_kernel(place_ref, own_ref, other_ref, kernel_ref, term_ref):
    core = place_ref[1]
    rest = TAPS - HALF_PAD
    terms = slice(TERM_ROW - HALF_PAD, TERM_ROW - HALF_PAD + 4)

    def write(low_ref, high_ref):
        kernel_ref[0:HALF_PAD, :] = low_ref[...].astype(F32)
        high = high_ref[...].astype(F32)
        kernel_ref[HALF_PAD:TAPS, :] = high[0:rest]
        term_ref[...] = high[terms]

    @pl.when(core == 0)
    def _():
        write(own_ref, other_ref)

    @pl.when(core != 0)
    def _():
        write(other_ref, own_ref)


def split_block(place, own, other):
    share = own.shape[1]
    return pl.pallas_call(
        split_kernel,
        out_shape=[SHAPE((TAPS, share), F32), SHAPE((4, share), F32)],
        in_specs=[SM, VM, VM],
        out_specs=[VM, VM],
        compiler_params=params(24),
        name="split_block",
    )(place, *near([own, other]))


def per_device(image_maps, dw_kernel, channel_terms, head_weight, text_feats):
    members = lax.axis_size("fsdp")
    member = lax.axis_index("fsdp")
    core = lax.axis_index("dp") % 2
    place = jnp.stack([member, core]).astype(jnp.int32)
    others = range(1, members)
    pair_masks = bits_up(members)
    dp_masks = bits_up(lax.axis_size("dp"))
    down = dp_masks[::-1]
    share = head_weight.shape[0]

    kernels = [swap(dw_kernel, "fsdp", m) for m in others]
    terms = [swap(channel_terms, "fsdp", m) for m in others]
    mixed_own, sum_own, weight_own, x_here = own_block(place, image_maps, dw_kernel, channel_terms)

    text_rows = text_feats
    for mask in pair_masks:
        text_rows = stack_rows(text_rows, swap(text_rows, "fsdp", mask), sum_own)
    text_rows = stack_rows(text_rows, swap(text_rows, "dp", 1), (terms or [sum_own])[-1])
    text_masks = down[:-1]
    pieces, head_here, weight_rest, mixed_rest, saved = forward_block(
        place, head_weight, x_here, (mixed_own, sum_own, weight_own), text_rows, kernels, terms
    )
    weights = (weight_own, weight_rest)
    far_rows = swap(text_rows, "dp", text_masks[0])
    pieces = [pieces[0]] + [swap(pieces[m], "fsdp", m) for m in others]
    group, partial = head_project(pieces, head_here)
    orders = [saved[4]] + [partial] * len(text_masks)
    for mask, order in zip(text_masks[1:], orders):
        text_rows = stack_rows(text_rows, far_rows, order)
        far_rows = swap(text_rows, "dp", mask)
    texts = (text_rows, far_rows)

    partials = [partial] + [swap(partial, "fsdp", m) for m in others]
    packed, grads = loss_block(partials, texts, group, head_here)
    grads = [grads[0]] + [swap(grads[m], "fsdp", m) for m in others]

    packed = stack_rows(packed, swap(packed, "dp", down[0]), packed)
    keep, give, flow, shared = terms_block(
        place, grads, packed, x_here, weights, (mixed_own, mixed_rest), saved
    )
    for mask in down[1:-1]:
        packed = stack_rows(packed, swap(packed, "dp", mask), shared)
    packed = (packed, swap(packed, "dp", down[-1]))

    chip = chip_sums(keep, swap(give, "dp", 1))
    image_grads, token = image_block(0, place, flow, weights, shared, chip[0], None)
    sent = add_all([chip[0]] + [swap(chip[m], "fsdp", m) for m in others], token)
    for image in range(1, image_maps.shape[0]):
        image_grads, token = image_block(image, place, flow, weights, shared, sent, image_grads)
    ring_masks = dp_masks[1:]
    for mask in ring_masks[:-1]:
        sent = add_all([sent, swap(sent, "dp", mask)], token)
    head_grads, text_grads = head_grads_block(packed, text_feats, share, sent)
    sent = add_all([sent, swap(sent, "dp", ring_masks[-1])], text_grads)
    kernel_grads, term_grads = split_block(place, sent, swap(sent, "dp", 1))
    return (image_grads, kernel_grads, term_grads, head_grads, text_grads)


def solution(mesh):
    in_specs = (
        P(("dp", "fsdp"), None, None, None),
        P(None, "fsdp"),
        P(None, "fsdp"),
        P("fsdp", None),
        P(("dp", "fsdp"), None),
    )
    out_specs = (
        P(("dp", "fsdp"), None, None, None),
        P(None, "fsdp"),
        P(None, "fsdp"),
        P("fsdp", None),
        P(("dp", "fsdp"), None),
    )
    return jax.shard_map(
        per_device, mesh=mesh, in_specs=in_specs, out_specs=out_specs, check_vma=False
    )
```

```python
import jax
import jax.numpy as jnp
from jax import lax
from jax.experimental import pallas as pl
from jax.experimental.pallas import tpu as pltpu
from jax.sharding import PartitionSpec as P

EPS = 1e-06
LOGIT_SCALE = 10.0
LOGIT_BIAS = -2.0
KER = 7
REACH = KER // 2
TAPS = KER * KER
LANES = 128
ROWS_PAD = 64
HALF_PAD = ROWS_PAD // 2
TERM_ROW = 56
BF = jnp.bfloat16
F32 = jnp.float32


def swap(value, axis, mask):
    count = lax.axis_size(axis)
    return lax.ppermute(value, axis, [(source, source ^ mask) for source in range(count)])


def tree_gather(value, axis, masks):
    for mask in masks:
        value = jnp.concatenate([value, swap(value, axis, mask)], axis=0)
    return value


def bits_up(count):
    masks = []
    mask = 1
    while mask < count:
        masks.append(mask)
        mask *= 2
    return masks


def params(mebibytes):
    return pltpu.CompilerParams(vmem_limit_bytes=mebibytes * 1024 * 1024)


def far(arrays):
    return [pltpu.with_memory_space_constraint(value, pltpu.HBM) for value in arrays]


def near(arrays):
    return [pltpu.with_memory_space_constraint(value, pltpu.VMEM) for value in arrays]


VM = pl.BlockSpec(memory_space=pltpu.VMEM)
SM = pl.BlockSpec(memory_space=pltpu.SMEM)
HB = pl.BlockSpec(memory_space=pltpu.HBM)
ANY = pl.BlockSpec(memory_space=pl.ANY)
SHAPE = jax.ShapeDtypeStruct


def lane_block(index, width):
    return pl.ds(pl.multiple_of(index * width, LANES), width)


def shift_cols(value, step):
    if step == 0:
        return value
    width = value.shape[0]
    rolled = pltpu.roll(value, (-step) % width, 0)
    col = lax.broadcasted_iota(jnp.int32, value.shape, 0)
    inside = (col < width - step) if step > 0 else (col >= -step)
    return jnp.where(inside, rolled, 0.0)


def conv_rows(rows, tap_row, flip):
    height = len(rows)
    sums = [None] * height
    for b in range(KER):
        moved = [shift_cols(row, b - REACH) for row in rows]
        for a in range(KER):
            tap = (KER - 1 - a) * KER + (KER - 1 - b) if flip else a * KER + b
            weight = tap_row(tap)
            for h in range(max(0, REACH - a), min(height, height + REACH - a)):
                term = moved[h + a - REACH] * weight
                sums[h] = term if sums[h] is None else sums[h] + term
    return sums


def stack_rows(low, high, order):
    def kernel(low_ref, high_ref, order_ref, out_ref):
        both = jnp.concatenate([low_ref[...].astype(F32), high_ref[...].astype(F32)], axis=0)
        out_ref[...] = both.astype(out_ref.dtype)

    rows, width = low.shape
    return pl.pallas_call(
        kernel,
        out_shape=SHAPE((2 * rows, width), low.dtype),
        in_specs=[VM, VM, ANY],
        out_specs=VM,
        compiler_params=params(24),
        name="stack_rows",
    )(low, high, order)


def add_all(values, order):
    def kernel(*refs):
        total = refs[0][...].astype(F32)
        for ref in refs[1:-2]:
            total = total + ref[...].astype(F32)
        refs[-1][...] = total.astype(BF)

    return pl.pallas_call(
        kernel,
        out_shape=SHAPE(values[0].shape, BF),
        in_specs=[VM] * len(values) + [ANY],
        out_specs=VM,
        compiler_params=params(24),
        name="add_all",
    )(*values, order)


def chip_sums(keep, give):
    members = keep.shape[0]

    def kernel(keep_ref, give_ref, *out_refs):
        for m in range(members):
            out_refs[m][...] = (keep_ref[m].astype(F32) + give_ref[m].astype(F32)).astype(BF)

    return pl.pallas_call(
        kernel,
        out_shape=[SHAPE(keep.shape[1:], BF)] * members,
        in_specs=[VM, VM],
        out_specs=[VM] * members,
        compiler_params=params(24),
        name="chip_sums",
    )(keep, give)


def tile_of(base_piece, t, member, share):
    per_piece = share // LANES
    piece = base_piece + t // per_piece
    return lane_block((member ^ piece) * per_piece + t % per_piece, LANES)


def conv_tiles(tiles, base_piece, member, share, x_ref, weight_ref, mixed_ref, sum_ref):
    images, height = x_ref.shape[:2]

    @pl.loop(0, tiles)
    def _(t):
        lanes = lane_block(t, LANES)
        source = tile_of(base_piece, t, member, share)
        bias = weight_ref[TERM_ROW : TERM_ROW + 1, lanes]
        for i in range(images):
            rows = [x_ref[i, h, :, source].astype(F32) for h in range(height)]
            sums = conv_rows(rows, lambda tap: weight_ref[tap : tap + 1, lanes], False)
            for h in range(height):
                value = sums[h] + bias
                mixed_ref[i, h, :, lanes] = value
                sum_ref[i, h] += value


def own_kernel(
    members, place_ref, x_hbm, kernel_hbm, term_hbm, text_hbm, mixed_ref, sum_ref, weight_ref, x_ref, text_ref, kernel_ref, term_ref, sems
):
    share = kernel_hbm.shape[1]
    member = place_ref[0]
    copies = [
        pltpu.make_async_copy(kernel_hbm, kernel_ref, sems.at[0]),
        pltpu.make_async_copy(term_hbm, term_ref, sems.at[1]),
    ]
    for m in range(members):
        lanes = lane_block(member ^ m, share)
        copies.append(
            pltpu.make_async_copy(
                x_hbm.at[:, :, :, lanes], x_ref.at[:, :, :, lanes], sems.at[2 + m]
            )
        )
    copies.append(pltpu.make_async_copy(text_hbm, text_ref, sems.at[2 + members]))
    for copy in copies:
        copy.start()
    sum_ref[...] = jnp.zeros_like(sum_ref)
    for copy in copies[:3]:
        copy.wait()
    weight_ref[0:TAPS, :] = kernel_ref[...].astype(F32)
    weight_ref[TERM_ROW : TERM_ROW + 4, :] = term_ref[...].astype(F32)
    conv_tiles(share // LANES, 0, member, share, x_ref, weight_ref, mixed_ref, sum_ref)
    for copy in copies[3:]:
        copy.wait()


def own_block(place, image_maps, dw_kernel, channel_terms, text_feats):
    images, height, width, channels = image_maps.shape
    share = dw_kernel.shape[1]
    members = channels // share
    return pl.pallas_call(
        lambda *refs: own_kernel(members, *refs),
        out_shape=[
            SHAPE((images, height, width, share), F32),
            SHAPE((images, height, width, LANES), F32),
            SHAPE((ROWS_PAD, share), F32),
            SHAPE(image_maps.shape, BF),
            SHAPE(text_feats.shape, BF),
        ],
        in_specs=[SM, HB, HB, HB, HB],
        out_specs=[VM] * 5,
        scratch_shapes=[
            pltpu.VMEM(dw_kernel.shape, BF),
            pltpu.VMEM(channel_terms.shape, BF),
            pltpu.SemaphoreType.DMA((3 + members,)),
        ],
        compiler_params=params(24),
        name="own_block",
    )(place, *far([image_maps, dw_kernel, channel_terms, text_feats]))


def forward_kernel(members, place_ref, head_hbm, x_ref, mixed_own, sum_own, weight_own, order_ref, *refs):
    kernel_refs, refs = refs[: members - 1], refs[members - 1 :]
    term_refs, refs = refs[: members - 1], refs[members - 1 :]
    piece_refs, refs = refs[:members], refs[members:]
    head_ref, weight_rest, mixed_rest, mean_ref, rstd_ref, hatsum_ref, hat_ref, hrstd_ref, sum_ref, pool_ref, sem = refs
    images, height, width, channels = x_ref.shape
    share = channels // members
    cells = height * width
    member = place_ref[0]
    head_copy = pltpu.make_async_copy(head_hbm, head_ref, sem)
    head_copy.start()
    for m in range(1, members):
        lanes = slice((m - 1) * share, m * share)
        weight_rest[0:TAPS, lanes] = kernel_refs[m - 1][...].astype(F32)
        weight_rest[TERM_ROW : TERM_ROW + 4, lanes] = term_refs[m - 1][...].astype(F32)
    sum_ref[...] = sum_own[...]
    own_tiles = share // LANES
    rest_tiles = (members - 1) * own_tiles
    conv_tiles(rest_tiles, 1, member, share, x_ref, weight_rest, mixed_rest, sum_ref)
    parts = [(0, own_tiles, mixed_own, weight_own), (1, rest_tiles, mixed_rest, weight_rest)]

    mean = jnp.sum(sum_ref[...], axis=-1, keepdims=True) * (1.0 / channels)
    mean_ref[...] = jnp.broadcast_to(mean, mean_ref.shape)
    sum_ref[...] = jnp.zeros_like(sum_ref)
    for base, tiles, mixed_ref, weight_ref in parts:

        @pl.loop(0, tiles)
        def _(t):
            lanes = lane_block(t, LANES)
            for i in range(images):
                for h in range(height):
                    value = mixed_ref[i, h, :, lanes] - mean_ref[i, h]
                    sum_ref[i, h] += value * value

    var = jnp.sum(sum_ref[...], axis=-1, keepdims=True) * (1.0 / channels)
    rstd_ref[...] = jnp.broadcast_to(lax.rsqrt(var + EPS), rstd_ref.shape)
    for base, tiles, mixed_ref, weight_ref in parts:

        @pl.loop(0, tiles)
        def _(t):
            lanes = lane_block(t, LANES)
            wide = lane_block(t + base * own_tiles, LANES)
            source = tile_of(base, t, member, share)
            scale = (
                weight_ref[TERM_ROW + 1 : TERM_ROW + 2, lanes]
                * weight_ref[TERM_ROW + 2 : TERM_ROW + 3, lanes]
            )
            for i in range(images):
                hats = jnp.zeros((width, LANES), F32)
                plain = jnp.zeros((width, LANES), F32)
                for h in range(height):
                    hats = hats + (mixed_ref[i, h, :, lanes] - mean_ref[i, h]) * rstd_ref[i, h]
                    plain = plain + x_ref[i, h, :, source].astype(F32)
                hat_row = jnp.sum(hats, axis=0, keepdims=True)
                hatsum_ref[i : i + 1, wide] = hat_row
                pool_ref[i : i + 1, wide] = (
                    jnp.sum(plain, axis=0, keepdims=True) + scale * hat_row
                ) * (1.0 / cells)

    pooled = pool_ref[...]
    centered = pooled - jnp.mean(pooled, axis=1, keepdims=True)
    head_rstd = lax.rsqrt(jnp.mean(centered * centered, axis=1, keepdims=True) + EPS)
    hat = centered * head_rstd
    hat_ref[...] = hat
    hrstd_ref[...] = jnp.broadcast_to(head_rstd, hrstd_ref.shape)
    for m in range(members):
        gain = (
            weight_own[TERM_ROW + 3 : TERM_ROW + 4, :]
            if m == 0
            else weight_rest[TERM_ROW + 3 : TERM_ROW + 4, (m - 1) * share : m * share]
        )
        piece_refs[m][...] = (hat[:, m * share : (m + 1) * share] * gain).astype(BF)
    head_copy.wait()


def forward_block(place, head_weight, x_here, own, order, kernels, terms):
    images, height, width, channels = x_here.shape
    members = len(kernels) + 1
    share = channels // members
    cell = (images, height, width, LANES)
    outs = [SHAPE((images, share), BF)] * members + [
        SHAPE(head_weight.shape, BF),
        SHAPE((ROWS_PAD, channels - share), F32),
        SHAPE((images, height, width, channels - share), F32),
        SHAPE(cell, F32),
        SHAPE(cell, F32),
        SHAPE((images, channels), F32),
        SHAPE((images, channels), F32),
        SHAPE((images, LANES), F32),
    ]
    result = pl.pallas_call(
        lambda *refs: forward_kernel(members, *refs),
        out_shape=outs,
        in_specs=[SM, HB, VM, VM, VM, VM, ANY] + [VM] * (2 * (members - 1)),
        out_specs=[VM] * len(outs),
        scratch_shapes=[
            pltpu.VMEM(cell, F32),
            pltpu.VMEM((images, channels), F32),
            pltpu.SemaphoreType.DMA,
        ],
        compiler_params=params(24),
        name="forward_block",
    )(place, *far([head_weight]), *near([x_here, *own]), order, *near([*kernels, *terms]))
    return result[:members], result[members], result[members + 1], result[members + 2], result[members + 3 :]


def head_kernel(members, *refs):
    group = jnp.concatenate([ref[...].astype(F32) for ref in refs[:members]], axis=0).astype(BF)
    weight_ref, group_ref, out_ref = refs[members:]
    group_ref[...] = group
    out_ref[...] = jnp.dot(group, weight_ref[...], preferred_element_type=F32)


def head_project(pieces, head_weight):
    members = len(pieces)
    share, embed_width = head_weight.shape
    rows = members * pieces[0].shape[0]
    return pl.pallas_call(
        lambda *refs: head_kernel(members, *refs),
        out_shape=[SHAPE((rows, share), BF), SHAPE((rows, embed_width), F32)],
        in_specs=[VM] * (members + 1),
        out_specs=[VM, VM],
        compiler_params=params(24),
        name="head_project",
    )(*near([*pieces, head_weight]))


def inverse_norm(vectors):
    return lax.rsqrt(jnp.sum(vectors * vectors, axis=1, keepdims=True) + EPS)


def pair_weights(images, texts):
    logits = (
        LOGIT_SCALE
        * lax.dot_general(images, texts, (((1,), (1,)), ((), ())), preferred_element_type=F32)
        + LOGIT_BIAS
    )
    here = lax.broadcasted_iota(jnp.int32, logits.shape, 0)
    there = lax.broadcasted_iota(jnp.int32, logits.shape, 1)
    positive = jnp.where(here == there, 1.0, 0.0).astype(F32)
    return (jax.nn.sigmoid(logits) - positive).astype(BF)


def unit_back(unit, inverse, grad):
    return inverse * (grad - unit * jnp.sum(unit * grad, axis=1, keepdims=True))


def loss_kernel(members, *refs):
    partials, refs = refs[:members], refs[members:]
    text_low, text_high, group_ref, weight_ref, packed_ref = refs[:5]
    piece_refs = refs[5:]
    total_rows, width = partials[0].shape
    rows = total_rows // members
    share = group_ref.shape[1]
    embed = partials[0][...]
    for m in range(1, members):
        embed = embed + jnp.concatenate(
            [partials[m][(k ^ m) * rows : (k ^ m) * rows + rows, :] for k in range(members)], axis=0
        )
    inverse = inverse_norm(embed)
    unit = embed * inverse
    unit_bf = unit.astype(BF)
    raw = jnp.concatenate([text_low[...], text_high[...]], axis=0).astype(F32)
    texts = (raw * inverse_norm(raw)).astype(BF)
    unit_grad = LOGIT_SCALE * jnp.dot(
        pair_weights(unit_bf, texts), texts, preferred_element_type=F32
    )
    embed_grad = unit_back(unit, inverse, unit_grad).astype(BF)
    packed_ref[:, 0:share] = group_ref[...]
    packed_ref[:, share : share + width] = embed_grad
    packed_ref[:, share + width : share + 2 * width] = unit_bf
    part = lax.dot_general(
        embed_grad, weight_ref[...], (((1,), (1,)), ((), ())), preferred_element_type=F32
    )
    for m in range(members):
        piece_refs[m][...] = part[m * rows : m * rows + rows]


def loss_block(partials, texts, group, head_weight):
    members = len(partials)
    total_rows, embed_width = partials[0].shape
    share = head_weight.shape[0]
    result = pl.pallas_call(
        lambda *refs: loss_kernel(members, *refs),
        out_shape=[SHAPE((total_rows, share + 2 * embed_width), BF)]
        + [SHAPE((total_rows // members, share), F32)] * members,
        in_specs=[VM] * (members + 4),
        out_specs=[VM] * (members + 1),
        compiler_params=params(24),
        name="loss_block",
    )(*near([*partials, *texts, group, head_weight]))
    return result[0], result[1:]


def terms_kernel(members, place_ref, *refs):
    grad_refs, refs = refs[:members], refs[members:]
    order_ref, x_ref, weight_own, weight_rest, mixed_own, mixed_rest, mean_ref, rstd_ref, hatsum_ref, hat_ref, hrstd_ref = refs[:11]
    keep_ref, give_ref, flow_ref, shared_ref, scaled_ref, dot_ref, sums_ref, taps_ref = refs[11:]
    images, height, width, channels = x_ref.shape
    share = channels // members
    own_tiles = share // LANES
    rest_tiles = (members - 1) * own_tiles
    cells = height * width
    member = place_ref[0]
    core = place_ref[1]
    parts = [(0, own_tiles, mixed_own), (1, rest_tiles, mixed_rest)]

    def term_row(row):
        return jnp.concatenate(
            [weight_own[TERM_ROW + row : TERM_ROW + row + 1, :], weight_rest[TERM_ROW + row : TERM_ROW + row + 1, :]],
            axis=1,
        )

    grad = jnp.concatenate([ref[...] for ref in grad_refs], axis=1)
    hat = hat_ref[...]
    sums_ref[...] = jnp.zeros_like(sums_ref)
    sums_ref[TERM_ROW + 3 : TERM_ROW + 4, :] = jnp.sum(grad * hat, axis=0, keepdims=True)
    inner = grad * term_row(3)
    shared = (
        hrstd_ref[:, 0:1]
        * (
            inner
            - jnp.mean(inner, axis=1, keepdims=True)
            - hat * jnp.mean(inner * hat, axis=1, keepdims=True)
        )
        * (1.0 / cells)
    )
    shared_ref[...] = shared
    gain = term_row(1)
    scale = term_row(2)
    hat_total = jnp.sum(shared * hatsum_ref[...], axis=0, keepdims=True)
    sums_ref[TERM_ROW + 1 : TERM_ROW + 2, :] = hat_total * scale
    sums_ref[TERM_ROW + 2 : TERM_ROW + 3, :] = hat_total * gain
    scaled = shared * (gain * scale)
    scaled_ref[...] = scaled - jnp.mean(scaled, axis=1, keepdims=True)
    dot_ref[...] = jnp.zeros_like(dot_ref)
    for base, tiles, mixed_ref in parts:

        @pl.loop(0, tiles)
        def _(t):
            lanes = lane_block(t, LANES)
            wide = lane_block(t + base * own_tiles, LANES)
            for i in range(images):
                factor = scaled_ref[i : i + 1, wide]
                for h in range(height):
                    dot_ref[i, h] += factor * (mixed_ref[i, h, :, lanes] - mean_ref[i, h])

    dots = jnp.sum(dot_ref[...], axis=-1, keepdims=True) * (1.0 / channels)
    dot_ref[...] = jnp.broadcast_to(dots, dot_ref.shape) * rstd_ref[...] * rstd_ref[...]
    for base, tiles, mixed_ref in parts:

        @pl.loop(0, tiles)
        def _(t):
            lanes = lane_block(t, LANES)
            wide = lane_block(t + base * own_tiles, LANES)
            source = tile_of(base, t, member, share)
            flows = []
            for i in range(images):
                factor = scaled_ref[i : i + 1, wide]
                flow_rows = []
                for h in range(height):
                    centered = mixed_ref[i, h, :, lanes] - mean_ref[i, h]
                    flow = rstd_ref[i, h] * (factor - centered * dot_ref[i, h])
                    flow_ref[i, h, :, wide] = flow
                    flow_rows.append(flow)
                flows.append(flow_rows)
            bias = flows[0][0]
            for i in range(images):
                for h in range(height):
                    if i or h:
                        bias = bias + flows[i][h]
            taps_ref[TAPS * width : TAPS * width + width, :] = bias
            for b in range(KER):
                totals = [None] * KER
                for i in range(images):
                    moved = [
                        shift_cols(x_ref[i, h, :, source].astype(F32), b - REACH)
                        for h in range(height)
                    ]
                    for a in range(KER):
                        for h in range(max(0, REACH - a), min(height, height + REACH - a)):
                            term = flows[i][h] * moved[h + a - REACH]
                            totals[a] = term if totals[a] is None else totals[a] + term
                for a in range(KER):
                    tap = a * KER + b
                    taps_ref[tap * width : tap * width + width, :] = totals[a]
            rows = TAPS + 1
            total = taps_ref[pl.ds(0, rows, stride=width), :]
            for s in range(1, width):
                total = total + taps_ref[pl.ds(s, rows, stride=width), :]
            sums_ref[0:TAPS, wide] = total[0:TAPS]
            sums_ref[TERM_ROW : TERM_ROW + 1, wide] = total[TAPS : TAPS + 1]

    for m in range(members):
        lanes = slice(m * share, (m + 1) * share)
        keep_ref[m] = sums_ref[pl.ds(pl.multiple_of(core * HALF_PAD, HALF_PAD), HALF_PAD), lanes].astype(BF)
        give_ref[m] = sums_ref[pl.ds(pl.multiple_of((1 - core) * HALF_PAD, HALF_PAD), HALF_PAD), lanes].astype(BF)


def terms_block(place, grads, order, x_here, weights, mixed, saved):
    images, height, width, channels = x_here.shape
    members = len(grads)
    share = channels // members
    half = SHAPE((members, HALF_PAD, share), BF)
    return pl.pallas_call(
        lambda *refs: terms_kernel(members, *refs),
        out_shape=[half, half, SHAPE(x_here.shape, F32), SHAPE((images, channels), F32)],
        in_specs=[SM] + [VM] * members + [ANY] + [VM] * 10,
        out_specs=[VM] * 4,
        scratch_shapes=[
            pltpu.VMEM((images, channels), F32),
            pltpu.VMEM((images, height, width, LANES), F32),
            pltpu.VMEM((ROWS_PAD, channels), F32),
            pltpu.VMEM(((TAPS + 1) * width, LANES), F32),
        ],
        compiler_params=params(24),
        name="terms_block",
    )(place, *near(grads), order, *near([x_here, *weights, *mixed, *saved]))


def images_kernel(image, base, place_ref, flow_ref, weight_own, weight_rest, shared_ref, out_ref, token_ref):
    height, width, channels = flow_ref.shape[1:]
    share = weight_own.shape[1]
    own_tiles = share // LANES
    step = pl.program_id(0) + base
    token_ref[...] = jnp.zeros_like(token_ref)

    def piece(weight_ref, first):
        @pl.loop(0, own_tiles)
        def _(t):
            lanes = lane_block(t, LANES)
            wide = lane_block(t + step * own_tiles, LANES)
            near_lanes = lane_block(t + (step - first) * own_tiles, LANES)
            rows = [flow_ref[image, h, :, wide] for h in range(height)]
            sums = conv_rows(rows, lambda tap: weight_ref[tap : tap + 1, near_lanes], True)
            for h in range(height):
                out_ref[0, h, :, lanes] = (sums[h] + shared_ref[image : image + 1, wide]).astype(BF)

    if base == 0:

        @pl.when(step == 0)
        def _():
            piece(weight_own, 0)

    @pl.when(step != 0)
    def _():
        piece(weight_rest, 1)


def image_block(image, base, count, place, flow, weights, shared, order, out):
    first = out is None
    share = weights[0].shape[1]
    operands = [place, *near([flow, *weights, shared]), order] + ([] if first else [out])

    def kernel(*refs):
        images_kernel(image, base, *refs[:5], refs[-2], refs[-1])

    return pl.pallas_call(
        kernel,
        grid_spec=pltpu.PrefetchScalarGridSpec(
            num_scalar_prefetch=1,
            grid=(count,),
            in_specs=[VM, VM, VM, VM, ANY] + ([] if first else [HB]),
            out_specs=[
                pl.BlockSpec(
                    (1,) + flow.shape[1:3] + (share,),
                    lambda step, place_ref: (image, 0, 0, place_ref[0] ^ (step + base)),
                ),
                pl.BlockSpec((8, LANES), lambda step, place_ref: (0, 0)),
            ],
        ),
        out_shape=[SHAPE(flow.shape, BF), SHAPE((8, LANES), F32)],
        input_output_aliases={} if first else {6: 0},
        compiler_params=params(24),
        name="image_block",
    )(*operands)


def head_grads_kernel(block, packed_low, packed_high, text_ref, order_ref, head_ref, text_grad_ref, token_ref):
    share = packed_low.shape[1] - 2 * text_ref.shape[1]
    width = text_ref.shape[1]
    step = pl.program_id(0)
    lanes = lane_block(step, block)
    grads = slice(share, share + width)
    images = jnp.concatenate([packed_low[:, lanes], packed_high[:, lanes]], axis=0)
    grad = jnp.concatenate([packed_low[:, grads], packed_high[:, grads]], axis=0)
    head_ref[...] = lax.dot_general(
        images, grad, (((0,), (0,)), ((), ())), preferred_element_type=F32
    )

    @pl.when(step == 0)
    def _():
        token_ref[...] = jnp.zeros_like(token_ref)
        units = slice(share + width, share + 2 * width)
        unit_all = jnp.concatenate([packed_low[:, units], packed_high[:, units]], axis=0)
        raw = text_ref[...].astype(F32)
        inverse = inverse_norm(raw)
        unit = raw * inverse
        pairs = pair_weights(unit_all, unit.astype(BF))
        text_sum = LOGIT_SCALE * lax.dot_general(
            pairs, unit_all, (((0,), (0,)), ((), ())), preferred_element_type=F32
        )
        text_grad_ref[...] = unit_back(unit, inverse, text_sum)


def head_grads_block(packed, text_here, share, order):
    rows, width = text_here.shape
    block = 256 if share % 256 == 0 else LANES
    return pl.pallas_call(
        lambda *refs: head_grads_kernel(block, *refs),
        grid=(share // block,),
        out_shape=[
            SHAPE((share, width), F32),
            SHAPE((rows, width), F32),
            SHAPE((8, LANES), F32),
        ],
        in_specs=[VM, VM, VM, ANY],
        out_specs=[
            pl.BlockSpec((block, width), lambda step: (step, 0)),
            pl.BlockSpec((rows, width), lambda step: (0, 0)),
            pl.BlockSpec((8, LANES), lambda step: (0, 0)),
        ],
        compiler_params=params(24),
        name="head_grads_block",
    )(*near([*packed, text_here]), order)


def split_kernel(place_ref, own_ref, other_ref, kernel_ref, term_ref):
    core = place_ref[1]
    rest = TAPS - HALF_PAD
    terms = slice(TERM_ROW - HALF_PAD, TERM_ROW - HALF_PAD + 4)

    def write(low_ref, high_ref):
        kernel_ref[0:HALF_PAD, :] = low_ref[...].astype(F32)
        high = high_ref[...].astype(F32)
        kernel_ref[HALF_PAD:TAPS, :] = high[0:rest]
        term_ref[...] = high[terms]

    @pl.when(core == 0)
    def _():
        write(own_ref, other_ref)

    @pl.when(core != 0)
    def _():
        write(other_ref, own_ref)


def split_block(place, own, other):
    share = own.shape[1]
    return pl.pallas_call(
        split_kernel,
        out_shape=[SHAPE((TAPS, share), F32), SHAPE((4, share), F32)],
        in_specs=[SM, VM, VM],
        out_specs=[VM, VM],
        compiler_params=params(24),
        name="split_block",
    )(place, *near([own, other]))


def per_device(image_maps, dw_kernel, channel_terms, head_weight, text_feats):
    members = lax.axis_size("fsdp")
    member = lax.axis_index("fsdp")
    core = lax.axis_index("dp") % 2
    place = jnp.stack([member, core]).astype(jnp.int32)
    others = range(1, members)
    pair_masks = bits_up(members)
    dp_masks = bits_up(lax.axis_size("dp"))
    down = dp_masks[::-1]
    share = head_weight.shape[0]

    kernels = [swap(dw_kernel, "fsdp", m) for m in others]
    terms = [swap(channel_terms, "fsdp", m) for m in others]
    mixed_own, sum_own, weight_own, x_here, text_here = own_block(
        place, image_maps, dw_kernel, channel_terms, text_feats
    )

    text_rows = stack_rows(text_here, swap(text_feats, "fsdp", 1), sum_own)
    for mask in pair_masks[1:]:
        text_rows = stack_rows(text_rows, swap(text_rows, "fsdp", mask), sum_own)
    text_rows = stack_rows(text_rows, swap(text_rows, "dp", 1), (terms or [sum_own])[-1])
    text_masks = down[:-1]
    pieces, head_here, weight_rest, mixed_rest, saved = forward_block(
        place, head_weight, x_here, (mixed_own, sum_own, weight_own), text_rows, kernels, terms
    )
    weights = (weight_own, weight_rest)
    far_rows = swap(text_rows, "dp", text_masks[0])
    pieces = [pieces[0]] + [swap(pieces[m], "fsdp", m) for m in others]
    group, partial = head_project(pieces, head_here)
    orders = [saved[4]] + [partial] * len(text_masks)
    for mask, order in zip(text_masks[1:], orders):
        text_rows = stack_rows(text_rows, far_rows, order)
        far_rows = swap(text_rows, "dp", mask)
    texts = (text_rows, far_rows)

    partials = [partial] + [swap(partial, "fsdp", m) for m in others]
    packed, grads = loss_block(partials, texts, group, head_here)
    grads = [grads[0]] + [swap(grads[m], "fsdp", m) for m in others]

    packed = stack_rows(packed, swap(packed, "dp", down[0]), packed)
    keep, give, flow, shared = terms_block(
        place, grads, packed, x_here, weights, (mixed_own, mixed_rest), saved
    )

    parts = [(image, base) for image in range(image_maps.shape[0]) for base in (0, members // 2)]
    image_grads = None

    def image_parts(count, order, image_grads):
        token = order
        for _ in range(min(count, len(parts))):
            image, base = parts.pop(0)
            image_grads, token = image_block(
                image, base, members // 2, place, flow, weights, shared, order, image_grads
            )
        return image_grads, token

    chip = chip_sums(keep, swap(give, "dp", 1))
    gather_masks = list(down[1:])
    moving = swap(packed, "dp", gather_masks.pop(0))
    image_grads, token = image_parts(1, chip[0], None)
    sent = add_all([chip[0]] + [swap(chip[m], "fsdp", m) for m in others], token)
    ring_masks = dp_masks[1:]
    counts = [1] + [2] * len(ring_masks)
    for mask, count in zip(ring_masks[:-1], counts):
        packed = stack_rows(packed, moving, token)
        moving = swap(packed, "dp", gather_masks.pop(0))
        image_grads, token = image_parts(count, sent, image_grads)
        sent = add_all([sent, swap(sent, "dp", mask)], token)
    image_grads, token = image_parts(len(parts), sent, image_grads)
    while gather_masks:
        packed = stack_rows(packed, moving, token)
        moving = swap(packed, "dp", gather_masks.pop(0))
    head_grads, text_grads, token = head_grads_block((packed, moving), text_here, share, sent)
    sent = add_all([sent, swap(sent, "dp", ring_masks[-1])], token)
    kernel_grads, term_grads = split_block(place, sent, swap(sent, "dp", 1))
    return (image_grads, kernel_grads, term_grads, head_grads, text_grads)


def solution(mesh):
    in_specs = (
        P(("dp", "fsdp"), None, None, None),
        P(None, "fsdp"),
        P(None, "fsdp"),
        P("fsdp", None),
        P(("dp", "fsdp"), None),
    )
    out_specs = (
        P(("dp", "fsdp"), None, None, None),
        P(None, "fsdp"),
        P(None, "fsdp"),
        P("fsdp", None),
        P(("dp", "fsdp"), None),
    )
    return jax.shard_map(
        per_device, mesh=mesh, in_specs=in_specs, out_specs=out_specs, check_vma=False
    )
```

```python
import jax
import jax.numpy as jnp
from jax import lax
from jax.experimental import pallas as pl
from jax.experimental.pallas import tpu as pltpu
from jax.sharding import PartitionSpec as P

EPS = 1e-06
LOGIT_SCALE = 10.0
LOGIT_BIAS = -2.0
KER = 7
REACH = KER // 2
TAPS = KER * KER
LANES = 128
ROWS_PAD = 64
HALF_PAD = ROWS_PAD // 2
TERM_ROW = 56
GAIN_ROW = TAPS
WEIGHT_ROWS = 56
DOTS_COST = 3.0
SUM_COST = 1.0
BF = jnp.bfloat16
F32 = jnp.float32


def swap(value, axis, mask):
    count = lax.axis_size(axis)
    return lax.ppermute(value, axis, [(source, source ^ mask) for source in range(count)])


def tree_gather(value, axis, masks):
    for mask in masks:
        value = jnp.concatenate([value, swap(value, axis, mask)], axis=0)
    return value


def bits_up(count):
    masks = []
    mask = 1
    while mask < count:
        masks.append(mask)
        mask *= 2
    return masks


def params(mebibytes):
    return pltpu.CompilerParams(vmem_limit_bytes=mebibytes * 1024 * 1024)


def cost(micros):
    return pl.CostEstimate(flops=int(micros * 1.1e9), bytes_accessed=0, transcendentals=0)


def far(arrays):
    return [pltpu.with_memory_space_constraint(value, pltpu.HBM) for value in arrays]


def near(arrays):
    return [pltpu.with_memory_space_constraint(value, pltpu.VMEM) for value in arrays]


VM = pl.BlockSpec(memory_space=pltpu.VMEM)
SM = pl.BlockSpec(memory_space=pltpu.SMEM)
HB = pl.BlockSpec(memory_space=pltpu.HBM)
ANY = pl.BlockSpec(memory_space=pl.ANY)
SHAPE = jax.ShapeDtypeStruct


def lane_block(index, width):
    return pl.ds(pl.multiple_of(index * width, LANES), width)


def shift_cols(value, step):
    if step == 0:
        return value
    width = value.shape[0]
    rolled = pltpu.roll(value, (-step) % width, 0)
    col = lax.broadcasted_iota(jnp.int32, value.shape, 0)
    inside = (col < width - step) if step > 0 else (col >= -step)
    return jnp.where(inside, rolled, 0.0)


def conv_rows(rows, tap_row, flip):
    height = len(rows)
    sums = [None] * height
    for b in range(KER):
        moved = [shift_cols(row, b - REACH) for row in rows]
        for a in range(KER):
            tap = (KER - 1 - a) * KER + (KER - 1 - b) if flip else a * KER + b
            weight = tap_row(tap)
            for h in range(max(0, REACH - a), min(height, height + REACH - a)):
                term = moved[h + a - REACH] * weight
                sums[h] = term if sums[h] is None else sums[h] + term
    return sums


def stack_rows(low, high, order):
    def kernel(low_ref, high_ref, order_ref, out_ref):
        both = jnp.concatenate([low_ref[...].astype(F32), high_ref[...].astype(F32)], axis=0)
        out_ref[...] = both.astype(out_ref.dtype)

    rows, width = low.shape
    return pl.pallas_call(
        kernel,
        out_shape=SHAPE((2 * rows, width), low.dtype),
        in_specs=[VM, VM, ANY],
        out_specs=VM,
        compiler_params=params(24),
        name="stack_rows",
    )(low, high, order)


def add_all(values, order):
    def kernel(*refs):
        total = refs[0][...].astype(F32)
        for ref in refs[1:-2]:
            total = total + ref[...].astype(F32)
        refs[-1][...] = total.astype(BF)

    return pl.pallas_call(
        kernel,
        out_shape=SHAPE(values[0].shape, BF),
        in_specs=[VM] * len(values) + [ANY],
        out_specs=VM,
        compiler_params=params(24),
        name="add_all",
    )(*values, order)


def hold(value, order):
    def kernel(value_ref, order_ref, out_ref):
        out_ref[...] = value_ref[...]

    return pl.pallas_call(
        kernel,
        out_shape=SHAPE(value.shape, value.dtype),
        in_specs=[VM, ANY],
        out_specs=VM,
        compiler_params=params(24),
        name="hold",
    )(value, order)


def chip_sums(keep, give, order):
    members = keep.shape[0]

    def kernel(keep_ref, give_ref, order_ref, *out_refs):
        for m in range(members):
            out_refs[m][...] = (keep_ref[m].astype(F32) + give_ref[m].astype(F32)).astype(BF)

    return pl.pallas_call(
        kernel,
        out_shape=[SHAPE(keep.shape[1:], BF)] * members,
        in_specs=[VM, VM, ANY],
        out_specs=[VM] * members,
        compiler_params=params(24),
        name="chip_sums",
    )(keep, give, order)


def tile_of(base_piece, t, member, share):
    per_piece = share // LANES
    piece = base_piece + t // per_piece
    return lane_block((member ^ piece) * per_piece + t % per_piece, LANES)


def conv_tiles(tiles, base_piece, member, share, x_ref, weight_ref, mixed_ref, sum_ref):
    images, height = x_ref.shape[:2]

    @pl.loop(0, tiles)
    def _(t):
        lanes = lane_block(t, LANES)
        source = tile_of(base_piece, t, member, share)
        bias = weight_ref[GAIN_ROW : GAIN_ROW + 1, lanes]
        for i in range(images):
            rows = [x_ref[i, h, :, source].astype(F32) for h in range(height)]
            sums = conv_rows(rows, lambda tap: weight_ref[tap : tap + 1, lanes], False)
            for h in range(height):
                value = sums[h] + bias
                mixed_ref[i, h, :, lanes] = value
                sum_ref[i, h] += value


def text_chunks(embed_width, share):
    return [
        (chunk, first, min(share, embed_width - first))
        for chunk, first in enumerate(range(0, embed_width, share))
    ]


def pack_rows(texts, embed_width, share):
    return (4 + texts * len(text_chunks(embed_width, share)) + 7) // 8 * 8


def load_kernel(x_hbm, kernel_hbm, term_hbm, text_hbm, x_ref, weight_ref, text_ref, kernel_ref, term_ref, sems):
    copies = [
        pltpu.make_async_copy(kernel_hbm, kernel_ref, sems.at[0]),
        pltpu.make_async_copy(term_hbm, term_ref, sems.at[1]),
        pltpu.make_async_copy(text_hbm, text_ref, sems.at[2]),
        pltpu.make_async_copy(x_hbm, x_ref, sems.at[3]),
    ]
    for copy in copies:
        copy.start()
    for copy in copies[:3]:
        copy.wait()
    weight_ref[0:TAPS, :] = kernel_ref[...].astype(F32)
    weight_ref[GAIN_ROW : GAIN_ROW + 4, :] = term_ref[...].astype(F32)
    copies[3].wait()


def load_block(image_maps, dw_kernel, channel_terms, text_feats):
    share = dw_kernel.shape[1]
    return pl.pallas_call(
        load_kernel,
        out_shape=[
            SHAPE(image_maps.shape, BF),
            SHAPE((WEIGHT_ROWS, share), F32),
            SHAPE(text_feats.shape, BF),
        ],
        in_specs=[HB, HB, HB, HB],
        out_specs=[VM] * 3,
        scratch_shapes=[
            pltpu.VMEM(dw_kernel.shape, BF),
            pltpu.VMEM(channel_terms.shape, BF),
            pltpu.SemaphoreType.DMA((4,)),
        ],
        compiler_params=params(24),
        name="load_block",
    )(*far([image_maps, dw_kernel, channel_terms, text_feats]))


def pack_block(weight_own, text_here, text_core):
    images, embed_width = text_here.shape
    share = weight_own.shape[1]
    texts = 2 * images
    rows = pack_rows(texts, embed_width, share)

    def kernel(weight_ref, here_ref, core_ref, packed_ref, rows_ref):
        rows_ref[...] = jnp.zeros_like(rows_ref)
        rows_ref[0:4, :] = weight_ref[GAIN_ROW : GAIN_ROW + 4, :]
        both = jnp.concatenate([here_ref[...].astype(F32), core_ref[...].astype(F32)], axis=0)
        for chunk, first, width in text_chunks(embed_width, share):
            row = 4 + chunk * texts
            rows_ref[row : row + texts, 0:width] = both[:, first : first + width]
        packed_ref[...] = rows_ref[...].astype(BF)

    return pl.pallas_call(
        kernel,
        out_shape=SHAPE((rows, share), BF),
        in_specs=[VM] * 3,
        out_specs=VM,
        scratch_shapes=[pltpu.VMEM((rows, share), F32)],
        compiler_params=params(24),
        name="pack_block",
    )(*near([weight_own, text_here, text_core]))


def text_stack(text_here, text_core, packs, order):
    images, embed_width = text_here.shape
    share = packs[0].shape[1]
    members = len(packs) + 1
    total = 2 * members * images

    def kernel(*refs):
        here_ref, core_ref, pack_refs, out_ref, rows_ref = refs[0], refs[1], refs[2 : members + 1], refs[-2], refs[-1]
        half = members * images
        rows_ref[0:images, :] = here_ref[...].astype(F32)
        rows_ref[half : half + images, :] = core_ref[...].astype(F32)
        for m in range(1, members):
            pack = pack_refs[m - 1][...].astype(F32)
            for chunk, first, width in text_chunks(embed_width, share):
                for core in range(2):
                    row = 4 + (chunk * 2 + core) * images
                    place = core * half + m * images
                    rows_ref[place : place + images, first : first + width] = pack[
                        row : row + images, 0:width
                    ]
        out_ref[...] = rows_ref[...].astype(BF)

    return pl.pallas_call(
        kernel,
        out_shape=SHAPE((total, embed_width), BF),
        in_specs=[VM] * (members + 1) + [ANY],
        out_specs=VM,
        scratch_shapes=[pltpu.VMEM((total, embed_width), F32)],
        compiler_params=params(24),
        name="text_stack",
    )(text_here, text_core, *packs, order)


def own_block(place, x_here, weight_own):
    images, height, width, channels = x_here.shape
    share = weight_own.shape[1]

    def kernel(place_ref, x_ref, weight_ref, mixed_ref, sum_ref):
        sum_ref[...] = jnp.zeros_like(sum_ref)
        conv_tiles(share // LANES, 0, place_ref[0], share, x_ref, weight_ref, mixed_ref, sum_ref)

    return pl.pallas_call(
        kernel,
        out_shape=[
            SHAPE((images, height, width, share), F32),
            SHAPE((images, height, width, LANES), F32),
        ],
        in_specs=[SM, VM, VM],
        out_specs=[VM] * 2,
        compiler_params=params(24),
        name="own_block",
    )(place, *near([x_here, weight_own]))


def forward_kernel(members, place_ref, head_hbm, x_ref, mixed_own, sum_own, weight_own, order_ref, *refs):
    kernel_refs, refs = refs[: members - 1], refs[members - 1 :]
    pack_refs, refs = refs[: members - 1], refs[members - 1 :]
    piece_refs, refs = refs[:members], refs[members:]
    head_ref, weight_rest, mixed_rest, mean_ref, rstd_ref, hatsum_ref, hat_ref, hrstd_ref, sum_ref, pool_ref, sem = refs
    images, height, width, channels = x_ref.shape
    share = channels // members
    cells = height * width
    member = place_ref[0]
    head_copy = pltpu.make_async_copy(head_hbm, head_ref, sem)
    head_copy.start()
    for m in range(1, members):
        lanes = slice((m - 1) * share, m * share)
        weight_rest[0:TAPS, lanes] = kernel_refs[m - 1][...].astype(F32)
        weight_rest[GAIN_ROW : GAIN_ROW + 4, lanes] = pack_refs[m - 1][...].astype(F32)[0:4]
    sum_ref[...] = sum_own[...]
    own_tiles = share // LANES
    rest_tiles = (members - 1) * own_tiles
    conv_tiles(rest_tiles, 1, member, share, x_ref, weight_rest, mixed_rest, sum_ref)
    parts = [(0, own_tiles, mixed_own, weight_own), (1, rest_tiles, mixed_rest, weight_rest)]

    mean = jnp.sum(sum_ref[...], axis=-1, keepdims=True) * (1.0 / channels)
    mean_ref[...] = jnp.broadcast_to(mean, mean_ref.shape)
    sum_ref[...] = jnp.zeros_like(sum_ref)
    for base, tiles, mixed_ref, weight_ref in parts:

        @pl.loop(0, tiles)
        def _(t):
            lanes = lane_block(t, LANES)
            for i in range(images):
                for h in range(height):
                    value = mixed_ref[i, h, :, lanes] - mean_ref[i, h]
                    sum_ref[i, h] += value * value

    var = jnp.sum(sum_ref[...], axis=-1, keepdims=True) * (1.0 / channels)
    rstd_ref[...] = jnp.broadcast_to(lax.rsqrt(var + EPS), rstd_ref.shape)
    for base, tiles, mixed_ref, weight_ref in parts:

        @pl.loop(0, tiles)
        def _(t):
            lanes = lane_block(t, LANES)
            wide = lane_block(t + base * own_tiles, LANES)
            source = tile_of(base, t, member, share)
            scale = (
                weight_ref[GAIN_ROW + 1 : GAIN_ROW + 2, lanes]
                * weight_ref[GAIN_ROW + 2 : GAIN_ROW + 3, lanes]
            )
            for i in range(images):
                hats = jnp.zeros((width, LANES), F32)
                plain = jnp.zeros((width, LANES), F32)
                for h in range(height):
                    hats = hats + (mixed_ref[i, h, :, lanes] - mean_ref[i, h]) * rstd_ref[i, h]
                    plain = plain + x_ref[i, h, :, source].astype(F32)
                hat_row = jnp.sum(hats, axis=0, keepdims=True)
                hatsum_ref[i : i + 1, wide] = hat_row
                pool_ref[i : i + 1, wide] = (
                    jnp.sum(plain, axis=0, keepdims=True) + scale * hat_row
                ) * (1.0 / cells)

    pooled = pool_ref[...]
    centered = pooled - jnp.mean(pooled, axis=1, keepdims=True)
    head_rstd = lax.rsqrt(jnp.mean(centered * centered, axis=1, keepdims=True) + EPS)
    hat = centered * head_rstd
    hat_ref[...] = hat
    hrstd_ref[...] = jnp.broadcast_to(head_rstd, hrstd_ref.shape)
    for m in range(members):
        gain = (
            weight_own[GAIN_ROW + 3 : GAIN_ROW + 4, :]
            if m == 0
            else weight_rest[GAIN_ROW + 3 : GAIN_ROW + 4, (m - 1) * share : m * share]
        )
        piece_refs[m][...] = (hat[:, m * share : (m + 1) * share] * gain).astype(BF)
    head_copy.wait()


def forward_block(place, head_weight, x_here, own, order, kernels, packs):
    images, height, width, channels = x_here.shape
    members = len(packs) + 1
    share = channels // members
    cell = (images, height, width, LANES)
    outs = [SHAPE((images, share), BF)] * members + [
        SHAPE(head_weight.shape, BF),
        SHAPE((WEIGHT_ROWS, channels - share), F32),
        SHAPE((images, height, width, channels - share), F32),
        SHAPE(cell, F32),
        SHAPE(cell, F32),
        SHAPE((images, channels), F32),
        SHAPE((images, channels), F32),
        SHAPE((images, LANES), F32),
    ]
    result = pl.pallas_call(
        lambda *refs: forward_kernel(members, *refs),
        out_shape=outs,
        in_specs=[SM, HB, VM, VM, VM, VM, ANY] + [VM] * (2 * (members - 1)),
        out_specs=[VM] * len(outs),
        scratch_shapes=[
            pltpu.VMEM(cell, F32),
            pltpu.VMEM((images, channels), F32),
            pltpu.SemaphoreType.DMA,
        ],
        compiler_params=params(24),
        name="forward_block",
    )(place, *far([head_weight]), *near([x_here, *own]), order, *near([*kernels, *packs]))
    return result[:members], result[members], result[members + 1], result[members + 2], result[members + 3 :]


def head_kernel(members, *refs):
    group = jnp.concatenate([ref[...].astype(F32) for ref in refs[:members]], axis=0).astype(BF)
    weight_ref, group_ref, out_ref = refs[members:]
    group_ref[...] = group
    out_ref[...] = jnp.dot(group, weight_ref[...], preferred_element_type=F32)


def head_project(pieces, head_weight):
    members = len(pieces)
    share, embed_width = head_weight.shape
    rows = members * pieces[0].shape[0]
    return pl.pallas_call(
        lambda *refs: head_kernel(members, *refs),
        out_shape=[SHAPE((rows, share), BF), SHAPE((rows, embed_width), F32)],
        in_specs=[VM] * (members + 1),
        out_specs=[VM, VM],
        compiler_params=params(24),
        cost_estimate=cost(0.5),
        name="head_project",
    )(*near([*pieces, head_weight]))


def inverse_norm(vectors):
    return lax.rsqrt(jnp.sum(vectors * vectors, axis=1, keepdims=True) + EPS)


def pair_weights(images, texts):
    logits = (
        LOGIT_SCALE
        * lax.dot_general(images, texts, (((1,), (1,)), ((), ())), preferred_element_type=F32)
        + LOGIT_BIAS
    )
    here = lax.broadcasted_iota(jnp.int32, logits.shape, 0)
    there = lax.broadcasted_iota(jnp.int32, logits.shape, 1)
    positive = jnp.where(here == there, 1.0, 0.0).astype(F32)
    return (jax.nn.sigmoid(logits) - positive).astype(BF)


def unit_back(unit, inverse, grad):
    return inverse * (grad - unit * jnp.sum(unit * grad, axis=1, keepdims=True))


def embed_sum_kernel(members, *refs):
    total_rows = refs[0].shape[0]
    rows = total_rows // members
    embed = refs[0][...]
    for m in range(1, members):
        embed = embed + jnp.concatenate(
            [refs[m][(k ^ m) * rows : (k ^ m) * rows + rows, :] for k in range(members)], axis=0
        )
    refs[members][...] = embed


def embed_sum(partials):
    members = len(partials)
    return pl.pallas_call(
        lambda *refs: embed_sum_kernel(members, *refs),
        out_shape=SHAPE(partials[0].shape, F32),
        in_specs=[VM] * members,
        out_specs=VM,
        compiler_params=params(24),
        cost_estimate=cost(SUM_COST),
        name="embed_sum",
    )(*near(partials))


def loss_kernel(members, embed_ref, text_low, text_high, group_ref, weight_ref, packed_ref, *piece_refs):
    total_rows, width = embed_ref.shape
    rows = total_rows // members
    share = group_ref.shape[1]
    embed = embed_ref[...]
    inverse = inverse_norm(embed)
    unit = embed * inverse
    unit_bf = unit.astype(BF)
    raw = jnp.concatenate([text_low[...], text_high[...]], axis=0).astype(F32)
    texts = (raw * inverse_norm(raw)).astype(BF)
    unit_grad = LOGIT_SCALE * jnp.dot(
        pair_weights(unit_bf, texts), texts, preferred_element_type=F32
    )
    embed_grad = unit_back(unit, inverse, unit_grad).astype(BF)
    packed_ref[:, 0:share] = group_ref[...]
    packed_ref[:, share : share + width] = embed_grad
    packed_ref[:, share + width : share + 2 * width] = unit_bf
    part = lax.dot_general(
        embed_grad, weight_ref[...], (((1,), (1,)), ((), ())), preferred_element_type=F32
    )
    for m in range(members):
        piece_refs[m][...] = part[m * rows : m * rows + rows]


def loss_block(members, embed, texts, group, head_weight):
    total_rows, embed_width = embed.shape
    share = head_weight.shape[0]
    result = pl.pallas_call(
        lambda *refs: loss_kernel(members, *refs),
        out_shape=[SHAPE((total_rows, share + 2 * embed_width), BF)]
        + [SHAPE((total_rows // members, share), F32)] * members,
        in_specs=[VM] * 5,
        out_specs=[VM] * (members + 1),
        compiler_params=params(24),
        name="loss_block",
    )(*near([embed, *texts, group, head_weight]))
    return result[0], result[1:]


def pool_grad_kernel(members, cells, *refs):
    grad_refs, refs = refs[:members], refs[members:]
    weight_own, weight_rest, hatsum_ref, hat_ref, hrstd_ref, shared_ref, scaled_ref, rows_ref = refs

    def term_row(row):
        return jnp.concatenate(
            [weight_own[GAIN_ROW + row : GAIN_ROW + row + 1, :], weight_rest[GAIN_ROW + row : GAIN_ROW + row + 1, :]],
            axis=1,
        )

    grad = jnp.concatenate([ref[...] for ref in grad_refs], axis=1)
    hat = hat_ref[...]
    inner = grad * term_row(3)
    shared = (
        hrstd_ref[:, 0:1]
        * (
            inner
            - jnp.mean(inner, axis=1, keepdims=True)
            - hat * jnp.mean(inner * hat, axis=1, keepdims=True)
        )
        * (1.0 / cells)
    )
    shared_ref[...] = shared
    gain = term_row(1)
    scale = term_row(2)
    hat_total = jnp.sum(shared * hatsum_ref[...], axis=0, keepdims=True)
    rows_ref[...] = jnp.zeros_like(rows_ref)
    rows_ref[1:2, :] = hat_total * scale
    rows_ref[2:3, :] = hat_total * gain
    rows_ref[3:4, :] = jnp.sum(grad * hat, axis=0, keepdims=True)
    scaled = shared * (gain * scale)
    scaled_ref[...] = scaled - jnp.mean(scaled, axis=1, keepdims=True)


def pool_grad_block(grads, cells, weights, hatsum, hat, hrstd):
    members = len(grads)
    images, channels = hat.shape
    return pl.pallas_call(
        lambda *refs: pool_grad_kernel(members, cells, *refs),
        out_shape=[
            SHAPE((images, channels), F32),
            SHAPE((images, channels), F32),
            SHAPE((8, channels), F32),
        ],
        in_specs=[VM] * (members + 5),
        out_specs=[VM] * 3,
        compiler_params=params(24),
        cost_estimate=cost(0.4),
        name="pool_grad_block",
    )(*near([*grads, *weights, hatsum, hat, hrstd]))


def dots_kernel(scaled_ref, mixed_own, mixed_rest, mean_ref, rstd_ref, dot_ref):
    images, height = dot_ref.shape[:2]
    channels = scaled_ref.shape[1]
    own_tiles = mixed_own.shape[3] // LANES
    rest_tiles = mixed_rest.shape[3] // LANES
    dot_ref[...] = jnp.zeros_like(dot_ref)
    for first, tiles, mixed_ref in [(0, own_tiles, mixed_own), (own_tiles, rest_tiles, mixed_rest)]:

        @pl.loop(0, tiles)
        def _(t):
            lanes = lane_block(t, LANES)
            wide = lane_block(t + first, LANES)
            for i in range(images):
                factor = scaled_ref[i : i + 1, wide]
                for h in range(height):
                    dot_ref[i, h] += factor * (mixed_ref[i, h, :, lanes] - mean_ref[i, h])

    dots = jnp.sum(dot_ref[...], axis=-1, keepdims=True) * (1.0 / channels)
    dot_ref[...] = jnp.broadcast_to(dots, dot_ref.shape) * rstd_ref[...] * rstd_ref[...]


def dots_block(scaled, mixed, mean, rstd):
    return pl.pallas_call(
        dots_kernel,
        out_shape=SHAPE(mean.shape, F32),
        in_specs=[VM] * 5,
        out_specs=VM,
        compiler_params=params(24),
        cost_estimate=cost(DOTS_COST),
        name="dots_block",
    )(*near([scaled, *mixed, mean, rstd]))


def terms_kernel(base, share, place_ref, x_ref, scaled_ref, rows_ref, mixed_ref, mean_ref, rstd_ref, dot_ref, *refs):
    keep_ref, give_ref, flow_ref, sums_ref, taps_ref = refs
    images, height, width = x_ref.shape[:3]
    channels = mixed_ref.shape[3]
    own_tiles = share // LANES
    member = place_ref[0]
    core = place_ref[1]
    first = base * share
    sums_ref[TAPS // 8 * 8 : TERM_ROW, :] = jnp.zeros((TERM_ROW - TAPS // 8 * 8, channels), F32)
    sums_ref[TERM_ROW:ROWS_PAD, :] = rows_ref[:, first : first + channels]

    @pl.loop(0, channels // LANES)
    def _(t):
        lanes = lane_block(t, LANES)
        wide = lane_block(t + base * own_tiles, LANES)
        source = tile_of(base, t, member, share)
        flows = []
        for i in range(images):
            factor = scaled_ref[i : i + 1, wide]
            flow_rows = []
            for h in range(height):
                centered = mixed_ref[i, h, :, lanes] - mean_ref[i, h]
                flow = rstd_ref[i, h] * (factor - centered * dot_ref[i, h])
                flow_ref[i, h, :, lanes] = flow
                flow_rows.append(flow)
            flows.append(flow_rows)
        bias = flows[0][0]
        for i in range(images):
            for h in range(height):
                if i or h:
                    bias = bias + flows[i][h]
        taps_ref[TAPS * width : TAPS * width + width, :] = bias
        for b in range(KER):
            totals = [None] * KER
            for i in range(images):
                moved = [
                    shift_cols(x_ref[i, h, :, source].astype(F32), b - REACH)
                    for h in range(height)
                ]
                for a in range(KER):
                    for h in range(max(0, REACH - a), min(height, height + REACH - a)):
                        term = flows[i][h] * moved[h + a - REACH]
                        totals[a] = term if totals[a] is None else totals[a] + term
            for a in range(KER):
                tap = a * KER + b
                taps_ref[tap * width : tap * width + width, :] = totals[a]
        rows = TAPS + 1
        total = taps_ref[pl.ds(0, rows, stride=width), :]
        for s in range(1, width):
            total = total + taps_ref[pl.ds(s, rows, stride=width), :]
        sums_ref[0:TAPS, lanes] = total[0:TAPS]
        sums_ref[TERM_ROW : TERM_ROW + 1, lanes] = total[TAPS : TAPS + 1]

    for m in range(channels // share):
        lanes = slice(m * share, (m + 1) * share)
        keep_ref[m] = sums_ref[pl.ds(pl.multiple_of(core * HALF_PAD, HALF_PAD), HALF_PAD), lanes].astype(BF)
        give_ref[m] = sums_ref[pl.ds(pl.multiple_of((1 - core) * HALF_PAD, HALF_PAD), HALF_PAD), lanes].astype(BF)


def terms_block(base, share, place, order, x_here, scaled, rows, mixed, mean, rstd, dots):
    width = x_here.shape[2]
    channels = mixed.shape[3]
    half = SHAPE((channels // share, HALF_PAD, share), BF)
    return pl.pallas_call(
        lambda place_ref, order_ref, *refs: terms_kernel(base, share, place_ref, *refs),
        out_shape=[half, half, SHAPE(mixed.shape, F32)],
        in_specs=[SM, ANY] + [VM] * 7,
        out_specs=[VM] * 3,
        scratch_shapes=[
            pltpu.VMEM((ROWS_PAD, channels), F32),
            pltpu.VMEM(((TAPS + 1) * width, LANES), F32),
        ],
        compiler_params=params(24),
        name="terms_block",
    )(place, order, *near([x_here, scaled, rows, mixed, mean, rstd, dots]))


def images_kernel(image, base, place_ref, flow_own, flow_rest, weight_own, weight_rest, shared_ref, out_ref, token_ref):
    height = flow_own.shape[1]
    share = weight_own.shape[1]
    own_tiles = share // LANES
    step = pl.program_id(0) + base
    token_ref[...] = jnp.zeros_like(token_ref)

    def piece(flow_ref, weight_ref, first):
        @pl.loop(0, own_tiles)
        def _(t):
            lanes = lane_block(t, LANES)
            wide = lane_block(t + step * own_tiles, LANES)
            near_lanes = lane_block(t + (step - first) * own_tiles, LANES)
            rows = [flow_ref[image, h, :, near_lanes] for h in range(height)]
            sums = conv_rows(rows, lambda tap: weight_ref[tap : tap + 1, near_lanes], True)
            for h in range(height):
                out_ref[0, h, :, lanes] = (sums[h] + shared_ref[image : image + 1, wide]).astype(BF)

    if base == 0:

        @pl.when(step == 0)
        def _():
            piece(flow_own, weight_own, 0)

    @pl.when(step != 0)
    def _():
        piece(flow_rest, weight_rest, 1)


def image_block(image, base, count, place, flow, weights, shared, order, out):
    first = out is None
    share = weights[0].shape[1]
    operands = [place, *near([*flow, *weights, shared]), order] + ([] if first else [out])

    def kernel(*refs):
        images_kernel(image, base, *refs[:6], refs[-2], refs[-1])

    return pl.pallas_call(
        kernel,
        grid_spec=pltpu.PrefetchScalarGridSpec(
            num_scalar_prefetch=1,
            grid=(count,),
            in_specs=[VM] * 5 + [ANY] + ([] if first else [HB]),
            out_specs=[
                pl.BlockSpec(
                    (1,) + flow[0].shape[1:3] + (share,),
                    lambda step, place_ref: (image, 0, 0, place_ref[0] ^ (step + base)),
                ),
                pl.BlockSpec((8, LANES), lambda step, place_ref: (0, 0)),
            ],
        ),
        out_shape=[
            SHAPE(flow[0].shape[:3] + (shared.shape[1],), BF),
            SHAPE((8, LANES), F32),
        ],
        input_output_aliases={} if first else {7: 0},
        compiler_params=params(24),
        cost_estimate=cost(1.5),
        name="image_block",
    )(*operands)


def head_grads_kernel(block, packed_low, packed_high, text_ref, order_ref, head_ref, text_grad_ref, token_ref):
    share = packed_low.shape[1] - 2 * text_ref.shape[1]
    width = text_ref.shape[1]
    step = pl.program_id(0)
    lanes = lane_block(step, block)
    grads = slice(share, share + width)
    images = jnp.concatenate([packed_low[:, lanes], packed_high[:, lanes]], axis=0)
    grad = jnp.concatenate([packed_low[:, grads], packed_high[:, grads]], axis=0)
    head_ref[...] = lax.dot_general(
        images, grad, (((0,), (0,)), ((), ())), preferred_element_type=F32
    )

    @pl.when(step == 0)
    def _():
        token_ref[...] = jnp.zeros_like(token_ref)
        units = slice(share + width, share + 2 * width)
        unit_all = jnp.concatenate([packed_low[:, units], packed_high[:, units]], axis=0)
        raw = text_ref[...].astype(F32)
        inverse = inverse_norm(raw)
        unit = raw * inverse
        pairs = pair_weights(unit_all, unit.astype(BF))
        text_sum = LOGIT_SCALE * lax.dot_general(
            pairs, unit_all, (((0,), (0,)), ((), ())), preferred_element_type=F32
        )
        text_grad_ref[...] = unit_back(unit, inverse, text_sum)


def head_grads_block(packed, text_here, share, order):
    rows, width = text_here.shape
    block = 256 if share % 256 == 0 else LANES
    return pl.pallas_call(
        lambda *refs: head_grads_kernel(block, *refs),
        grid=(share // block,),
        out_shape=[
            SHAPE((share, width), F32),
            SHAPE((rows, width), F32),
            SHAPE((8, LANES), F32),
        ],
        in_specs=[VM, VM, VM, ANY],
        out_specs=[
            pl.BlockSpec((block, width), lambda step: (step, 0)),
            pl.BlockSpec((rows, width), lambda step: (0, 0)),
            pl.BlockSpec((8, LANES), lambda step: (0, 0)),
        ],
        compiler_params=params(24),
        name="head_grads_block",
    )(*near([*packed, text_here]), order)


def split_kernel(place_ref, own_ref, other_ref, kernel_ref, term_ref):
    core = place_ref[1]
    rest = TAPS - HALF_PAD
    terms = slice(TERM_ROW - HALF_PAD, TERM_ROW - HALF_PAD + 4)

    def write(low_ref, high_ref):
        kernel_ref[0:HALF_PAD, :] = low_ref[...].astype(F32)
        high = high_ref[...].astype(F32)
        kernel_ref[HALF_PAD:TAPS, :] = high[0:rest]
        term_ref[...] = high[terms]

    @pl.when(core == 0)
    def _():
        write(own_ref, other_ref)

    @pl.when(core != 0)
    def _():
        write(other_ref, own_ref)


def split_block(place, own, other):
    share = own.shape[1]
    return pl.pallas_call(
        split_kernel,
        out_shape=[SHAPE((TAPS, share), F32), SHAPE((4, share), F32)],
        in_specs=[SM, VM, VM],
        out_specs=[VM, VM],
        compiler_params=params(24),
        name="split_block",
    )(place, *near([own, other]))


def per_device(image_maps, dw_kernel, channel_terms, head_weight, text_feats):
    members = lax.axis_size("fsdp")
    member = lax.axis_index("fsdp")
    core = lax.axis_index("dp") % 2
    place = jnp.stack([member, core]).astype(jnp.int32)
    others = range(1, members)
    dp_masks = bits_up(lax.axis_size("dp"))
    down = dp_masks[::-1]
    share = head_weight.shape[0]

    kernels = [swap(dw_kernel, "fsdp", m) for m in others]
    text_core = swap(text_feats, "dp", 1)
    x_here, weight_own, text_here = load_block(image_maps, dw_kernel, channel_terms, text_feats)
    pack_own = pack_block(weight_own, text_here, text_core)
    packs = [swap(pack_own, "fsdp", m) for m in others]
    mixed_own, sum_own = own_block(place, x_here, weight_own)

    text_rows = text_stack(text_here, text_core, packs, sum_own)
    text_masks = down[:-1]
    pieces, head_here, weight_rest, mixed_rest, saved = forward_block(
        place, head_weight, x_here, (mixed_own, sum_own, weight_own), text_rows, kernels, packs
    )
    weights = (weight_own, weight_rest)
    far_rows = swap(text_rows, "dp", text_masks[0])
    pieces = [pieces[0]] + [swap(pieces[m], "fsdp", m) for m in others]
    group, partial = head_project(pieces, head_here)
    orders = [saved[4]] + [partial] * len(text_masks)
    for mask, order in zip(text_masks[1:], orders):
        text_rows = stack_rows(text_rows, far_rows, order)
        far_rows = swap(text_rows, "dp", mask)
    texts = (text_rows, far_rows)

    partials = [partial] + [swap(partial, "fsdp", m) for m in others]
    packed, grads = loss_block(members, embed_sum(partials), texts, group, head_here)
    grads = [grads[0]] + [swap(grads[m], "fsdp", m) for m in others]

    mean, rstd, hatsum, hat, hrstd = saved
    cells = image_maps.shape[1] * image_maps.shape[2]
    shared, scaled, term_rows = pool_grad_block(grads, cells, weights, hatsum, hat, hrstd)
    mixed = (mixed_own, mixed_rest)
    dots = dots_block(scaled, mixed, mean, rstd)
    moving = swap(packed, "dp", down[0])

    def terms_part(base, mixed_part, order):
        return terms_block(
            base, share, place, order, x_here, scaled, term_rows, mixed_part, mean, rstd, dots
        )

    packed = stack_rows(packed, moving, dots)
    keep_rest, give_rest, flow_rest = terms_part(1, mixed_rest, packed)
    keep_own, give_own, flow_own = terms_part(0, mixed_own, keep_rest)
    flow = (flow_own, flow_rest)

    parts = [(image, base) for image in range(image_maps.shape[0]) for base in (0, members // 2)]
    image_grads = None

    def image_parts(count, order, image_grads):
        token = order
        for _ in range(min(count, len(parts))):
            image, base = parts.pop(0)
            image_grads, token = image_block(
                image, base, members // 2, place, flow, weights, shared, order, image_grads
            )
        return image_grads, token

    chip = chip_sums(keep_rest, swap(give_rest, "dp", 1), keep_own)
    chip_own = chip_sums(keep_own, swap(give_own, "dp", 1), chip[0])[0]
    gather_masks = list(down[1:])
    image_grads, token = image_parts(1, chip[0], None)
    packed = hold(packed, token)
    moving = swap(packed, "dp", gather_masks.pop(0))
    sent = add_all([chip_own] + [swap(chip[m - 1], "fsdp", m) for m in others], token)
    ring_masks = dp_masks[1:]
    counts = [1] + [2] * len(ring_masks)
    for mask, count in zip(ring_masks[:-1], counts):
        image_grads, token = image_parts(count, sent, image_grads)
        if mask == ring_masks[0]:
            packed = stack_rows(packed, moving, token)
            moving = swap(packed, "dp", gather_masks.pop(0))
        sent = add_all([sent, swap(sent, "dp", mask)], token)
    image_grads, token = image_parts(len(parts), sent, image_grads)
    while gather_masks:
        packed = stack_rows(packed, moving, token)
        moving = swap(packed, "dp", gather_masks.pop(0))
    head_grads, text_grads, token = head_grads_block((packed, moving), text_here, share, sent)
    sent = add_all([sent, swap(sent, "dp", ring_masks[-1])], token)
    kernel_grads, term_grads = split_block(place, sent, swap(sent, "dp", 1))
    return (image_grads, kernel_grads, term_grads, head_grads, text_grads)


def solution(mesh):
    in_specs = (
        P(("dp", "fsdp"), None, None, None),
        P(None, "fsdp"),
        P(None, "fsdp"),
        P("fsdp", None),
        P(("dp", "fsdp"), None),
    )
    out_specs = (
        P(("dp", "fsdp"), None, None, None),
        P(None, "fsdp"),
        P(None, "fsdp"),
        P("fsdp", None),
        P(("dp", "fsdp"), None),
    )
    return jax.shard_map(
        per_device, mesh=mesh, in_specs=in_specs, out_specs=out_specs, check_vma=False
    )
```

```python
import jax
import jax.numpy as jnp
from jax import lax
from jax.experimental import pallas as pl
from jax.experimental.pallas import tpu as pltpu
from jax.sharding import PartitionSpec as P

EPS = 1e-06
LOGIT_SCALE = 10.0
LOGIT_BIAS = -2.0
KER = 7
REACH = KER // 2
TAPS = KER * KER
LANES = 128
ROWS_PAD = 64
HALF_PAD = ROWS_PAD // 2
TERM_ROW = 56
GAIN_ROW = TAPS
WEIGHT_ROWS = 56
GROUP = 4
DOTS_COST = 3.0
SUM_COST = 1.0
BF = jnp.bfloat16
F32 = jnp.float32


def swap(value, axis, mask):
    count = lax.axis_size(axis)
    return lax.ppermute(value, axis, [(source, source ^ mask) for source in range(count)])


def tree_gather(value, axis, masks):
    for mask in masks:
        value = jnp.concatenate([value, swap(value, axis, mask)], axis=0)
    return value


def bits_up(count):
    masks = []
    mask = 1
    while mask < count:
        masks.append(mask)
        mask *= 2
    return masks


def params(mebibytes):
    return pltpu.CompilerParams(vmem_limit_bytes=mebibytes * 1024 * 1024)


def cost(micros):
    return pl.CostEstimate(flops=int(micros * 1.1e9), bytes_accessed=0, transcendentals=0)


def far(arrays):
    return [pltpu.with_memory_space_constraint(value, pltpu.HBM) for value in arrays]


def near(arrays):
    return [pltpu.with_memory_space_constraint(value, pltpu.VMEM) for value in arrays]


VM = pl.BlockSpec(memory_space=pltpu.VMEM)
SM = pl.BlockSpec(memory_space=pltpu.SMEM)
HB = pl.BlockSpec(memory_space=pltpu.HBM)
ANY = pl.BlockSpec(memory_space=pl.ANY)
SHAPE = jax.ShapeDtypeStruct


def lane_block(index, width):
    return pl.ds(pl.multiple_of(index * width, LANES), width)


def shift_cols(value, step):
    if step == 0:
        return value
    width = value.shape[0]
    rolled = pltpu.roll(value, (-step) % width, 0)
    col = lax.broadcasted_iota(jnp.int32, value.shape, 0)
    inside = (col < width - step) if step > 0 else (col >= -step)
    return jnp.where(inside, rolled, 0.0)


def conv_rows(rows, tap_row, flip):
    height = len(rows)
    sums = [None] * height
    for b in range(KER):
        moved = [shift_cols(row, b - REACH) for row in rows]
        for a in range(KER):
            tap = (KER - 1 - a) * KER + (KER - 1 - b) if flip else a * KER + b
            weight = tap_row(tap)
            for h in range(max(0, REACH - a), min(height, height + REACH - a)):
                term = moved[h + a - REACH] * weight
                sums[h] = term if sums[h] is None else sums[h] + term
    return sums


def stack_rows(low, high, order):
    def kernel(low_ref, high_ref, order_ref, out_ref):
        both = jnp.concatenate([low_ref[...].astype(F32), high_ref[...].astype(F32)], axis=0)
        out_ref[...] = both.astype(out_ref.dtype)

    rows, width = low.shape
    return pl.pallas_call(
        kernel,
        out_shape=SHAPE((2 * rows, width), low.dtype),
        in_specs=[VM, VM, ANY],
        out_specs=VM,
        compiler_params=params(24),
        name="stack_rows",
    )(low, high, order)


def add_all(values, order):
    def kernel(*refs):
        total = refs[0][...].astype(F32)
        for ref in refs[1:-2]:
            total = total + ref[...].astype(F32)
        refs[-1][...] = total.astype(BF)

    return pl.pallas_call(
        kernel,
        out_shape=SHAPE(values[0].shape, BF),
        in_specs=[VM] * len(values) + [ANY],
        out_specs=VM,
        compiler_params=params(24),
        name="add_all",
    )(*values, order)


def hold(value, order):
    def kernel(value_ref, order_ref, out_ref):
        out_ref[...] = value_ref[...]

    return pl.pallas_call(
        kernel,
        out_shape=SHAPE(value.shape, value.dtype),
        in_specs=[VM, ANY],
        out_specs=VM,
        compiler_params=params(24),
        name="hold",
    )(value, order)


def chip_sums(keep, give, order):
    members = keep.shape[0]

    def kernel(keep_ref, give_ref, order_ref, *out_refs):
        for m in range(members):
            out_refs[m][...] = (keep_ref[m].astype(F32) + give_ref[m].astype(F32)).astype(BF)

    return pl.pallas_call(
        kernel,
        out_shape=[SHAPE(keep.shape[1:], BF)] * members,
        in_specs=[VM, VM, ANY],
        out_specs=[VM] * members,
        compiler_params=params(24),
        name="chip_sums",
    )(keep, give, order)


def tile_of(base_piece, t, member, share):
    per_piece = share // LANES
    piece = base_piece + t // per_piece
    return lane_block((member ^ piece) * per_piece + t % per_piece, LANES)


def cells_fit(images, height, width, share):
    return images == 2 and height == 8 and width == 8 and share % (GROUP * LANES) == 0


def conv_scratch():
    return [
        pltpu.VMEM((8, 64, LANES), F32),
        pltpu.VMEM((8, 8, 8, LANES), F32),
        pltpu.VMEM((8 * WEIGHT_ROWS, LANES), F32),
        pltpu.VMEM((TAPS, 8, LANES), F32),
    ]


def load_cells(turn_ref, cell_ref):
    for h in range(8):
        for w in range(8):
            cell_ref[h, w] = turn_ref[h, pl.ds(w, 8, stride=8), :]


def conv_cells(groups, base_piece, member, share, x_ref, weight_ref, mixed_ref, sum_ref, scratch):
    turn_ref, cell_ref, spread_ref, tap_ref = scratch
    per_piece = share // (GROUP * LANES)

    @pl.loop(0, groups)
    def _(g):
        piece = base_piece + g // per_piece
        start = ((member ^ piece) * per_piece + g % per_piece) * GROUP * LANES
        for c in range(GROUP):
            lanes = pl.ds(pl.multiple_of(g * GROUP * LANES + c * LANES, LANES), LANES)
            source = pl.ds(pl.multiple_of(start + c * LANES, LANES), LANES)
            column = weight_ref[:, lanes]
            for i in range(2):
                slot = i * GROUP + c
                spread_ref[slot * WEIGHT_ROWS : (slot + 1) * WEIGHT_ROWS, :] = column
                for h in range(8):
                    turn_ref[h, slot * 8 : slot * 8 + 8, :] = x_ref[i, h, :, source].astype(F32)
        for tap in range(TAPS):
            tap_ref[tap] = spread_ref[pl.ds(tap, 8, stride=WEIGHT_ROWS), :]
        bias = spread_ref[pl.ds(GAIN_ROW, 8, stride=WEIGHT_ROWS), :]
        load_cells(turn_ref, cell_ref)
        for h in range(8):
            sums = [bias] * 8
            for a in range(max(0, REACH - h), min(KER, 8 + REACH - h)):
                row = [cell_ref[h + a - REACH, w] for w in range(8)]
                for b in range(KER):
                    weight = tap_ref[a * KER + b]
                    for w in range(max(0, REACH - b), min(8, 8 + REACH - b)):
                        sums[w] = sums[w] + row[w + b - REACH] * weight
            for w in range(8):
                turn_ref[h, w * 8 : w * 8 + 8, :] = sums[w]
        for h in range(8):
            for i in range(2):
                for c in range(GROUP):
                    lanes = pl.ds(pl.multiple_of(g * GROUP * LANES + c * LANES, LANES), LANES)
                    value = turn_ref[h, pl.ds(i * GROUP + c, 8, stride=8), :]
                    mixed_ref[i, h, :, lanes] = value
                    sum_ref[i, h] += value


def conv_tiles(tiles, base_piece, member, share, x_ref, weight_ref, mixed_ref, sum_ref, scratch):
    images, height, width = x_ref.shape[:3]
    if cells_fit(images, height, width, share):
        conv_cells(
            tiles // GROUP, base_piece, member, share, x_ref, weight_ref, mixed_ref, sum_ref, scratch
        )
        return

    @pl.loop(0, tiles)
    def _(t):
        lanes = lane_block(t, LANES)
        source = tile_of(base_piece, t, member, share)
        bias = weight_ref[GAIN_ROW : GAIN_ROW + 1, lanes]
        for i in range(images):
            rows = [x_ref[i, h, :, source].astype(F32) for h in range(height)]
            sums = conv_rows(rows, lambda tap: weight_ref[tap : tap + 1, lanes], False)
            for h in range(height):
                value = sums[h] + bias
                mixed_ref[i, h, :, lanes] = value
                sum_ref[i, h] += value


def text_chunks(embed_width, share):
    return [
        (chunk, first, min(share, embed_width - first))
        for chunk, first in enumerate(range(0, embed_width, share))
    ]


def pack_rows(texts, embed_width, share):
    return (4 + texts * len(text_chunks(embed_width, share)) + 7) // 8 * 8


def load_kernel(x_hbm, kernel_hbm, term_hbm, text_hbm, x_ref, weight_ref, text_ref, kernel_ref, term_ref, sems):
    copies = [
        pltpu.make_async_copy(kernel_hbm, kernel_ref, sems.at[0]),
        pltpu.make_async_copy(term_hbm, term_ref, sems.at[1]),
        pltpu.make_async_copy(text_hbm, text_ref, sems.at[2]),
        pltpu.make_async_copy(x_hbm, x_ref, sems.at[3]),
    ]
    for copy in copies:
        copy.start()
    for copy in copies[:3]:
        copy.wait()
    weight_ref[0:TAPS, :] = kernel_ref[...].astype(F32)
    weight_ref[GAIN_ROW : GAIN_ROW + 4, :] = term_ref[...].astype(F32)
    copies[3].wait()


def load_block(image_maps, dw_kernel, channel_terms, text_feats):
    share = dw_kernel.shape[1]
    return pl.pallas_call(
        load_kernel,
        out_shape=[
            SHAPE(image_maps.shape, BF),
            SHAPE((WEIGHT_ROWS, share), F32),
            SHAPE(text_feats.shape, BF),
        ],
        in_specs=[HB, HB, HB, HB],
        out_specs=[VM] * 3,
        scratch_shapes=[
            pltpu.VMEM(dw_kernel.shape, BF),
            pltpu.VMEM(channel_terms.shape, BF),
            pltpu.SemaphoreType.DMA((4,)),
        ],
        compiler_params=params(24),
        name="load_block",
    )(*far([image_maps, dw_kernel, channel_terms, text_feats]))


def pack_block(weight_own, text_here, text_core):
    images, embed_width = text_here.shape
    share = weight_own.shape[1]
    texts = 2 * images
    rows = pack_rows(texts, embed_width, share)

    def kernel(weight_ref, here_ref, core_ref, packed_ref, rows_ref):
        rows_ref[...] = jnp.zeros_like(rows_ref)
        rows_ref[0:4, :] = weight_ref[GAIN_ROW : GAIN_ROW + 4, :]
        both = jnp.concatenate([here_ref[...].astype(F32), core_ref[...].astype(F32)], axis=0)
        for chunk, first, width in text_chunks(embed_width, share):
            row = 4 + chunk * texts
            rows_ref[row : row + texts, 0:width] = both[:, first : first + width]
        packed_ref[...] = rows_ref[...].astype(BF)

    return pl.pallas_call(
        kernel,
        out_shape=SHAPE((rows, share), BF),
        in_specs=[VM] * 3,
        out_specs=VM,
        scratch_shapes=[pltpu.VMEM((rows, share), F32)],
        compiler_params=params(24),
        name="pack_block",
    )(*near([weight_own, text_here, text_core]))


def text_stack(text_here, text_core, packs, order):
    images, embed_width = text_here.shape
    share = packs[0].shape[1]
    members = len(packs) + 1
    total = 2 * members * images

    def kernel(*refs):
        here_ref, core_ref, pack_refs, out_ref, rows_ref = refs[0], refs[1], refs[2 : members + 1], refs[-2], refs[-1]
        half = members * images
        rows_ref[0:images, :] = here_ref[...].astype(F32)
        rows_ref[half : half + images, :] = core_ref[...].astype(F32)
        for m in range(1, members):
            pack = pack_refs[m - 1][...].astype(F32)
            for chunk, first, width in text_chunks(embed_width, share):
                for core in range(2):
                    row = 4 + (chunk * 2 + core) * images
                    place = core * half + m * images
                    rows_ref[place : place + images, first : first + width] = pack[
                        row : row + images, 0:width
                    ]
        out_ref[...] = rows_ref[...].astype(BF)

    return pl.pallas_call(
        kernel,
        out_shape=SHAPE((total, embed_width), BF),
        in_specs=[VM] * (members + 1) + [ANY],
        out_specs=VM,
        scratch_shapes=[pltpu.VMEM((total, embed_width), F32)],
        compiler_params=params(24),
        name="text_stack",
    )(text_here, text_core, *packs, order)


def own_block(place, x_here, weight_own):
    images, height, width, channels = x_here.shape
    share = weight_own.shape[1]

    def kernel(place_ref, x_ref, weight_ref, mixed_ref, sum_ref, *scratch):
        sum_ref[...] = jnp.zeros_like(sum_ref)
        conv_tiles(
            share // LANES, 0, place_ref[0], share, x_ref, weight_ref, mixed_ref, sum_ref, scratch
        )

    return pl.pallas_call(
        kernel,
        out_shape=[
            SHAPE((images, height, width, share), F32),
            SHAPE((images, height, width, LANES), F32),
        ],
        in_specs=[SM, VM, VM],
        out_specs=[VM] * 2,
        scratch_shapes=conv_scratch(),
        compiler_params=params(24),
        name="own_block",
    )(place, *near([x_here, weight_own]))


def forward_kernel(members, place_ref, head_hbm, x_ref, mixed_own, sum_own, weight_own, order_ref, *refs):
    kernel_refs, refs = refs[: members - 1], refs[members - 1 :]
    pack_refs, refs = refs[: members - 1], refs[members - 1 :]
    piece_refs, refs = refs[:members], refs[members:]
    head_ref, weight_rest, mixed_rest, mean_ref, rstd_ref, hatsum_ref, hat_ref, hrstd_ref, sum_ref, pool_ref, sem = refs[:11]
    scratch = refs[11:]
    images, height, width, channels = x_ref.shape
    share = channels // members
    cells = height * width
    member = place_ref[0]
    head_copy = pltpu.make_async_copy(head_hbm, head_ref, sem)
    head_copy.start()
    for m in range(1, members):
        lanes = slice((m - 1) * share, m * share)
        weight_rest[0:TAPS, lanes] = kernel_refs[m - 1][...].astype(F32)
        weight_rest[GAIN_ROW : GAIN_ROW + 4, lanes] = pack_refs[m - 1][...].astype(F32)[0:4]
    sum_ref[...] = sum_own[...]
    own_tiles = share // LANES
    rest_tiles = (members - 1) * own_tiles
    conv_tiles(rest_tiles, 1, member, share, x_ref, weight_rest, mixed_rest, sum_ref, scratch)
    parts = [(0, own_tiles, mixed_own, weight_own), (1, rest_tiles, mixed_rest, weight_rest)]

    mean = jnp.sum(sum_ref[...], axis=-1, keepdims=True) * (1.0 / channels)
    mean_ref[...] = jnp.broadcast_to(mean, mean_ref.shape)
    sum_ref[...] = jnp.zeros_like(sum_ref)
    for base, tiles, mixed_ref, weight_ref in parts:

        @pl.loop(0, tiles)
        def _(t):
            lanes = lane_block(t, LANES)
            for i in range(images):
                for h in range(height):
                    value = mixed_ref[i, h, :, lanes] - mean_ref[i, h]
                    sum_ref[i, h] += value * value

    var = jnp.sum(sum_ref[...], axis=-1, keepdims=True) * (1.0 / channels)
    rstd_ref[...] = jnp.broadcast_to(lax.rsqrt(var + EPS), rstd_ref.shape)
    for base, tiles, mixed_ref, weight_ref in parts:

        @pl.loop(0, tiles)
        def _(t):
            lanes = lane_block(t, LANES)
            wide = lane_block(t + base * own_tiles, LANES)
            source = tile_of(base, t, member, share)
            scale = (
                weight_ref[GAIN_ROW + 1 : GAIN_ROW + 2, lanes]
                * weight_ref[GAIN_ROW + 2 : GAIN_ROW + 3, lanes]
            )
            for i in range(images):
                hats = jnp.zeros((width, LANES), F32)
                plain = jnp.zeros((width, LANES), F32)
                for h in range(height):
                    hats = hats + (mixed_ref[i, h, :, lanes] - mean_ref[i, h]) * rstd_ref[i, h]
                    plain = plain + x_ref[i, h, :, source].astype(F32)
                hat_row = jnp.sum(hats, axis=0, keepdims=True)
                hatsum_ref[i : i + 1, wide] = hat_row
                pool_ref[i : i + 1, wide] = (
                    jnp.sum(plain, axis=0, keepdims=True) + scale * hat_row
                ) * (1.0 / cells)

    pooled = pool_ref[...]
    centered = pooled - jnp.mean(pooled, axis=1, keepdims=True)
    head_rstd = lax.rsqrt(jnp.mean(centered * centered, axis=1, keepdims=True) + EPS)
    hat = centered * head_rstd
    hat_ref[...] = hat
    hrstd_ref[...] = jnp.broadcast_to(head_rstd, hrstd_ref.shape)
    for m in range(members):
        gain = (
            weight_own[GAIN_ROW + 3 : GAIN_ROW + 4, :]
            if m == 0
            else weight_rest[GAIN_ROW + 3 : GAIN_ROW + 4, (m - 1) * share : m * share]
        )
        piece_refs[m][...] = (hat[:, m * share : (m + 1) * share] * gain).astype(BF)
    head_copy.wait()


def forward_block(place, head_weight, x_here, own, order, kernels, packs):
    images, height, width, channels = x_here.shape
    members = len(packs) + 1
    share = channels // members
    cell = (images, height, width, LANES)
    outs = [SHAPE((images, share), BF)] * members + [
        SHAPE(head_weight.shape, BF),
        SHAPE((WEIGHT_ROWS, channels - share), F32),
        SHAPE((images, height, width, channels - share), F32),
        SHAPE(cell, F32),
        SHAPE(cell, F32),
        SHAPE((images, channels), F32),
        SHAPE((images, channels), F32),
        SHAPE((images, LANES), F32),
    ]
    result = pl.pallas_call(
        lambda *refs: forward_kernel(members, *refs),
        out_shape=outs,
        in_specs=[SM, HB, VM, VM, VM, VM, ANY] + [VM] * (2 * (members - 1)),
        out_specs=[VM] * len(outs),
        scratch_shapes=[
            pltpu.VMEM(cell, F32),
            pltpu.VMEM((images, channels), F32),
            pltpu.SemaphoreType.DMA,
        ]
        + conv_scratch(),
        compiler_params=params(24),
        name="forward_block",
    )(place, *far([head_weight]), *near([x_here, *own]), order, *near([*kernels, *packs]))
    return result[:members], result[members], result[members + 1], result[members + 2], result[members + 3 :]


def head_kernel(members, *refs):
    group = jnp.concatenate([ref[...].astype(F32) for ref in refs[:members]], axis=0).astype(BF)
    weight_ref, group_ref, out_ref = refs[members:]
    group_ref[...] = group
    out_ref[...] = jnp.dot(group, weight_ref[...], preferred_element_type=F32)


def head_project(pieces, head_weight):
    members = len(pieces)
    share, embed_width = head_weight.shape
    rows = members * pieces[0].shape[0]
    return pl.pallas_call(
        lambda *refs: head_kernel(members, *refs),
        out_shape=[SHAPE((rows, share), BF), SHAPE((rows, embed_width), F32)],
        in_specs=[VM] * (members + 1),
        out_specs=[VM, VM],
        compiler_params=params(24),
        cost_estimate=cost(0.5),
        name="head_project",
    )(*near([*pieces, head_weight]))


def inverse_norm(vectors):
    return lax.rsqrt(jnp.sum(vectors * vectors, axis=1, keepdims=True) + EPS)


def pair_weights(images, texts):
    logits = (
        LOGIT_SCALE
        * lax.dot_general(images, texts, (((1,), (1,)), ((), ())), preferred_element_type=F32)
        + LOGIT_BIAS
    )
    here = lax.broadcasted_iota(jnp.int32, logits.shape, 0)
    there = lax.broadcasted_iota(jnp.int32, logits.shape, 1)
    positive = jnp.where(here == there, 1.0, 0.0).astype(F32)
    return (jax.nn.sigmoid(logits) - positive).astype(BF)


def unit_back(unit, inverse, grad):
    return inverse * (grad - unit * jnp.sum(unit * grad, axis=1, keepdims=True))


def embed_sum_kernel(members, *refs):
    total_rows = refs[0].shape[0]
    rows = total_rows // members
    embed = refs[0][...]
    for m in range(1, members):
        embed = embed + jnp.concatenate(
            [refs[m][(k ^ m) * rows : (k ^ m) * rows + rows, :] for k in range(members)], axis=0
        )
    refs[members][...] = embed


def embed_sum(partials):
    members = len(partials)
    return pl.pallas_call(
        lambda *refs: embed_sum_kernel(members, *refs),
        out_shape=SHAPE(partials[0].shape, F32),
        in_specs=[VM] * members,
        out_specs=VM,
        compiler_params=params(24),
        cost_estimate=cost(SUM_COST),
        name="embed_sum",
    )(*near(partials))


def loss_kernel(members, embed_ref, text_low, text_high, group_ref, weight_ref, packed_ref, *piece_refs):
    total_rows, width = embed_ref.shape
    rows = total_rows // members
    share = group_ref.shape[1]
    embed = embed_ref[...]
    inverse = inverse_norm(embed)
    unit = embed * inverse
    unit_bf = unit.astype(BF)
    raw = jnp.concatenate([text_low[...], text_high[...]], axis=0).astype(F32)
    texts = (raw * inverse_norm(raw)).astype(BF)
    unit_grad = LOGIT_SCALE * jnp.dot(
        pair_weights(unit_bf, texts), texts, preferred_element_type=F32
    )
    embed_grad = unit_back(unit, inverse, unit_grad).astype(BF)
    packed_ref[:, 0:share] = group_ref[...]
    packed_ref[:, share : share + width] = embed_grad
    packed_ref[:, share + width : share + 2 * width] = unit_bf
    part = lax.dot_general(
        embed_grad, weight_ref[...], (((1,), (1,)), ((), ())), preferred_element_type=F32
    )
    for m in range(members):
        piece_refs[m][...] = part[m * rows : m * rows + rows]


def loss_block(members, embed, texts, group, head_weight):
    total_rows, embed_width = embed.shape
    share = head_weight.shape[0]
    result = pl.pallas_call(
        lambda *refs: loss_kernel(members, *refs),
        out_shape=[SHAPE((total_rows, share + 2 * embed_width), BF)]
        + [SHAPE((total_rows // members, share), F32)] * members,
        in_specs=[VM] * 5,
        out_specs=[VM] * (members + 1),
        compiler_params=params(24),
        name="loss_block",
    )(*near([embed, *texts, group, head_weight]))
    return result[0], result[1:]


def pool_grad_kernel(members, cells, *refs):
    grad_refs, refs = refs[:members], refs[members:]
    weight_own, weight_rest, hatsum_ref, hat_ref, hrstd_ref, shared_ref, scaled_ref, rows_ref = refs

    def term_row(row):
        return jnp.concatenate(
            [weight_own[GAIN_ROW + row : GAIN_ROW + row + 1, :], weight_rest[GAIN_ROW + row : GAIN_ROW + row + 1, :]],
            axis=1,
        )

    grad = jnp.concatenate([ref[...] for ref in grad_refs], axis=1)
    hat = hat_ref[...]
    inner = grad * term_row(3)
    shared = (
        hrstd_ref[:, 0:1]
        * (
            inner
            - jnp.mean(inner, axis=1, keepdims=True)
            - hat * jnp.mean(inner * hat, axis=1, keepdims=True)
        )
        * (1.0 / cells)
    )
    shared_ref[...] = shared
    gain = term_row(1)
    scale = term_row(2)
    hat_total = jnp.sum(shared * hatsum_ref[...], axis=0, keepdims=True)
    rows_ref[...] = jnp.zeros_like(rows_ref)
    rows_ref[1:2, :] = hat_total * scale
    rows_ref[2:3, :] = hat_total * gain
    rows_ref[3:4, :] = jnp.sum(grad * hat, axis=0, keepdims=True)
    scaled = shared * (gain * scale)
    scaled_ref[...] = scaled - jnp.mean(scaled, axis=1, keepdims=True)


def pool_grad_block(grads, cells, weights, hatsum, hat, hrstd):
    members = len(grads)
    images, channels = hat.shape
    return pl.pallas_call(
        lambda *refs: pool_grad_kernel(members, cells, *refs),
        out_shape=[
            SHAPE((images, channels), F32),
            SHAPE((images, channels), F32),
            SHAPE((8, channels), F32),
        ],
        in_specs=[VM] * (members + 5),
        out_specs=[VM] * 3,
        compiler_params=params(24),
        cost_estimate=cost(0.4),
        name="pool_grad_block",
    )(*near([*grads, *weights, hatsum, hat, hrstd]))


def dots_kernel(scaled_ref, mixed_own, mixed_rest, mean_ref, rstd_ref, dot_ref):
    images, height = dot_ref.shape[:2]
    channels = scaled_ref.shape[1]
    own_tiles = mixed_own.shape[3] // LANES
    rest_tiles = mixed_rest.shape[3] // LANES
    dot_ref[...] = jnp.zeros_like(dot_ref)
    for first, tiles, mixed_ref in [(0, own_tiles, mixed_own), (own_tiles, rest_tiles, mixed_rest)]:

        @pl.loop(0, tiles)
        def _(t):
            lanes = lane_block(t, LANES)
            wide = lane_block(t + first, LANES)
            for i in range(images):
                factor = scaled_ref[i : i + 1, wide]
                for h in range(height):
                    dot_ref[i, h] += factor * (mixed_ref[i, h, :, lanes] - mean_ref[i, h])

    dots = jnp.sum(dot_ref[...], axis=-1, keepdims=True) * (1.0 / channels)
    dot_ref[...] = jnp.broadcast_to(dots, dot_ref.shape) * rstd_ref[...] * rstd_ref[...]


def dots_block(scaled, mixed, mean, rstd):
    return pl.pallas_call(
        dots_kernel,
        out_shape=SHAPE(mean.shape, F32),
        in_specs=[VM] * 5,
        out_specs=VM,
        compiler_params=params(24),
        cost_estimate=cost(DOTS_COST),
        name="dots_block",
    )(*near([scaled, *mixed, mean, rstd]))


def terms_kernel(base, share, place_ref, x_ref, scaled_ref, rows_ref, mixed_ref, mean_ref, rstd_ref, dot_ref, *refs):
    keep_ref, give_ref, flow_ref, sums_ref, taps_ref, turn_x, turn_flow, cell_x, cell_flow = refs
    images, height, width = x_ref.shape[:3]
    channels = mixed_ref.shape[3]
    own_tiles = share // LANES
    member = place_ref[0]
    core = place_ref[1]
    first = base * share
    sums_ref[TAPS // 8 * 8 : TERM_ROW, :] = jnp.zeros((TERM_ROW - TAPS // 8 * 8, channels), F32)
    sums_ref[TERM_ROW:ROWS_PAD, :] = rows_ref[:, first : first + channels]

    if cells_fit(images, height, width, share):
        per_piece = share // (GROUP * LANES)

        @pl.loop(0, channels // (GROUP * LANES))
        def _(g):
            piece = base + g // per_piece
            start = ((member ^ piece) * per_piece + g % per_piece) * GROUP * LANES
            for c in range(GROUP):
                here = g * GROUP * LANES + c * LANES
                lanes = pl.ds(pl.multiple_of(here, LANES), LANES)
                wide = pl.ds(pl.multiple_of(first + here, LANES), LANES)
                source = pl.ds(pl.multiple_of(start + c * LANES, LANES), LANES)
                for i in range(images):
                    slot = (i * GROUP + c) * width
                    factor = scaled_ref[i : i + 1, wide]
                    for h in range(height):
                        centered = mixed_ref[i, h, :, lanes] - mean_ref[i, h]
                        flow = rstd_ref[i, h] * (factor - centered * dot_ref[i, h])
                        flow_ref[i, h, :, lanes] = flow
                        turn_flow[h, slot : slot + width, :] = flow
                        turn_x[h, slot : slot + width, :] = x_ref[i, h, :, source].astype(F32)
            load_cells(turn_flow, cell_flow)
            load_cells(turn_x, cell_x)
            bias = None
            for a in range(KER):
                totals = [None] * KER
                for h in range(max(0, REACH - a), min(height, height + REACH - a)):
                    flows = [cell_flow[h, w] for w in range(width)]
                    row = [cell_x[h + a - REACH, w] for w in range(width)]
                    for b in range(KER):
                        for w in range(max(0, REACH - b), min(width, width + REACH - b)):
                            term = flows[w] * row[w + b - REACH]
                            totals[b] = term if totals[b] is None else totals[b] + term
                    if a == REACH:
                        for w in range(width):
                            bias = flows[w] if bias is None else bias + flows[w]
                for b in range(KER):
                    tap = a * KER + b
                    taps_ref[tap * 8 : tap * 8 + 8, :] = totals[b]
            taps_ref[TAPS * 8 : TAPS * 8 + 8, :] = bias
            for c in range(GROUP):
                lanes = pl.ds(pl.multiple_of(g * GROUP * LANES + c * LANES, LANES), LANES)
                total = (
                    taps_ref[pl.ds(c, TAPS + 1, stride=8), :]
                    + taps_ref[pl.ds(GROUP + c, TAPS + 1, stride=8), :]
                )
                sums_ref[0:TAPS, lanes] = total[0:TAPS]
                sums_ref[TERM_ROW : TERM_ROW + 1, lanes] = total[TAPS : TAPS + 1]

    else:
        @pl.loop(0, channels // LANES)
        def _(t):
            lanes = lane_block(t, LANES)
            wide = lane_block(t + base * own_tiles, LANES)
            source = tile_of(base, t, member, share)
            flows = []
            for i in range(images):
                factor = scaled_ref[i : i + 1, wide]
                flow_rows = []
                for h in range(height):
                    centered = mixed_ref[i, h, :, lanes] - mean_ref[i, h]
                    flow = rstd_ref[i, h] * (factor - centered * dot_ref[i, h])
                    flow_ref[i, h, :, lanes] = flow
                    flow_rows.append(flow)
                flows.append(flow_rows)
            bias = flows[0][0]
            for i in range(images):
                for h in range(height):
                    if i or h:
                        bias = bias + flows[i][h]
            taps_ref[TAPS * width : TAPS * width + width, :] = bias
            for b in range(KER):
                totals = [None] * KER
                for i in range(images):
                    moved = [
                        shift_cols(x_ref[i, h, :, source].astype(F32), b - REACH)
                        for h in range(height)
                    ]
                    for a in range(KER):
                        for h in range(max(0, REACH - a), min(height, height + REACH - a)):
                            term = flows[i][h] * moved[h + a - REACH]
                            totals[a] = term if totals[a] is None else totals[a] + term
                for a in range(KER):
                    tap = a * KER + b
                    taps_ref[tap * width : tap * width + width, :] = totals[a]
            rows = TAPS + 1
            total = taps_ref[pl.ds(0, rows, stride=width), :]
            for s in range(1, width):
                total = total + taps_ref[pl.ds(s, rows, stride=width), :]
            sums_ref[0:TAPS, lanes] = total[0:TAPS]
            sums_ref[TERM_ROW : TERM_ROW + 1, lanes] = total[TAPS : TAPS + 1]

    for m in range(channels // share):
        lanes = slice(m * share, (m + 1) * share)
        keep_ref[m] = sums_ref[pl.ds(pl.multiple_of(core * HALF_PAD, HALF_PAD), HALF_PAD), lanes].astype(BF)
        give_ref[m] = sums_ref[pl.ds(pl.multiple_of((1 - core) * HALF_PAD, HALF_PAD), HALF_PAD), lanes].astype(BF)


def terms_block(base, share, place, order, x_here, scaled, rows, mixed, mean, rstd, dots):
    width = x_here.shape[2]
    channels = mixed.shape[3]
    half = SHAPE((channels // share, HALF_PAD, share), BF)
    return pl.pallas_call(
        lambda place_ref, order_ref, *refs: terms_kernel(base, share, place_ref, *refs),
        out_shape=[half, half, SHAPE(mixed.shape, F32)],
        in_specs=[SM, ANY] + [VM] * 7,
        out_specs=[VM] * 3,
        scratch_shapes=[
            pltpu.VMEM((ROWS_PAD, channels), F32),
            pltpu.VMEM(((TAPS + 1) * width, LANES), F32),
            pltpu.VMEM((8, 64, LANES), F32),
            pltpu.VMEM((8, 64, LANES), F32),
            pltpu.VMEM((8, 8, 8, LANES), F32),
            pltpu.VMEM((8, 8, 8, LANES), F32),
        ],
        compiler_params=params(24),
        name="terms_block",
    )(place, order, *near([x_here, scaled, rows, mixed, mean, rstd, dots]))


def images_kernel(image, base, place_ref, flow_own, flow_rest, weight_own, weight_rest, shared_ref, out_ref, token_ref):
    height = flow_own.shape[1]
    share = weight_own.shape[1]
    own_tiles = share // LANES
    step = pl.program_id(0) + base
    token_ref[...] = jnp.zeros_like(token_ref)

    def piece(flow_ref, weight_ref, first):
        @pl.loop(0, own_tiles)
        def _(t):
            lanes = lane_block(t, LANES)
            wide = lane_block(t + step * own_tiles, LANES)
            near_lanes = lane_block(t + (step - first) * own_tiles, LANES)
            rows = [flow_ref[image, h, :, near_lanes] for h in range(height)]
            sums = conv_rows(rows, lambda tap: weight_ref[tap : tap + 1, near_lanes], True)
            for h in range(height):
                out_ref[0, h, :, lanes] = (sums[h] + shared_ref[image : image + 1, wide]).astype(BF)

    if base == 0:

        @pl.when(step == 0)
        def _():
            piece(flow_own, weight_own, 0)

    @pl.when(step != 0)
    def _():
        piece(flow_rest, weight_rest, 1)


def image_block(image, base, count, place, flow, weights, shared, order, out):
    first = out is None
    share = weights[0].shape[1]
    operands = [place, *near([*flow, *weights, shared]), order] + ([] if first else [out])

    def kernel(*refs):
        images_kernel(image, base, *refs[:6], refs[-2], refs[-1])

    return pl.pallas_call(
        kernel,
        grid_spec=pltpu.PrefetchScalarGridSpec(
            num_scalar_prefetch=1,
            grid=(count,),
            in_specs=[VM] * 5 + [ANY] + ([] if first else [HB]),
            out_specs=[
                pl.BlockSpec(
                    (1,) + flow[0].shape[1:3] + (share,),
                    lambda step, place_ref: (image, 0, 0, place_ref[0] ^ (step + base)),
                ),
                pl.BlockSpec((8, LANES), lambda step, place_ref: (0, 0)),
            ],
        ),
        out_shape=[
            SHAPE(flow[0].shape[:3] + (shared.shape[1],), BF),
            SHAPE((8, LANES), F32),
        ],
        input_output_aliases={} if first else {7: 0},
        compiler_params=params(24),
        cost_estimate=cost(1.5),
        name="image_block",
    )(*operands)


def head_grads_kernel(block, packed_low, packed_high, text_ref, order_ref, head_ref, text_grad_ref, token_ref):
    share = packed_low.shape[1] - 2 * text_ref.shape[1]
    width = text_ref.shape[1]
    step = pl.program_id(0)
    lanes = lane_block(step, block)
    grads = slice(share, share + width)
    images = jnp.concatenate([packed_low[:, lanes], packed_high[:, lanes]], axis=0)
    grad = jnp.concatenate([packed_low[:, grads], packed_high[:, grads]], axis=0)
    head_ref[...] = lax.dot_general(
        images, grad, (((0,), (0,)), ((), ())), preferred_element_type=F32
    )

    @pl.when(step == 0)
    def _():
        token_ref[...] = jnp.zeros_like(token_ref)
        units = slice(share + width, share + 2 * width)
        unit_all = jnp.concatenate([packed_low[:, units], packed_high[:, units]], axis=0)
        raw = text_ref[...].astype(F32)
        inverse = inverse_norm(raw)
        unit = raw * inverse
        pairs = pair_weights(unit_all, unit.astype(BF))
        text_sum = LOGIT_SCALE * lax.dot_general(
            pairs, unit_all, (((0,), (0,)), ((), ())), preferred_element_type=F32
        )
        text_grad_ref[...] = unit_back(unit, inverse, text_sum)


def head_grads_block(packed, text_here, share, order):
    rows, width = text_here.shape
    block = 256 if share % 256 == 0 else LANES
    return pl.pallas_call(
        lambda *refs: head_grads_kernel(block, *refs),
        grid=(share // block,),
        out_shape=[
            SHAPE((share, width), F32),
            SHAPE((rows, width), F32),
            SHAPE((8, LANES), F32),
        ],
        in_specs=[VM, VM, VM, ANY],
        out_specs=[
            pl.BlockSpec((block, width), lambda step: (step, 0)),
            pl.BlockSpec((rows, width), lambda step: (0, 0)),
            pl.BlockSpec((8, LANES), lambda step: (0, 0)),
        ],
        compiler_params=params(24),
        name="head_grads_block",
    )(*near([*packed, text_here]), order)


def split_kernel(place_ref, own_ref, other_ref, kernel_ref, term_ref):
    core = place_ref[1]
    rest = TAPS - HALF_PAD
    terms = slice(TERM_ROW - HALF_PAD, TERM_ROW - HALF_PAD + 4)

    def write(low_ref, high_ref):
        kernel_ref[0:HALF_PAD, :] = low_ref[...].astype(F32)
        high = high_ref[...].astype(F32)
        kernel_ref[HALF_PAD:TAPS, :] = high[0:rest]
        term_ref[...] = high[terms]

    @pl.when(core == 0)
    def _():
        write(own_ref, other_ref)

    @pl.when(core != 0)
    def _():
        write(other_ref, own_ref)


def split_block(place, own, other):
    share = own.shape[1]
    return pl.pallas_call(
        split_kernel,
        out_shape=[SHAPE((TAPS, share), F32), SHAPE((4, share), F32)],
        in_specs=[SM, VM, VM],
        out_specs=[VM, VM],
        compiler_params=params(24),
        name="split_block",
    )(place, *near([own, other]))


def per_device(image_maps, dw_kernel, channel_terms, head_weight, text_feats):
    members = lax.axis_size("fsdp")
    member = lax.axis_index("fsdp")
    core = lax.axis_index("dp") % 2
    place = jnp.stack([member, core]).astype(jnp.int32)
    others = range(1, members)
    dp_masks = bits_up(lax.axis_size("dp"))
    down = dp_masks[::-1]
    share = head_weight.shape[0]

    kernels = [swap(dw_kernel, "fsdp", m) for m in others]
    text_core = swap(text_feats, "dp", 1)
    x_here, weight_own, text_here = load_block(image_maps, dw_kernel, channel_terms, text_feats)
    pack_own = pack_block(weight_own, text_here, text_core)
    packs = [swap(pack_own, "fsdp", m) for m in others]
    mixed_own, sum_own = own_block(place, x_here, weight_own)

    text_rows = text_stack(text_here, text_core, packs, sum_own)
    text_masks = down[:-1]
    pieces, head_here, weight_rest, mixed_rest, saved = forward_block(
        place, head_weight, x_here, (mixed_own, sum_own, weight_own), text_rows, kernels, packs
    )
    weights = (weight_own, weight_rest)
    far_rows = swap(text_rows, "dp", text_masks[0])
    pieces = [pieces[0]] + [swap(pieces[m], "fsdp", m) for m in others]
    group, partial = head_project(pieces, head_here)
    orders = [saved[4]] + [partial] * len(text_masks)
    for mask, order in zip(text_masks[1:], orders):
        text_rows = stack_rows(text_rows, far_rows, order)
        far_rows = swap(text_rows, "dp", mask)
    texts = (text_rows, far_rows)

    partials = [partial] + [swap(partial, "fsdp", m) for m in others]
    packed, grads = loss_block(members, embed_sum(partials), texts, group, head_here)
    grads = [grads[0]] + [swap(grads[m], "fsdp", m) for m in others]

    mean, rstd, hatsum, hat, hrstd = saved
    cells = image_maps.shape[1] * image_maps.shape[2]
    shared, scaled, term_rows = pool_grad_block(grads, cells, weights, hatsum, hat, hrstd)
    mixed = (mixed_own, mixed_rest)
    dots = dots_block(scaled, mixed, mean, rstd)
    moving = swap(packed, "dp", down[0])

    def terms_part(base, mixed_part, order):
        return terms_block(
            base, share, place, order, x_here, scaled, term_rows, mixed_part, mean, rstd, dots
        )

    packed = stack_rows(packed, moving, dots)
    keep_rest, give_rest, flow_rest = terms_part(1, mixed_rest, packed)
    keep_own, give_own, flow_own = terms_part(0, mixed_own, keep_rest)
    flow = (flow_own, flow_rest)

    parts = [(image, base) for image in range(image_maps.shape[0]) for base in (0, members // 2)]
    image_grads = None

    def image_parts(count, order, image_grads):
        token = order
        for _ in range(min(count, len(parts))):
            image, base = parts.pop(0)
            image_grads, token = image_block(
                image, base, members // 2, place, flow, weights, shared, order, image_grads
            )
        return image_grads, token

    chip = chip_sums(keep_rest, swap(give_rest, "dp", 1), keep_own)
    chip_own = chip_sums(keep_own, swap(give_own, "dp", 1), chip[0])[0]
    gather_masks = list(down[1:])
    image_grads, token = image_parts(1, chip[0], None)
    packed = hold(packed, token)
    moving = swap(packed, "dp", gather_masks.pop(0))
    sent = add_all([chip_own] + [swap(chip[m - 1], "fsdp", m) for m in others], token)
    ring_masks = dp_masks[1:]
    counts = [1] + [2] * len(ring_masks)
    for mask, count in zip(ring_masks[:-1], counts):
        image_grads, token = image_parts(count, sent, image_grads)
        if mask == ring_masks[0]:
            packed = stack_rows(packed, moving, token)
            moving = swap(packed, "dp", gather_masks.pop(0))
        sent = add_all([sent, swap(sent, "dp", mask)], token)
    image_grads, token = image_parts(len(parts), sent, image_grads)
    while gather_masks:
        packed = stack_rows(packed, moving, token)
        moving = swap(packed, "dp", gather_masks.pop(0))
    head_grads, text_grads, token = head_grads_block((packed, moving), text_here, share, sent)
    sent = add_all([sent, swap(sent, "dp", ring_masks[-1])], token)
    kernel_grads, term_grads = split_block(place, sent, swap(sent, "dp", 1))
    return (image_grads, kernel_grads, term_grads, head_grads, text_grads)


def solution(mesh):
    in_specs = (
        P(("dp", "fsdp"), None, None, None),
        P(None, "fsdp"),
        P(None, "fsdp"),
        P("fsdp", None),
        P(("dp", "fsdp"), None),
    )
    out_specs = (
        P(("dp", "fsdp"), None, None, None),
        P(None, "fsdp"),
        P(None, "fsdp"),
        P("fsdp", None),
        P(("dp", "fsdp"), None),
    )
    return jax.shard_map(
        per_device, mesh=mesh, in_specs=in_specs, out_specs=out_specs, check_vma=False
    )
```

```python
import jax
import jax.numpy as jnp
from jax import lax
from jax.experimental import pallas as pl
from jax.experimental.pallas import tpu as pltpu
from jax.sharding import PartitionSpec as P

EPS = 1e-06
LOGIT_SCALE = 10.0
LOGIT_BIAS = -2.0
KER = 7
REACH = KER // 2
TAPS = KER * KER
LANES = 128
ROWS_PAD = 64
HALF_PAD = ROWS_PAD // 2
TERM_ROW = 56
GAIN_ROW = TAPS
WEIGHT_ROWS = 56
GROUP = 4
DOTS_COST = 3.0
SUM_COST = 1.0
BF = jnp.bfloat16
F32 = jnp.float32


def swap(value, axis, mask):
    count = lax.axis_size(axis)
    return lax.ppermute(value, axis, [(source, source ^ mask) for source in range(count)])


def bits_up(count):
    masks = []
    mask = 1
    while mask < count:
        masks.append(mask)
        mask *= 2
    return masks


def params(mebibytes):
    return pltpu.CompilerParams(vmem_limit_bytes=mebibytes * 1024 * 1024)


def cost(micros):
    return pl.CostEstimate(flops=int(micros * 1.1e9), bytes_accessed=0, transcendentals=0)


def far(arrays):
    return [pltpu.with_memory_space_constraint(value, pltpu.HBM) for value in arrays]


def near(arrays):
    return [pltpu.with_memory_space_constraint(value, pltpu.VMEM) for value in arrays]


VM = pl.BlockSpec(memory_space=pltpu.VMEM)
SM = pl.BlockSpec(memory_space=pltpu.SMEM)
HB = pl.BlockSpec(memory_space=pltpu.HBM)
ANY = pl.BlockSpec(memory_space=pl.ANY)
SHAPE = jax.ShapeDtypeStruct


def lane_block(index, width):
    return pl.ds(pl.multiple_of(index * width, LANES), width)


def shift_cols(value, step):
    if step == 0:
        return value
    width = value.shape[0]
    rolled = pltpu.roll(value, (-step) % width, 0)
    col = lax.broadcasted_iota(jnp.int32, value.shape, 0)
    inside = (col < width - step) if step > 0 else (col >= -step)
    return jnp.where(inside, rolled, 0.0)


def conv_rows(rows, tap_row, flip):
    height = len(rows)
    sums = [None] * height
    for b in range(KER):
        moved = [shift_cols(row, b - REACH) for row in rows]
        for a in range(KER):
            tap = (KER - 1 - a) * KER + (KER - 1 - b) if flip else a * KER + b
            weight = tap_row(tap)
            for h in range(max(0, REACH - a), min(height, height + REACH - a)):
                term = moved[h + a - REACH] * weight
                sums[h] = term if sums[h] is None else sums[h] + term
    return sums


def stack_rows(low, high, order):
    def kernel(low_ref, high_ref, order_ref, out_ref):
        both = jnp.concatenate([low_ref[...].astype(F32), high_ref[...].astype(F32)], axis=0)
        out_ref[...] = both.astype(out_ref.dtype)

    rows, width = low.shape
    return pl.pallas_call(
        kernel,
        out_shape=SHAPE((2 * rows, width), low.dtype),
        in_specs=[VM, VM, ANY],
        out_specs=VM,
        compiler_params=params(24),
        name="stack_rows",
    )(low, high, order)


def add_all(values, order):
    def kernel(*refs):
        total = refs[0][...].astype(F32)
        for ref in refs[1:-2]:
            total = total + ref[...].astype(F32)
        refs[-1][...] = total.astype(BF)

    return pl.pallas_call(
        kernel,
        out_shape=SHAPE(values[0].shape, BF),
        in_specs=[VM] * len(values) + [ANY],
        out_specs=VM,
        compiler_params=params(24),
        name="add_all",
    )(*values, order)


def hold(value, order):
    def kernel(value_ref, order_ref, out_ref):
        out_ref[...] = value_ref[...]

    return pl.pallas_call(
        kernel,
        out_shape=SHAPE(value.shape, value.dtype),
        in_specs=[VM, ANY],
        out_specs=VM,
        compiler_params=params(24),
        name="hold",
    )(value, order)


def chip_sums(keep, give, order):
    members = keep.shape[0]

    def kernel(keep_ref, give_ref, order_ref, *out_refs):
        for m in range(members):
            out_refs[m][...] = (keep_ref[m].astype(F32) + give_ref[m].astype(F32)).astype(BF)

    return pl.pallas_call(
        kernel,
        out_shape=[SHAPE(keep.shape[1:], BF)] * members,
        in_specs=[VM, VM, ANY],
        out_specs=[VM] * members,
        compiler_params=params(24),
        name="chip_sums",
    )(keep, give, order)


def tile_of(base_piece, t, member, share):
    per_piece = share // LANES
    piece = base_piece + t // per_piece
    return lane_block((member ^ piece) * per_piece + t % per_piece, LANES)


def cells_fit(images, height, width, share):
    return images == 2 and height == 8 and width == 8 and share % (GROUP * LANES) == 0


def conv_scratch():
    return [
        pltpu.VMEM((8, 64, LANES), F32),
        pltpu.VMEM((8, 8, 8, LANES), F32),
        pltpu.VMEM((8 * WEIGHT_ROWS, LANES), F32),
        pltpu.VMEM((TAPS, 8, LANES), F32),
    ]


def load_cells(turn_ref, cell_ref):
    for h in range(8):
        for w in range(8):
            cell_ref[h, w] = turn_ref[h, pl.ds(w, 8, stride=8), :]


def conv_group(scratch, start, flip):
    turn_ref, cell_ref, spread_ref, tap_ref = scratch
    for tap in range(TAPS):
        source = TAPS - 1 - tap if flip else tap
        tap_ref[tap] = spread_ref[pl.ds(source, 8, stride=WEIGHT_ROWS), :]
    load_cells(turn_ref, cell_ref)
    for h in range(8):
        sums = [start] * 8
        for a in range(max(0, REACH - h), min(KER, 8 + REACH - h)):
            row = [cell_ref[h + a - REACH, w] for w in range(8)]
            for b in range(KER):
                weight = tap_ref[a * KER + b]
                for w in range(max(0, REACH - b), min(8, 8 + REACH - b)):
                    term = row[w + b - REACH] * weight
                    sums[w] = term if sums[w] is None else sums[w] + term
        for w in range(8):
            turn_ref[h, w * 8 : w * 8 + 8, :] = sums[w]


def conv_cells(groups, base_piece, member, share, x_ref, weight_ref, mixed_ref, sum_ref, scratch):
    turn_ref, cell_ref, spread_ref, tap_ref = scratch
    per_piece = share // (GROUP * LANES)

    @pl.loop(0, groups)
    def _(g):
        piece = base_piece + g // per_piece
        start = ((member ^ piece) * per_piece + g % per_piece) * GROUP * LANES
        for c in range(GROUP):
            lanes = pl.ds(pl.multiple_of(g * GROUP * LANES + c * LANES, LANES), LANES)
            source = pl.ds(pl.multiple_of(start + c * LANES, LANES), LANES)
            column = weight_ref[:, lanes]
            for i in range(2):
                slot = i * GROUP + c
                spread_ref[slot * WEIGHT_ROWS : (slot + 1) * WEIGHT_ROWS, :] = column
                for h in range(8):
                    turn_ref[h, slot * 8 : slot * 8 + 8, :] = x_ref[i, h, :, source].astype(F32)
        bias = spread_ref[pl.ds(GAIN_ROW, 8, stride=WEIGHT_ROWS), :]
        conv_group(scratch, bias, False)
        for h in range(8):
            for i in range(2):
                for c in range(GROUP):
                    lanes = pl.ds(pl.multiple_of(g * GROUP * LANES + c * LANES, LANES), LANES)
                    value = turn_ref[h, pl.ds(i * GROUP + c, 8, stride=8), :]
                    mixed_ref[i, h, :, lanes] = value
                    sum_ref[i, h] += value


def conv_tiles(tiles, base_piece, member, share, x_ref, weight_ref, mixed_ref, sum_ref, scratch):
    images, height, width = x_ref.shape[:3]
    if cells_fit(images, height, width, share):
        conv_cells(
            tiles // GROUP, base_piece, member, share, x_ref, weight_ref, mixed_ref, sum_ref, scratch
        )
        return

    @pl.loop(0, tiles)
    def _(t):
        lanes = lane_block(t, LANES)
        source = tile_of(base_piece, t, member, share)
        bias = weight_ref[GAIN_ROW : GAIN_ROW + 1, lanes]
        for i in range(images):
            rows = [x_ref[i, h, :, source].astype(F32) for h in range(height)]
            sums = conv_rows(rows, lambda tap: weight_ref[tap : tap + 1, lanes], False)
            for h in range(height):
                value = sums[h] + bias
                mixed_ref[i, h, :, lanes] = value
                sum_ref[i, h] += value


def text_chunks(embed_width, share):
    return [
        (chunk, first, min(share, embed_width - first))
        for chunk, first in enumerate(range(0, embed_width, share))
    ]


def pack_rows(texts, embed_width, share):
    return (4 + texts * len(text_chunks(embed_width, share)) + 7) // 8 * 8


def load_kernel(x_hbm, kernel_hbm, term_hbm, text_hbm, x_ref, weight_ref, text_ref, kernel_ref, term_ref, sems):
    copies = [
        pltpu.make_async_copy(kernel_hbm, kernel_ref, sems.at[0]),
        pltpu.make_async_copy(term_hbm, term_ref, sems.at[1]),
        pltpu.make_async_copy(text_hbm, text_ref, sems.at[2]),
        pltpu.make_async_copy(x_hbm, x_ref, sems.at[3]),
    ]
    for copy in copies:
        copy.start()
    for copy in copies[:3]:
        copy.wait()
    weight_ref[0:TAPS, :] = kernel_ref[...].astype(F32)
    weight_ref[GAIN_ROW : GAIN_ROW + 4, :] = term_ref[...].astype(F32)
    copies[3].wait()


def load_block(image_maps, dw_kernel, channel_terms, text_feats):
    share = dw_kernel.shape[1]
    return pl.pallas_call(
        load_kernel,
        out_shape=[
            SHAPE(image_maps.shape, BF),
            SHAPE((WEIGHT_ROWS, share), F32),
            SHAPE(text_feats.shape, BF),
        ],
        in_specs=[HB, HB, HB, HB],
        out_specs=[VM] * 3,
        scratch_shapes=[
            pltpu.VMEM(dw_kernel.shape, BF),
            pltpu.VMEM(channel_terms.shape, BF),
            pltpu.SemaphoreType.DMA((4,)),
        ],
        compiler_params=params(24),
        name="load_block",
    )(*far([image_maps, dw_kernel, channel_terms, text_feats]))


def pack_block(weight_own, text_here, text_core):
    images, embed_width = text_here.shape
    share = weight_own.shape[1]
    texts = 2 * images
    rows = pack_rows(texts, embed_width, share)

    def kernel(weight_ref, here_ref, core_ref, packed_ref, rows_ref):
        rows_ref[...] = jnp.zeros_like(rows_ref)
        rows_ref[0:4, :] = weight_ref[GAIN_ROW : GAIN_ROW + 4, :]
        both = jnp.concatenate([here_ref[...].astype(F32), core_ref[...].astype(F32)], axis=0)
        for chunk, first, width in text_chunks(embed_width, share):
            row = 4 + chunk * texts
            rows_ref[row : row + texts, 0:width] = both[:, first : first + width]
        packed_ref[...] = rows_ref[...].astype(BF)

    return pl.pallas_call(
        kernel,
        out_shape=SHAPE((rows, share), BF),
        in_specs=[VM] * 3,
        out_specs=VM,
        scratch_shapes=[pltpu.VMEM((rows, share), F32)],
        compiler_params=params(24),
        name="pack_block",
    )(*near([weight_own, text_here, text_core]))


def text_stack(text_here, text_core, packs, order):
    images, embed_width = text_here.shape
    share = packs[0].shape[1]
    members = len(packs) + 1
    total = 2 * members * images

    def kernel(*refs):
        here_ref, core_ref, pack_refs, out_ref, rows_ref = refs[0], refs[1], refs[2 : members + 1], refs[-2], refs[-1]
        half = members * images
        rows_ref[0:images, :] = here_ref[...].astype(F32)
        rows_ref[half : half + images, :] = core_ref[...].astype(F32)
        for m in range(1, members):
            pack = pack_refs[m - 1][...].astype(F32)
            for chunk, first, width in text_chunks(embed_width, share):
                for core in range(2):
                    row = 4 + (chunk * 2 + core) * images
                    place = core * half + m * images
                    rows_ref[place : place + images, first : first + width] = pack[
                        row : row + images, 0:width
                    ]
        raw = rows_ref[...]
        out_ref[...] = (raw * inverse_norm(raw)).astype(BF)

    return pl.pallas_call(
        kernel,
        out_shape=SHAPE((total, embed_width), BF),
        in_specs=[VM] * (members + 1) + [ANY],
        out_specs=VM,
        scratch_shapes=[pltpu.VMEM((total, embed_width), F32)],
        compiler_params=params(24),
        name="text_stack",
    )(text_here, text_core, *packs, order)


def own_block(place, x_here, weight_own):
    images, height, width, channels = x_here.shape
    share = weight_own.shape[1]

    def kernel(place_ref, x_ref, weight_ref, mixed_ref, sum_ref, *scratch):
        sum_ref[...] = jnp.zeros_like(sum_ref)
        conv_tiles(
            share // LANES, 0, place_ref[0], share, x_ref, weight_ref, mixed_ref, sum_ref, scratch
        )

    return pl.pallas_call(
        kernel,
        out_shape=[
            SHAPE((images, height, width, share), F32),
            SHAPE((images, height, width, LANES), F32),
        ],
        in_specs=[SM, VM, VM],
        out_specs=[VM] * 2,
        scratch_shapes=conv_scratch(),
        compiler_params=params(24),
        name="own_block",
    )(place, *near([x_here, weight_own]))


def forward_kernel(members, place_ref, head_hbm, x_ref, mixed_own, sum_own, weight_own, order_ref, *refs):
    kernel_refs, refs = refs[: members - 1], refs[members - 1 :]
    pack_refs, refs = refs[: members - 1], refs[members - 1 :]
    piece_refs, refs = refs[:members], refs[members:]
    head_ref, weight_rest, mixed_rest, mean_ref, rstd_ref, hatsum_ref, hat_ref, hrstd_ref, sum_ref, pool_ref, sem = refs[:11]
    scratch = refs[11:]
    images, height, width, channels = x_ref.shape
    share = channels // members
    cells = height * width
    member = place_ref[0]
    head_copy = pltpu.make_async_copy(head_hbm, head_ref, sem)
    head_copy.start()
    for m in range(1, members):
        lanes = slice((m - 1) * share, m * share)
        weight_rest[0:TAPS, lanes] = kernel_refs[m - 1][...].astype(F32)
        weight_rest[GAIN_ROW : GAIN_ROW + 4, lanes] = pack_refs[m - 1][...].astype(F32)[0:4]
    sum_ref[...] = sum_own[...]
    own_tiles = share // LANES
    rest_tiles = (members - 1) * own_tiles
    conv_tiles(rest_tiles, 1, member, share, x_ref, weight_rest, mixed_rest, sum_ref, scratch)
    parts = [(0, own_tiles, mixed_own, weight_own), (1, rest_tiles, mixed_rest, weight_rest)]

    mean = jnp.sum(sum_ref[...], axis=-1, keepdims=True) * (1.0 / channels)
    mean_ref[...] = jnp.broadcast_to(mean, mean_ref.shape)
    sum_ref[...] = jnp.zeros_like(sum_ref)
    for base, tiles, mixed_ref, weight_ref in parts:

        @pl.loop(0, tiles)
        def _(t):
            lanes = lane_block(t, LANES)
            for i in range(images):
                for h in range(height):
                    value = mixed_ref[i, h, :, lanes] - mean_ref[i, h]
                    sum_ref[i, h] += value * value

    var = jnp.sum(sum_ref[...], axis=-1, keepdims=True) * (1.0 / channels)
    rstd_ref[...] = jnp.broadcast_to(lax.rsqrt(var + EPS), rstd_ref.shape)
    for base, tiles, mixed_ref, weight_ref in parts:

        @pl.loop(0, tiles)
        def _(t):
            lanes = lane_block(t, LANES)
            wide = lane_block(t + base * own_tiles, LANES)
            source = tile_of(base, t, member, share)
            scale = (
                weight_ref[GAIN_ROW + 1 : GAIN_ROW + 2, lanes]
                * weight_ref[GAIN_ROW + 2 : GAIN_ROW + 3, lanes]
            )
            for i in range(images):
                hats = jnp.zeros((width, LANES), F32)
                plain = jnp.zeros((width, LANES), F32)
                for h in range(height):
                    hats = hats + (mixed_ref[i, h, :, lanes] - mean_ref[i, h]) * rstd_ref[i, h]
                    plain = plain + x_ref[i, h, :, source].astype(F32)
                hat_row = jnp.sum(hats, axis=0, keepdims=True)
                hatsum_ref[i : i + 1, wide] = hat_row
                pool_ref[i : i + 1, wide] = (
                    jnp.sum(plain, axis=0, keepdims=True) + scale * hat_row
                ) * (1.0 / cells)

    pooled = pool_ref[...]
    centered = pooled - jnp.mean(pooled, axis=1, keepdims=True)
    head_rstd = lax.rsqrt(jnp.mean(centered * centered, axis=1, keepdims=True) + EPS)
    hat = centered * head_rstd
    hat_ref[...] = hat
    hrstd_ref[...] = jnp.broadcast_to(head_rstd, hrstd_ref.shape)
    for m in range(members):
        gain = (
            weight_own[GAIN_ROW + 3 : GAIN_ROW + 4, :]
            if m == 0
            else weight_rest[GAIN_ROW + 3 : GAIN_ROW + 4, (m - 1) * share : m * share]
        )
        piece_refs[m][...] = (hat[:, m * share : (m + 1) * share] * gain).astype(BF)
    head_copy.wait()


def forward_block(place, head_weight, x_here, own, order, kernels, packs):
    images, height, width, channels = x_here.shape
    members = len(packs) + 1
    share = channels // members
    cell = (images, height, width, LANES)
    outs = [SHAPE((images, share), BF)] * members + [
        SHAPE(head_weight.shape, BF),
        SHAPE((WEIGHT_ROWS, channels - share), F32),
        SHAPE((images, height, width, channels - share), F32),
        SHAPE(cell, F32),
        SHAPE(cell, F32),
        SHAPE((images, channels), F32),
        SHAPE((images, channels), F32),
        SHAPE((images, LANES), F32),
    ]
    result = pl.pallas_call(
        lambda *refs: forward_kernel(members, *refs),
        out_shape=outs,
        in_specs=[SM, HB, VM, VM, VM, VM, ANY] + [VM] * (2 * (members - 1)),
        out_specs=[VM] * len(outs),
        scratch_shapes=[
            pltpu.VMEM(cell, F32),
            pltpu.VMEM((images, channels), F32),
            pltpu.SemaphoreType.DMA,
        ]
        + conv_scratch(),
        compiler_params=params(24),
        name="forward_block",
    )(place, *far([head_weight]), *near([x_here, *own]), order, *near([*kernels, *packs]))
    return result[:members], result[members], result[members + 1], result[members + 2], result[members + 3 :]


def head_kernel(members, *refs):
    group = jnp.concatenate([ref[...].astype(F32) for ref in refs[:members]], axis=0).astype(BF)
    weight_ref, group_ref, out_ref = refs[members:]
    group_ref[...] = group
    out_ref[...] = jnp.dot(group, weight_ref[...], preferred_element_type=F32)


def head_project(pieces, head_weight):
    members = len(pieces)
    share, embed_width = head_weight.shape
    rows = members * pieces[0].shape[0]
    return pl.pallas_call(
        lambda *refs: head_kernel(members, *refs),
        out_shape=[SHAPE((rows, share), BF), SHAPE((rows, embed_width), F32)],
        in_specs=[VM] * (members + 1),
        out_specs=[VM, VM],
        compiler_params=params(24),
        cost_estimate=cost(0.5),
        name="head_project",
    )(*near([*pieces, head_weight]))


def inverse_norm(vectors):
    return lax.rsqrt(jnp.sum(vectors * vectors, axis=1, keepdims=True) + EPS)


def pair_weights(images, texts):
    logits = (
        LOGIT_SCALE
        * lax.dot_general(images, texts, (((1,), (1,)), ((), ())), preferred_element_type=F32)
        + LOGIT_BIAS
    )
    here = lax.broadcasted_iota(jnp.int32, logits.shape, 0)
    there = lax.broadcasted_iota(jnp.int32, logits.shape, 1)
    positive = jnp.where(here == there, 1.0, 0.0).astype(F32)
    return (jax.nn.sigmoid(logits) - positive).astype(BF)


def unit_back(unit, inverse, grad):
    return inverse * (grad - unit * jnp.sum(unit * grad, axis=1, keepdims=True))


def embed_sum_kernel(members, *refs):
    total_rows = refs[0].shape[0]
    rows = total_rows // members
    embed = refs[0][...]
    for m in range(1, members):
        embed = embed + jnp.concatenate(
            [refs[m][(k ^ m) * rows : (k ^ m) * rows + rows, :] for k in range(members)], axis=0
        )
    refs[members][...] = embed


def embed_sum(partials):
    members = len(partials)
    return pl.pallas_call(
        lambda *refs: embed_sum_kernel(members, *refs),
        out_shape=SHAPE(partials[0].shape, F32),
        in_specs=[VM] * members,
        out_specs=VM,
        compiler_params=params(24),
        cost_estimate=cost(SUM_COST),
        name="embed_sum",
    )(*near(partials))


def loss_kernel(members, embed_ref, text_low, text_high, group_ref, weight_ref, packed_ref, *piece_refs):
    total_rows, width = embed_ref.shape
    rows = total_rows // members
    share = group_ref.shape[1]
    embed = embed_ref[...]
    inverse = inverse_norm(embed)
    unit = embed * inverse
    unit_bf = unit.astype(BF)
    texts = jnp.concatenate([text_low[...], text_high[...]], axis=0)
    unit_grad = LOGIT_SCALE * jnp.dot(
        pair_weights(unit_bf, texts), texts, preferred_element_type=F32
    )
    embed_grad = unit_back(unit, inverse, unit_grad).astype(BF)
    packed_ref[:, 0:share] = group_ref[...]
    packed_ref[:, share : share + width] = embed_grad
    packed_ref[:, share + width : share + 2 * width] = unit_bf
    part = lax.dot_general(
        embed_grad, weight_ref[...], (((1,), (1,)), ((), ())), preferred_element_type=F32
    )
    for m in range(members):
        piece_refs[m][...] = part[m * rows : m * rows + rows]


def loss_block(members, embed, texts, group, head_weight):
    total_rows, embed_width = embed.shape
    share = head_weight.shape[0]
    result = pl.pallas_call(
        lambda *refs: loss_kernel(members, *refs),
        out_shape=[SHAPE((total_rows, share + 2 * embed_width), BF)]
        + [SHAPE((total_rows // members, share), F32)] * members,
        in_specs=[VM] * 5,
        out_specs=[VM] * (members + 1),
        compiler_params=params(24),
        name="loss_block",
    )(*near([embed, *texts, group, head_weight]))
    return result[0], result[1:]


def pool_grad_kernel(members, cells, *refs):
    grad_refs, refs = refs[:members], refs[members:]
    weight_own, weight_rest, hatsum_ref, hat_ref, hrstd_ref, shared_ref, scaled_ref, rows_ref = refs

    def term_row(row):
        return jnp.concatenate(
            [weight_own[GAIN_ROW + row : GAIN_ROW + row + 1, :], weight_rest[GAIN_ROW + row : GAIN_ROW + row + 1, :]],
            axis=1,
        )

    grad = jnp.concatenate([ref[...] for ref in grad_refs], axis=1)
    hat = hat_ref[...]
    inner = grad * term_row(3)
    shared = (
        hrstd_ref[:, 0:1]
        * (
            inner
            - jnp.mean(inner, axis=1, keepdims=True)
            - hat * jnp.mean(inner * hat, axis=1, keepdims=True)
        )
        * (1.0 / cells)
    )
    shared_ref[...] = shared
    gain = term_row(1)
    scale = term_row(2)
    hat_total = jnp.sum(shared * hatsum_ref[...], axis=0, keepdims=True)
    rows_ref[...] = jnp.zeros_like(rows_ref)
    rows_ref[1:2, :] = hat_total * scale
    rows_ref[2:3, :] = hat_total * gain
    rows_ref[3:4, :] = jnp.sum(grad * hat, axis=0, keepdims=True)
    scaled = shared * (gain * scale)
    scaled_ref[...] = scaled - jnp.mean(scaled, axis=1, keepdims=True)


def pool_grad_block(grads, cells, weights, hatsum, hat, hrstd):
    members = len(grads)
    images, channels = hat.shape
    return pl.pallas_call(
        lambda *refs: pool_grad_kernel(members, cells, *refs),
        out_shape=[
            SHAPE((images, channels), F32),
            SHAPE((images, channels), F32),
            SHAPE((8, channels), F32),
        ],
        in_specs=[VM] * (members + 5),
        out_specs=[VM] * 3,
        compiler_params=params(24),
        cost_estimate=cost(0.4),
        name="pool_grad_block",
    )(*near([*grads, *weights, hatsum, hat, hrstd]))


def dots_kernel(scaled_ref, mixed_own, mixed_rest, mean_ref, rstd_ref, dot_ref):
    images, height = dot_ref.shape[:2]
    channels = scaled_ref.shape[1]
    own_tiles = mixed_own.shape[3] // LANES
    rest_tiles = mixed_rest.shape[3] // LANES
    dot_ref[...] = jnp.zeros_like(dot_ref)
    for first, tiles, mixed_ref in [(0, own_tiles, mixed_own), (own_tiles, rest_tiles, mixed_rest)]:

        @pl.loop(0, tiles)
        def _(t):
            lanes = lane_block(t, LANES)
            wide = lane_block(t + first, LANES)
            for i in range(images):
                factor = scaled_ref[i : i + 1, wide]
                for h in range(height):
                    dot_ref[i, h] += factor * (mixed_ref[i, h, :, lanes] - mean_ref[i, h])

    dots = jnp.sum(dot_ref[...], axis=-1, keepdims=True) * (1.0 / channels)
    dot_ref[...] = jnp.broadcast_to(dots, dot_ref.shape) * rstd_ref[...] * rstd_ref[...]


def dots_block(scaled, mixed, mean, rstd):
    return pl.pallas_call(
        dots_kernel,
        out_shape=SHAPE(mean.shape, F32),
        in_specs=[VM] * 5,
        out_specs=VM,
        compiler_params=params(24),
        cost_estimate=cost(DOTS_COST),
        name="dots_block",
    )(*near([scaled, *mixed, mean, rstd]))


def terms_kernel(base, share, place_ref, x_ref, scaled_ref, rows_ref, mixed_ref, mean_ref, rstd_ref, dot_ref, *refs):
    keep_ref, give_ref, flow_ref, sums_ref, taps_ref, turn_x, turn_flow, cell_x, cell_flow = refs
    images, height, width = x_ref.shape[:3]
    channels = mixed_ref.shape[3]
    own_tiles = share // LANES
    member = place_ref[0]
    core = place_ref[1]
    first = base * share
    sums_ref[TAPS // 8 * 8 : TERM_ROW, :] = jnp.zeros((TERM_ROW - TAPS // 8 * 8, channels), F32)
    sums_ref[TERM_ROW:ROWS_PAD, :] = rows_ref[:, first : first + channels]

    if cells_fit(images, height, width, share):
        per_piece = share // (GROUP * LANES)

        @pl.loop(0, channels // (GROUP * LANES))
        def _(g):
            piece = base + g // per_piece
            start = ((member ^ piece) * per_piece + g % per_piece) * GROUP * LANES
            for c in range(GROUP):
                here = g * GROUP * LANES + c * LANES
                lanes = pl.ds(pl.multiple_of(here, LANES), LANES)
                wide = pl.ds(pl.multiple_of(first + here, LANES), LANES)
                source = pl.ds(pl.multiple_of(start + c * LANES, LANES), LANES)
                for i in range(images):
                    slot = (i * GROUP + c) * width
                    factor = scaled_ref[i : i + 1, wide]
                    for h in range(height):
                        centered = mixed_ref[i, h, :, lanes] - mean_ref[i, h]
                        flow = rstd_ref[i, h] * (factor - centered * dot_ref[i, h])
                        flow_ref[i, h, :, lanes] = flow
                        turn_flow[h, slot : slot + width, :] = flow
                        turn_x[h, slot : slot + width, :] = x_ref[i, h, :, source].astype(F32)
            load_cells(turn_flow, cell_flow)
            load_cells(turn_x, cell_x)
            bias = None
            for a in range(KER):
                totals = [None] * KER
                for h in range(max(0, REACH - a), min(height, height + REACH - a)):
                    flows = [cell_flow[h, w] for w in range(width)]
                    row = [cell_x[h + a - REACH, w] for w in range(width)]
                    for b in range(KER):
                        for w in range(max(0, REACH - b), min(width, width + REACH - b)):
                            term = flows[w] * row[w + b - REACH]
                            totals[b] = term if totals[b] is None else totals[b] + term
                    if a == REACH:
                        for w in range(width):
                            bias = flows[w] if bias is None else bias + flows[w]
                for b in range(KER):
                    tap = a * KER + b
                    taps_ref[tap * 8 : tap * 8 + 8, :] = totals[b]
            taps_ref[TAPS * 8 : TAPS * 8 + 8, :] = bias
            for c in range(GROUP):
                lanes = pl.ds(pl.multiple_of(g * GROUP * LANES + c * LANES, LANES), LANES)
                total = (
                    taps_ref[pl.ds(c, TAPS + 1, stride=8), :]
                    + taps_ref[pl.ds(GROUP + c, TAPS + 1, stride=8), :]
                )
                sums_ref[0:TAPS, lanes] = total[0:TAPS]
                sums_ref[TERM_ROW : TERM_ROW + 1, lanes] = total[TAPS : TAPS + 1]

    else:
        @pl.loop(0, channels // LANES)
        def _(t):
            lanes = lane_block(t, LANES)
            wide = lane_block(t + base * own_tiles, LANES)
            source = tile_of(base, t, member, share)
            flows = []
            for i in range(images):
                factor = scaled_ref[i : i + 1, wide]
                flow_rows = []
                for h in range(height):
                    centered = mixed_ref[i, h, :, lanes] - mean_ref[i, h]
                    flow = rstd_ref[i, h] * (factor - centered * dot_ref[i, h])
                    flow_ref[i, h, :, lanes] = flow
                    flow_rows.append(flow)
                flows.append(flow_rows)
            bias = flows[0][0]
            for i in range(images):
                for h in range(height):
                    if i or h:
                        bias = bias + flows[i][h]
            taps_ref[TAPS * width : TAPS * width + width, :] = bias
            for b in range(KER):
                totals = [None] * KER
                for i in range(images):
                    moved = [
                        shift_cols(x_ref[i, h, :, source].astype(F32), b - REACH)
                        for h in range(height)
                    ]
                    for a in range(KER):
                        for h in range(max(0, REACH - a), min(height, height + REACH - a)):
                            term = flows[i][h] * moved[h + a - REACH]
                            totals[a] = term if totals[a] is None else totals[a] + term
                for a in range(KER):
                    tap = a * KER + b
                    taps_ref[tap * width : tap * width + width, :] = totals[a]
            rows = TAPS + 1
            total = taps_ref[pl.ds(0, rows, stride=width), :]
            for s in range(1, width):
                total = total + taps_ref[pl.ds(s, rows, stride=width), :]
            sums_ref[0:TAPS, lanes] = total[0:TAPS]
            sums_ref[TERM_ROW : TERM_ROW + 1, lanes] = total[TAPS : TAPS + 1]

    for m in range(channels // share):
        lanes = slice(m * share, (m + 1) * share)
        keep_ref[m] = sums_ref[pl.ds(pl.multiple_of(core * HALF_PAD, HALF_PAD), HALF_PAD), lanes].astype(BF)
        give_ref[m] = sums_ref[pl.ds(pl.multiple_of((1 - core) * HALF_PAD, HALF_PAD), HALF_PAD), lanes].astype(BF)


def terms_block(base, share, place, order, x_here, scaled, rows, mixed, mean, rstd, dots):
    width = x_here.shape[2]
    channels = mixed.shape[3]
    half = SHAPE((channels // share, HALF_PAD, share), BF)
    return pl.pallas_call(
        lambda place_ref, order_ref, *refs: terms_kernel(base, share, place_ref, *refs),
        out_shape=[half, half, SHAPE(mixed.shape, F32)],
        in_specs=[SM, ANY] + [VM] * 7,
        out_specs=[VM] * 3,
        scratch_shapes=[
            pltpu.VMEM((ROWS_PAD, channels), F32),
            pltpu.VMEM(((TAPS + 1) * width, LANES), F32),
            pltpu.VMEM((8, 64, LANES), F32),
            pltpu.VMEM((8, 64, LANES), F32),
            pltpu.VMEM((8, 8, 8, LANES), F32),
            pltpu.VMEM((8, 8, 8, LANES), F32),
        ],
        compiler_params=params(24),
        name="terms_block",
    )(place, order, *near([x_here, scaled, rows, mixed, mean, rstd, dots]))


def images_kernel(image, base, place_ref, flow_own, flow_rest, weight_own, weight_rest, shared_ref, out_ref, token_ref):
    height = flow_own.shape[1]
    share = weight_own.shape[1]
    own_tiles = share // LANES
    step = pl.program_id(0) + base
    token_ref[...] = jnp.zeros_like(token_ref)

    def piece(flow_ref, weight_ref, first):
        @pl.loop(0, own_tiles)
        def _(t):
            lanes = lane_block(t, LANES)
            wide = lane_block(t + step * own_tiles, LANES)
            near_lanes = lane_block(t + (step - first) * own_tiles, LANES)
            rows = [flow_ref[image, h, :, near_lanes] for h in range(height)]
            sums = conv_rows(rows, lambda tap: weight_ref[tap : tap + 1, near_lanes], True)
            for h in range(height):
                out_ref[0, h, :, lanes] = (sums[h] + shared_ref[image : image + 1, wide]).astype(BF)

    if base == 0:

        @pl.when(step == 0)
        def _():
            piece(flow_own, weight_own, 0)

    @pl.when(step != 0)
    def _():
        piece(flow_rest, weight_rest, 1)


def image_block(image, base, count, place, flow, weights, shared, order, out):
    first = out is None
    share = weights[0].shape[1]
    operands = [place, *near([*flow, *weights, shared]), order] + ([] if first else [out])

    def kernel(*refs):
        images_kernel(image, base, *refs[:6], refs[-2], refs[-1])

    return pl.pallas_call(
        kernel,
        grid_spec=pltpu.PrefetchScalarGridSpec(
            num_scalar_prefetch=1,
            grid=(count,),
            in_specs=[VM] * 5 + [ANY] + ([] if first else [HB]),
            out_specs=[
                pl.BlockSpec(
                    (1,) + flow[0].shape[1:3] + (share,),
                    lambda step, place_ref: (image, 0, 0, place_ref[0] ^ (step + base)),
                ),
                pl.BlockSpec((8, LANES), lambda step, place_ref: (0, 0)),
            ],
        ),
        out_shape=[
            SHAPE(flow[0].shape[:3] + (shared.shape[1],), BF),
            SHAPE((8, LANES), F32),
        ],
        input_output_aliases={} if first else {7: 0},
        compiler_params=params(24),
        cost_estimate=cost(1.5),
        name="image_block",
    )(*operands)


def image_cells_kernel(base, place_ref, flow_own, flow_rest, weight_own, weight_rest, shared_ref, out_ref, token_ref, *scratch):
    turn_ref, _, spread_ref, _ = scratch
    own_groups = weight_own.shape[1] // (GROUP * LANES)
    group = pl.program_id(0) + base
    token_ref[...] = jnp.zeros_like(token_ref)

    def one(flow_ref, weight_ref, g):
        for c in range(GROUP):
            lanes = pl.ds(pl.multiple_of(g * GROUP * LANES + c * LANES, LANES), LANES)
            column = weight_ref[:, lanes]
            for i in range(2):
                slot = i * GROUP + c
                spread_ref[slot * WEIGHT_ROWS : (slot + 1) * WEIGHT_ROWS, :] = column
                for h in range(8):
                    turn_ref[h, slot * 8 : slot * 8 + 8, :] = flow_ref[i, h, :, lanes]
        conv_group(scratch, None, True)
        for c in range(GROUP):
            wide = pl.ds(pl.multiple_of(group * GROUP * LANES + c * LANES, LANES), LANES)
            for i in range(2):
                shared = shared_ref[i : i + 1, wide]
                for h in range(8):
                    value = turn_ref[h, pl.ds(i * GROUP + c, 8, stride=8), :]
                    out_ref[i, h, :, c * LANES : (c + 1) * LANES] = (value + shared).astype(BF)

    @pl.when(group < own_groups)
    def _():
        one(flow_own, weight_own, group)

    @pl.when(group >= own_groups)
    def _():
        one(flow_rest, weight_rest, group - own_groups)


def image_cells(base, count, place, flow, weights, shared, order, out):
    first = out is None
    groups = weights[0].shape[1] // (GROUP * LANES)
    images, height, width = flow[0].shape[:3]
    operands = [place, *near([*flow, *weights, shared]), order] + ([] if first else [out])

    def kernel(*refs):
        image_cells_kernel(base, *refs[:6], *refs[-6:])

    def index(step, place_ref):
        group = step + base
        return (0, 0, 0, (place_ref[0] ^ (group // groups)) * groups + group % groups)

    return pl.pallas_call(
        kernel,
        grid_spec=pltpu.PrefetchScalarGridSpec(
            num_scalar_prefetch=1,
            grid=(count,),
            in_specs=[VM] * 5 + [ANY] + ([] if first else [HB]),
            out_specs=[
                pl.BlockSpec((images, height, width, GROUP * LANES), index),
                pl.BlockSpec((8, LANES), lambda step, place_ref: (0, 0)),
            ],
            scratch_shapes=conv_scratch(),
        ),
        out_shape=[
            SHAPE((images, height, width, shared.shape[1]), BF),
            SHAPE((8, LANES), F32),
        ],
        input_output_aliases={} if first else {7: 0},
        compiler_params=params(24),
        cost_estimate=cost(1.5),
        name="image_cells",
    )(*operands)


def head_grads_kernel(block, packed_low, packed_high, text_ref, order_ref, head_ref, text_grad_ref, token_ref):
    share = packed_low.shape[1] - 2 * text_ref.shape[1]
    width = text_ref.shape[1]
    step = pl.program_id(0)
    lanes = lane_block(step, block)
    grads = slice(share, share + width)
    images = jnp.concatenate([packed_low[:, lanes], packed_high[:, lanes]], axis=0)
    grad = jnp.concatenate([packed_low[:, grads], packed_high[:, grads]], axis=0)
    head_ref[...] = lax.dot_general(
        images, grad, (((0,), (0,)), ((), ())), preferred_element_type=F32
    )

    @pl.when(step == 0)
    def _():
        token_ref[...] = jnp.zeros_like(token_ref)
        units = slice(share + width, share + 2 * width)
        unit_all = jnp.concatenate([packed_low[:, units], packed_high[:, units]], axis=0)
        raw = text_ref[...].astype(F32)
        inverse = inverse_norm(raw)
        unit = raw * inverse
        pairs = pair_weights(unit_all, unit.astype(BF))
        text_sum = LOGIT_SCALE * lax.dot_general(
            pairs, unit_all, (((0,), (0,)), ((), ())), preferred_element_type=F32
        )
        text_grad_ref[...] = unit_back(unit, inverse, text_sum)


def head_grads_block(packed, text_here, share, order):
    rows, width = text_here.shape
    block = 512 if share % 512 == 0 else LANES
    return pl.pallas_call(
        lambda *refs: head_grads_kernel(block, *refs),
        grid=(share // block,),
        out_shape=[
            SHAPE((share, width), F32),
            SHAPE((rows, width), F32),
            SHAPE((8, LANES), F32),
        ],
        in_specs=[VM, VM, VM, ANY],
        out_specs=[
            pl.BlockSpec((block, width), lambda step: (step, 0)),
            pl.BlockSpec((rows, width), lambda step: (0, 0)),
            pl.BlockSpec((8, LANES), lambda step: (0, 0)),
        ],
        compiler_params=params(24),
        name="head_grads_block",
    )(*near([*packed, text_here]), order)


def split_kernel(place_ref, own_ref, other_ref, kernel_ref, term_ref):
    core = place_ref[1]
    rest = TAPS - HALF_PAD
    terms = slice(TERM_ROW - HALF_PAD, TERM_ROW - HALF_PAD + 4)

    def write(low_ref, high_ref):
        kernel_ref[0:HALF_PAD, :] = low_ref[...].astype(F32)
        high = high_ref[...].astype(F32)
        kernel_ref[HALF_PAD:TAPS, :] = high[0:rest]
        term_ref[...] = high[terms]

    @pl.when(core == 0)
    def _():
        write(own_ref, other_ref)

    @pl.when(core != 0)
    def _():
        write(other_ref, own_ref)


def split_block(place, own, other):
    share = own.shape[1]
    return pl.pallas_call(
        split_kernel,
        out_shape=[SHAPE((TAPS, share), F32), SHAPE((4, share), F32)],
        in_specs=[SM, VM, VM],
        out_specs=[VM, VM],
        compiler_params=params(24),
        name="split_block",
    )(place, *near([own, other]))


def per_device(image_maps, dw_kernel, channel_terms, head_weight, text_feats):
    members = lax.axis_size("fsdp")
    member = lax.axis_index("fsdp")
    core = lax.axis_index("dp") % 2
    place = jnp.stack([member, core]).astype(jnp.int32)
    others = range(1, members)
    dp_masks = bits_up(lax.axis_size("dp"))
    down = dp_masks[::-1]
    share = head_weight.shape[0]

    kernels = [swap(dw_kernel, "fsdp", m) for m in others]
    text_core = swap(text_feats, "dp", 1)
    x_here, weight_own, text_here = load_block(image_maps, dw_kernel, channel_terms, text_feats)
    pack_own = pack_block(weight_own, text_here, text_core)
    packs = [swap(pack_own, "fsdp", m) for m in others]
    mixed_own, sum_own = own_block(place, x_here, weight_own)

    text_rows = text_stack(text_here, text_core, packs, sum_own)
    text_masks = down[:-1]
    pieces, head_here, weight_rest, mixed_rest, saved = forward_block(
        place, head_weight, x_here, (mixed_own, sum_own, weight_own), text_rows, kernels, packs
    )
    weights = (weight_own, weight_rest)
    far_rows = swap(text_rows, "dp", text_masks[0])
    pieces = [pieces[0]] + [swap(pieces[m], "fsdp", m) for m in others]
    group, partial = head_project(pieces, head_here)
    orders = [saved[4]] + [partial] * len(text_masks)
    for mask, order in zip(text_masks[1:], orders):
        text_rows = stack_rows(text_rows, far_rows, order)
        far_rows = swap(text_rows, "dp", mask)
    texts = (text_rows, far_rows)

    partials = [partial] + [swap(partial, "fsdp", m) for m in others]
    packed, grads = loss_block(members, embed_sum(partials), texts, group, head_here)
    grads = [grads[0]] + [swap(grads[m], "fsdp", m) for m in others]

    mean, rstd, hatsum, hat, hrstd = saved
    cells = image_maps.shape[1] * image_maps.shape[2]
    shared, scaled, term_rows = pool_grad_block(grads, cells, weights, hatsum, hat, hrstd)
    mixed = (mixed_own, mixed_rest)
    dots = dots_block(scaled, mixed, mean, rstd)
    gather_masks = [down[1], down[0]] + list(down[2:])
    moving = swap(packed, "dp", gather_masks.pop(0))

    def terms_part(base, mixed_part, order):
        return terms_block(
            base, share, place, order, x_here, scaled, term_rows, mixed_part, mean, rstd, dots
        )

    packed = stack_rows(packed, moving, dots)
    keep_rest, give_rest, flow_rest = terms_part(1, mixed_rest, packed)
    keep_own, give_own, flow_own = terms_part(0, mixed_own, keep_rest)
    flow = (flow_own, flow_rest)

    fits = cells_fit(*image_maps.shape[:3], share)
    image_grads = None
    if fits:
        groups = image_maps.shape[3] // (GROUP * LANES)
        edges = [0, groups // 6, groups // 2, groups]
        parts = [(low, high - low) for low, high in zip(edges, edges[1:]) if high > low]
    else:
        parts = [(image, base) for image in range(image_maps.shape[0]) for base in (0, members // 2)]

    def image_parts(count, order, image_grads):
        token = order
        for _ in range(min(count, len(parts))):
            first, second = parts.pop(0)
            if fits:
                image_grads, token = image_cells(
                    first, second, place, flow, weights, shared, order, image_grads
                )
            else:
                image_grads, token = image_block(
                    first, second, members // 2, place, flow, weights, shared, order, image_grads
                )
        return image_grads, token

    chip = chip_sums(keep_rest, swap(give_rest, "dp", 1), keep_own)
    chip_own = chip_sums(keep_own, swap(give_own, "dp", 1), chip[0])[0]
    image_grads, token = image_parts(1, chip[0], None)
    packed = hold(packed, token)
    moving = swap(packed, "dp", gather_masks.pop(0))
    sent = add_all([chip_own] + [swap(chip[m - 1], "fsdp", m) for m in others], token)
    ring_masks = dp_masks[1:]
    counts = [1] + [2] * len(ring_masks)
    for mask, count in zip(ring_masks[:-1], counts):
        image_grads, token = image_parts(count, sent, image_grads)
        if mask == ring_masks[0]:
            packed = stack_rows(packed, moving, token)
            moving = swap(packed, "dp", gather_masks.pop(0))
        sent = add_all([sent, swap(sent, "dp", mask)], token)
    image_grads, token = image_parts(len(parts), sent, image_grads)
    while gather_masks:
        packed = stack_rows(packed, moving, token)
        moving = swap(packed, "dp", gather_masks.pop(0))
    head_grads, text_grads, token = head_grads_block((packed, moving), text_here, share, sent)
    sent = add_all([sent, swap(sent, "dp", ring_masks[-1])], token)
    kernel_grads, term_grads = split_block(place, sent, swap(sent, "dp", 1))
    return (image_grads, kernel_grads, term_grads, head_grads, text_grads)


def solution(mesh):
    in_specs = (
        P(("dp", "fsdp"), None, None, None),
        P(None, "fsdp"),
        P(None, "fsdp"),
        P("fsdp", None),
        P(("dp", "fsdp"), None),
    )
    out_specs = (
        P(("dp", "fsdp"), None, None, None),
        P(None, "fsdp"),
        P(None, "fsdp"),
        P("fsdp", None),
        P(("dp", "fsdp"), None),
    )
    return jax.shard_map(
        per_device, mesh=mesh, in_specs=in_specs, out_specs=out_specs, check_vma=False
    )
```

```python
import jax
import jax.numpy as jnp
from jax import lax
from jax.experimental import pallas as pl
from jax.experimental.pallas import tpu as pltpu
from jax.sharding import PartitionSpec as P

EPS = 1e-06
LOGIT_SCALE = 10.0
LOGIT_BIAS = -2.0
KER = 7
REACH = KER // 2
TAPS = KER * KER
LANES = 128
ROWS_PAD = 64
HALF_PAD = ROWS_PAD // 2
TERM_ROW = 56
GAIN_ROW = TAPS
WEIGHT_ROWS = 56
GROUP = 4
DOTS_COST = 3.0
SUM_COST = 1.0
BF = jnp.bfloat16
F32 = jnp.float32


def swap(value, axis, mask):
    count = lax.axis_size(axis)
    return lax.ppermute(value, axis, [(source, source ^ mask) for source in range(count)])


def bits_up(count):
    masks = []
    mask = 1
    while mask < count:
        masks.append(mask)
        mask *= 2
    return masks


def params(mebibytes):
    return pltpu.CompilerParams(vmem_limit_bytes=mebibytes * 1024 * 1024)


def cost(micros):
    return pl.CostEstimate(flops=int(micros * 1.1e9), bytes_accessed=0, transcendentals=0)


def far(arrays):
    return [pltpu.with_memory_space_constraint(value, pltpu.HBM) for value in arrays]


def near(arrays):
    return [pltpu.with_memory_space_constraint(value, pltpu.VMEM) for value in arrays]


VM = pl.BlockSpec(memory_space=pltpu.VMEM)
SM = pl.BlockSpec(memory_space=pltpu.SMEM)
HB = pl.BlockSpec(memory_space=pltpu.HBM)
ANY = pl.BlockSpec(memory_space=pl.ANY)
SHAPE = jax.ShapeDtypeStruct


def lane_block(index, width):
    return pl.ds(pl.multiple_of(index * width, LANES), width)


def shift_cols(value, step):
    if step == 0:
        return value
    width = value.shape[0]
    rolled = pltpu.roll(value, (-step) % width, 0)
    col = lax.broadcasted_iota(jnp.int32, value.shape, 0)
    inside = (col < width - step) if step > 0 else (col >= -step)
    return jnp.where(inside, rolled, 0.0)


def conv_rows(rows, tap_row, flip):
    height = len(rows)
    sums = [None] * height
    for b in range(KER):
        moved = [shift_cols(row, b - REACH) for row in rows]
        for a in range(KER):
            tap = (KER - 1 - a) * KER + (KER - 1 - b) if flip else a * KER + b
            weight = tap_row(tap)
            for h in range(max(0, REACH - a), min(height, height + REACH - a)):
                term = moved[h + a - REACH] * weight
                sums[h] = term if sums[h] is None else sums[h] + term
    return sums


def stack_rows(low, high, order):
    def kernel(low_ref, high_ref, order_ref, out_ref):
        both = jnp.concatenate([low_ref[...].astype(F32), high_ref[...].astype(F32)], axis=0)
        out_ref[...] = both.astype(out_ref.dtype)

    rows, width = low.shape
    return pl.pallas_call(
        kernel,
        out_shape=SHAPE((2 * rows, width), low.dtype),
        in_specs=[VM, VM, ANY],
        out_specs=VM,
        compiler_params=params(24),
        name="stack_rows",
    )(low, high, order)


def add_all(values, order):
    def kernel(*refs):
        total = refs[0][...].astype(F32)
        for ref in refs[1:-2]:
            total = total + ref[...].astype(F32)
        refs[-1][...] = total.astype(BF)

    return pl.pallas_call(
        kernel,
        out_shape=SHAPE(values[0].shape, BF),
        in_specs=[VM] * len(values) + [ANY],
        out_specs=VM,
        compiler_params=params(24),
        name="add_all",
    )(*values, order)


def hold(value, order):
    def kernel(value_ref, order_ref, out_ref):
        out_ref[...] = value_ref[...]

    return pl.pallas_call(
        kernel,
        out_shape=SHAPE(value.shape, value.dtype),
        in_specs=[VM, ANY],
        out_specs=VM,
        compiler_params=params(24),
        name="hold",
    )(value, order)


def chip_sums(keep, give, order):
    members = keep.shape[0]

    def kernel(keep_ref, give_ref, order_ref, *out_refs):
        for m in range(members):
            out_refs[m][...] = (keep_ref[m].astype(F32) + give_ref[m].astype(F32)).astype(BF)

    return pl.pallas_call(
        kernel,
        out_shape=[SHAPE(keep.shape[1:], BF)] * members,
        in_specs=[VM, VM, ANY],
        out_specs=[VM] * members,
        compiler_params=params(24),
        name="chip_sums",
    )(keep, give, order)


def together(tiles):
    return GROUP if tiles % GROUP == 0 else 1


def tile_of(base_piece, t, member, share):
    per_piece = share // LANES
    piece = base_piece + t // per_piece
    return lane_block((member ^ piece) * per_piece + t % per_piece, LANES)


def cells_fit(images, height, width, share):
    return images == 2 and height == 8 and width == 8 and share % (GROUP * LANES) == 0


def conv_scratch():
    return [
        pltpu.VMEM((8, 64, LANES), F32),
        pltpu.VMEM((8, 8, 8, LANES), F32),
        pltpu.VMEM((8 * WEIGHT_ROWS, LANES), F32),
        pltpu.VMEM((TAPS, 8, LANES), F32),
    ]


def load_cells(turn_ref, cell_ref):
    for h in range(8):
        for w in range(8):
            cell_ref[h, w] = turn_ref[h, pl.ds(w, 8, stride=8), :]


def conv_group(scratch, start, flip):
    turn_ref, cell_ref, spread_ref, tap_ref = scratch
    for tap in range(TAPS):
        source = TAPS - 1 - tap if flip else tap
        tap_ref[tap] = spread_ref[pl.ds(source, 8, stride=WEIGHT_ROWS), :]
    load_cells(turn_ref, cell_ref)
    for h in range(8):
        sums = [start] * 8
        for a in range(max(0, REACH - h), min(KER, 8 + REACH - h)):
            row = [cell_ref[h + a - REACH, w] for w in range(8)]
            for b in range(KER):
                weight = tap_ref[a * KER + b]
                for w in range(max(0, REACH - b), min(8, 8 + REACH - b)):
                    term = row[w + b - REACH] * weight
                    sums[w] = term if sums[w] is None else sums[w] + term
        for w in range(8):
            turn_ref[h, w * 8 : w * 8 + 8, :] = sums[w]


def conv_cells(groups, base_piece, member, share, x_ref, weight_ref, mixed_ref, sum_ref, scratch):
    turn_ref, cell_ref, spread_ref, tap_ref = scratch
    per_piece = share // (GROUP * LANES)

    @pl.loop(0, groups)
    def _(g):
        piece = base_piece + g // per_piece
        start = ((member ^ piece) * per_piece + g % per_piece) * GROUP * LANES
        for c in range(GROUP):
            lanes = pl.ds(pl.multiple_of(g * GROUP * LANES + c * LANES, LANES), LANES)
            source = pl.ds(pl.multiple_of(start + c * LANES, LANES), LANES)
            column = weight_ref[:, lanes]
            for i in range(2):
                slot = i * GROUP + c
                spread_ref[slot * WEIGHT_ROWS : (slot + 1) * WEIGHT_ROWS, :] = column
                for h in range(8):
                    turn_ref[h, slot * 8 : slot * 8 + 8, :] = x_ref[i, h, :, source].astype(F32)
        bias = spread_ref[pl.ds(GAIN_ROW, 8, stride=WEIGHT_ROWS), :]
        conv_group(scratch, bias, False)
        for h in range(8):
            for i in range(2):
                total = None
                for c in range(GROUP):
                    lanes = pl.ds(pl.multiple_of(g * GROUP * LANES + c * LANES, LANES), LANES)
                    value = turn_ref[h, pl.ds(i * GROUP + c, 8, stride=8), :]
                    mixed_ref[i, h, :, lanes] = value
                    total = value if total is None else total + value
                sum_ref[i, h] += total


def conv_tiles(tiles, base_piece, member, share, x_ref, weight_ref, mixed_ref, sum_ref, scratch):
    images, height, width = x_ref.shape[:3]
    if cells_fit(images, height, width, share):
        conv_cells(
            tiles // GROUP, base_piece, member, share, x_ref, weight_ref, mixed_ref, sum_ref, scratch
        )
        return

    @pl.loop(0, tiles)
    def _(t):
        lanes = lane_block(t, LANES)
        source = tile_of(base_piece, t, member, share)
        bias = weight_ref[GAIN_ROW : GAIN_ROW + 1, lanes]
        for i in range(images):
            rows = [x_ref[i, h, :, source].astype(F32) for h in range(height)]
            sums = conv_rows(rows, lambda tap: weight_ref[tap : tap + 1, lanes], False)
            for h in range(height):
                value = sums[h] + bias
                mixed_ref[i, h, :, lanes] = value
                sum_ref[i, h] += value


def text_chunks(embed_width, share):
    return [
        (chunk, first, min(share, embed_width - first))
        for chunk, first in enumerate(range(0, embed_width, share))
    ]


def pack_rows(texts, embed_width, share):
    return (4 + texts * len(text_chunks(embed_width, share)) + 7) // 8 * 8


def load_kernel(x_hbm, kernel_hbm, term_hbm, text_hbm, x_ref, weight_ref, text_ref, kernel_ref, term_ref, sems):
    copies = [
        pltpu.make_async_copy(kernel_hbm, kernel_ref, sems.at[0]),
        pltpu.make_async_copy(term_hbm, term_ref, sems.at[1]),
        pltpu.make_async_copy(text_hbm, text_ref, sems.at[2]),
        pltpu.make_async_copy(x_hbm, x_ref, sems.at[3]),
    ]
    for copy in copies:
        copy.start()
    for copy in copies[:3]:
        copy.wait()
    weight_ref[0:TAPS, :] = kernel_ref[...].astype(F32)
    weight_ref[GAIN_ROW : GAIN_ROW + 4, :] = term_ref[...].astype(F32)
    copies[3].wait()


def load_block(image_maps, dw_kernel, channel_terms, text_feats):
    share = dw_kernel.shape[1]
    return pl.pallas_call(
        load_kernel,
        out_shape=[
            SHAPE(image_maps.shape, BF),
            SHAPE((WEIGHT_ROWS, share), F32),
            SHAPE(text_feats.shape, BF),
        ],
        in_specs=[HB, HB, HB, HB],
        out_specs=[VM] * 3,
        scratch_shapes=[
            pltpu.VMEM(dw_kernel.shape, BF),
            pltpu.VMEM(channel_terms.shape, BF),
            pltpu.SemaphoreType.DMA((4,)),
        ],
        compiler_params=params(24),
        name="load_block",
    )(*far([image_maps, dw_kernel, channel_terms, text_feats]))


def pack_block(weight_own, text_here, text_core):
    images, embed_width = text_here.shape
    share = weight_own.shape[1]
    texts = 2 * images
    rows = pack_rows(texts, embed_width, share)

    def kernel(weight_ref, here_ref, core_ref, packed_ref, rows_ref):
        rows_ref[...] = jnp.zeros_like(rows_ref)
        rows_ref[0:4, :] = weight_ref[GAIN_ROW : GAIN_ROW + 4, :]
        both = jnp.concatenate([here_ref[...].astype(F32), core_ref[...].astype(F32)], axis=0)
        for chunk, first, width in text_chunks(embed_width, share):
            row = 4 + chunk * texts
            rows_ref[row : row + texts, 0:width] = both[:, first : first + width]
        packed_ref[...] = rows_ref[...].astype(BF)

    return pl.pallas_call(
        kernel,
        out_shape=SHAPE((rows, share), BF),
        in_specs=[VM] * 3,
        out_specs=VM,
        scratch_shapes=[pltpu.VMEM((rows, share), F32)],
        compiler_params=params(24),
        name="pack_block",
    )(*near([weight_own, text_here, text_core]))


def text_stack(text_here, text_core, packs, order):
    images, embed_width = text_here.shape
    share = packs[0].shape[1]
    members = len(packs) + 1
    total = 2 * members * images

    def kernel(*refs):
        here_ref, core_ref, pack_refs, out_ref, rows_ref = refs[0], refs[1], refs[2 : members + 1], refs[-2], refs[-1]
        half = members * images
        rows_ref[0:images, :] = here_ref[...].astype(F32)
        rows_ref[half : half + images, :] = core_ref[...].astype(F32)
        for m in range(1, members):
            pack = pack_refs[m - 1][...].astype(F32)
            for chunk, first, width in text_chunks(embed_width, share):
                for core in range(2):
                    row = 4 + (chunk * 2 + core) * images
                    place = core * half + m * images
                    rows_ref[place : place + images, first : first + width] = pack[
                        row : row + images, 0:width
                    ]
        raw = rows_ref[...]
        out_ref[...] = (raw * inverse_norm(raw)).astype(BF)

    return pl.pallas_call(
        kernel,
        out_shape=SHAPE((total, embed_width), BF),
        in_specs=[VM] * (members + 1) + [ANY],
        out_specs=VM,
        scratch_shapes=[pltpu.VMEM((total, embed_width), F32)],
        compiler_params=params(24),
        name="text_stack",
    )(text_here, text_core, *packs, order)


def own_block(place, x_here, weight_own):
    images, height, width, channels = x_here.shape
    share = weight_own.shape[1]

    def kernel(place_ref, x_ref, weight_ref, mixed_ref, sum_ref, *scratch):
        sum_ref[...] = jnp.zeros_like(sum_ref)
        conv_tiles(
            share // LANES, 0, place_ref[0], share, x_ref, weight_ref, mixed_ref, sum_ref, scratch
        )

    return pl.pallas_call(
        kernel,
        out_shape=[
            SHAPE((images, height, width, share), F32),
            SHAPE((images, height, width, LANES), F32),
        ],
        in_specs=[SM, VM, VM],
        out_specs=[VM] * 2,
        scratch_shapes=conv_scratch(),
        compiler_params=params(24),
        name="own_block",
    )(place, *near([x_here, weight_own]))


def forward_kernel(members, place_ref, head_hbm, x_ref, mixed_own, sum_own, weight_own, order_ref, *refs):
    kernel_refs, refs = refs[: members - 1], refs[members - 1 :]
    pack_refs, refs = refs[: members - 1], refs[members - 1 :]
    piece_refs, refs = refs[:members], refs[members:]
    head_ref, weight_rest, mixed_rest, mean_ref, rstd_ref, hatsum_ref, hat_ref, hrstd_ref, sum_ref, pool_ref, sem = refs[:11]
    scratch = refs[11:]
    images, height, width, channels = x_ref.shape
    share = channels // members
    cells = height * width
    member = place_ref[0]
    head_copy = pltpu.make_async_copy(head_hbm, head_ref, sem)
    head_copy.start()
    for m in range(1, members):
        lanes = slice((m - 1) * share, m * share)
        weight_rest[0:TAPS, lanes] = kernel_refs[m - 1][...].astype(F32)
        weight_rest[GAIN_ROW : GAIN_ROW + 4, lanes] = pack_refs[m - 1][...].astype(F32)[0:4]
    sum_ref[...] = sum_own[...]
    own_tiles = share // LANES
    rest_tiles = (members - 1) * own_tiles
    conv_tiles(rest_tiles, 1, member, share, x_ref, weight_rest, mixed_rest, sum_ref, scratch)
    parts = [(0, own_tiles, mixed_own, weight_own), (1, rest_tiles, mixed_rest, weight_rest)]

    mean = jnp.sum(sum_ref[...], axis=-1, keepdims=True) * (1.0 / channels)
    mean_ref[...] = jnp.broadcast_to(mean, mean_ref.shape)
    sum_ref[...] = jnp.zeros_like(sum_ref)
    for base, tiles, mixed_ref, weight_ref in parts:

        @pl.loop(0, tiles // together(tiles))
        def _(t):
            for i in range(images):
                for h in range(height):
                    total = None
                    for k in range(together(tiles)):
                        lanes = lane_block(t * together(tiles) + k, LANES)
                        value = mixed_ref[i, h, :, lanes] - mean_ref[i, h]
                        total = value * value if total is None else total + value * value
                    sum_ref[i, h] += total

    var = jnp.sum(sum_ref[...], axis=-1, keepdims=True) * (1.0 / channels)
    rstd_ref[...] = jnp.broadcast_to(lax.rsqrt(var + EPS), rstd_ref.shape)
    for base, tiles, mixed_ref, weight_ref in parts:

        @pl.loop(0, tiles // together(tiles))
        def _(step):
            for k in range(together(tiles)):
                t = step * together(tiles) + k
                lanes = lane_block(t, LANES)
                wide = lane_block(t + base * own_tiles, LANES)
                source = tile_of(base, t, member, share)
                scale = (
                    weight_ref[GAIN_ROW + 1 : GAIN_ROW + 2, lanes]
                    * weight_ref[GAIN_ROW + 2 : GAIN_ROW + 3, lanes]
                )
                for i in range(images):
                    hats = jnp.zeros((width, LANES), F32)
                    plain = jnp.zeros((width, LANES), F32)
                    for h in range(height):
                        hats = hats + (mixed_ref[i, h, :, lanes] - mean_ref[i, h]) * rstd_ref[i, h]
                        plain = plain + x_ref[i, h, :, source].astype(F32)
                    hat_row = jnp.sum(hats, axis=0, keepdims=True)
                    hatsum_ref[i : i + 1, wide] = hat_row
                    pool_ref[i : i + 1, wide] = (
                        jnp.sum(plain, axis=0, keepdims=True) + scale * hat_row
                    ) * (1.0 / cells)

    pooled = pool_ref[...]
    centered = pooled - jnp.mean(pooled, axis=1, keepdims=True)
    head_rstd = lax.rsqrt(jnp.mean(centered * centered, axis=1, keepdims=True) + EPS)
    hat = centered * head_rstd
    hat_ref[...] = hat
    hrstd_ref[...] = jnp.broadcast_to(head_rstd, hrstd_ref.shape)
    for m in range(members):
        gain = (
            weight_own[GAIN_ROW + 3 : GAIN_ROW + 4, :]
            if m == 0
            else weight_rest[GAIN_ROW + 3 : GAIN_ROW + 4, (m - 1) * share : m * share]
        )
        piece_refs[m][...] = (hat[:, m * share : (m + 1) * share] * gain).astype(BF)
    head_copy.wait()


def forward_block(place, head_weight, x_here, own, order, kernels, packs):
    images, height, width, channels = x_here.shape
    members = len(packs) + 1
    share = channels // members
    cell = (images, height, width, LANES)
    outs = [SHAPE((images, share), BF)] * members + [
        SHAPE(head_weight.shape, BF),
        SHAPE((WEIGHT_ROWS, channels - share), F32),
        SHAPE((images, height, width, channels - share), F32),
        SHAPE(cell, F32),
        SHAPE(cell, F32),
        SHAPE((images, channels), F32),
        SHAPE((images, channels), F32),
        SHAPE((images, LANES), F32),
    ]
    result = pl.pallas_call(
        lambda *refs: forward_kernel(members, *refs),
        out_shape=outs,
        in_specs=[SM, HB, VM, VM, VM, VM, ANY] + [VM] * (2 * (members - 1)),
        out_specs=[VM] * len(outs),
        scratch_shapes=[
            pltpu.VMEM(cell, F32),
            pltpu.VMEM((images, channels), F32),
            pltpu.SemaphoreType.DMA,
        ]
        + conv_scratch(),
        compiler_params=params(24),
        name="forward_block",
    )(place, *far([head_weight]), *near([x_here, *own]), order, *near([*kernels, *packs]))
    return result[:members], result[members], result[members + 1], result[members + 2], result[members + 3 :]


def head_kernel(members, *refs):
    group = jnp.concatenate([ref[...].astype(F32) for ref in refs[:members]], axis=0).astype(BF)
    weight_ref, group_ref, out_ref = refs[members:]
    group_ref[...] = group
    out_ref[...] = jnp.dot(group, weight_ref[...], preferred_element_type=F32)


def head_project(pieces, head_weight):
    members = len(pieces)
    share, embed_width = head_weight.shape
    rows = members * pieces[0].shape[0]
    return pl.pallas_call(
        lambda *refs: head_kernel(members, *refs),
        out_shape=[SHAPE((rows, share), BF), SHAPE((rows, embed_width), F32)],
        in_specs=[VM] * (members + 1),
        out_specs=[VM, VM],
        compiler_params=params(24),
        cost_estimate=cost(0.5),
        name="head_project",
    )(*near([*pieces, head_weight]))


def inverse_norm(vectors):
    return lax.rsqrt(jnp.sum(vectors * vectors, axis=1, keepdims=True) + EPS)


def pair_weights(images, texts):
    logits = (
        LOGIT_SCALE
        * lax.dot_general(images, texts, (((1,), (1,)), ((), ())), preferred_element_type=F32)
        + LOGIT_BIAS
    )
    here = lax.broadcasted_iota(jnp.int32, logits.shape, 0)
    there = lax.broadcasted_iota(jnp.int32, logits.shape, 1)
    positive = jnp.where(here == there, 1.0, 0.0).astype(F32)
    return (jax.nn.sigmoid(logits) - positive).astype(BF)


def unit_back(unit, inverse, grad):
    return inverse * (grad - unit * jnp.sum(unit * grad, axis=1, keepdims=True))


def embed_sum_kernel(members, *refs):
    total_rows = refs[0].shape[0]
    rows = total_rows // members
    embed = refs[0][...]
    for m in range(1, members):
        embed = embed + jnp.concatenate(
            [refs[m][(k ^ m) * rows : (k ^ m) * rows + rows, :] for k in range(members)], axis=0
        )
    refs[members][...] = embed


def embed_sum(partials):
    members = len(partials)
    return pl.pallas_call(
        lambda *refs: embed_sum_kernel(members, *refs),
        out_shape=SHAPE(partials[0].shape, F32),
        in_specs=[VM] * members,
        out_specs=VM,
        compiler_params=params(24),
        cost_estimate=cost(SUM_COST),
        name="embed_sum",
    )(*near(partials))


def loss_kernel(members, embed_ref, text_low, text_high, group_ref, weight_ref, packed_ref, *piece_refs):
    total_rows, width = embed_ref.shape
    rows = total_rows // members
    share = group_ref.shape[1]
    embed = embed_ref[...]
    inverse = inverse_norm(embed)
    unit = embed * inverse
    unit_bf = unit.astype(BF)
    texts = jnp.concatenate([text_low[...], text_high[...]], axis=0)
    unit_grad = LOGIT_SCALE * jnp.dot(
        pair_weights(unit_bf, texts), texts, preferred_element_type=F32
    )
    embed_grad = unit_back(unit, inverse, unit_grad).astype(BF)
    packed_ref[:, 0:share] = group_ref[...]
    packed_ref[:, share : share + width] = embed_grad
    packed_ref[:, share + width : share + 2 * width] = unit_bf
    part = lax.dot_general(
        embed_grad, weight_ref[...], (((1,), (1,)), ((), ())), preferred_element_type=F32
    )
    for m in range(members):
        piece_refs[m][...] = part[m * rows : m * rows + rows]


def loss_block(members, embed, texts, group, head_weight):
    total_rows, embed_width = embed.shape
    share = head_weight.shape[0]
    result = pl.pallas_call(
        lambda *refs: loss_kernel(members, *refs),
        out_shape=[SHAPE((total_rows, share + 2 * embed_width), BF)]
        + [SHAPE((total_rows // members, share), F32)] * members,
        in_specs=[VM] * 5,
        out_specs=[VM] * (members + 1),
        compiler_params=params(24),
        name="loss_block",
    )(*near([embed, *texts, group, head_weight]))
    return result[0], result[1:]


def pool_grad_kernel(members, cells, *refs):
    grad_refs, refs = refs[:members], refs[members:]
    weight_own, weight_rest, hatsum_ref, hat_ref, hrstd_ref, shared_ref, scaled_ref, rows_ref = refs

    def term_row(row):
        return jnp.concatenate(
            [weight_own[GAIN_ROW + row : GAIN_ROW + row + 1, :], weight_rest[GAIN_ROW + row : GAIN_ROW + row + 1, :]],
            axis=1,
        )

    grad = jnp.concatenate([ref[...] for ref in grad_refs], axis=1)
    hat = hat_ref[...]
    inner = grad * term_row(3)
    shared = (
        hrstd_ref[:, 0:1]
        * (
            inner
            - jnp.mean(inner, axis=1, keepdims=True)
            - hat * jnp.mean(inner * hat, axis=1, keepdims=True)
        )
        * (1.0 / cells)
    )
    shared_ref[...] = shared
    gain = term_row(1)
    scale = term_row(2)
    hat_total = jnp.sum(shared * hatsum_ref[...], axis=0, keepdims=True)
    rows_ref[...] = jnp.zeros_like(rows_ref)
    rows_ref[1:2, :] = hat_total * scale
    rows_ref[2:3, :] = hat_total * gain
    rows_ref[3:4, :] = jnp.sum(grad * hat, axis=0, keepdims=True)
    scaled = shared * (gain * scale)
    scaled_ref[...] = scaled - jnp.mean(scaled, axis=1, keepdims=True)


def pool_grad_block(grads, cells, weights, hatsum, hat, hrstd):
    members = len(grads)
    images, channels = hat.shape
    return pl.pallas_call(
        lambda *refs: pool_grad_kernel(members, cells, *refs),
        out_shape=[
            SHAPE((images, channels), F32),
            SHAPE((images, channels), F32),
            SHAPE((8, channels), F32),
        ],
        in_specs=[VM] * (members + 5),
        out_specs=[VM] * 3,
        compiler_params=params(24),
        cost_estimate=cost(0.4),
        name="pool_grad_block",
    )(*near([*grads, *weights, hatsum, hat, hrstd]))


def dots_kernel(scaled_ref, mixed_own, mixed_rest, mean_ref, rstd_ref, dot_ref):
    images, height = dot_ref.shape[:2]
    channels = scaled_ref.shape[1]
    own_tiles = mixed_own.shape[3] // LANES
    rest_tiles = mixed_rest.shape[3] // LANES
    dot_ref[...] = jnp.zeros_like(dot_ref)
    for first, tiles, mixed_ref in [(0, own_tiles, mixed_own), (own_tiles, rest_tiles, mixed_rest)]:

        @pl.loop(0, tiles // together(tiles))
        def _(t):
            for i in range(images):
                for h in range(height):
                    total = None
                    for k in range(together(tiles)):
                        tile = t * together(tiles) + k
                        factor = scaled_ref[i : i + 1, lane_block(tile + first, LANES)]
                        term = factor * (mixed_ref[i, h, :, lane_block(tile, LANES)] - mean_ref[i, h])
                        total = term if total is None else total + term
                    dot_ref[i, h] += total

    dots = jnp.sum(dot_ref[...], axis=-1, keepdims=True) * (1.0 / channels)
    dot_ref[...] = jnp.broadcast_to(dots, dot_ref.shape) * rstd_ref[...] * rstd_ref[...]


def dots_block(scaled, mixed, mean, rstd):
    return pl.pallas_call(
        dots_kernel,
        out_shape=SHAPE(mean.shape, F32),
        in_specs=[VM] * 5,
        out_specs=VM,
        compiler_params=params(24),
        cost_estimate=cost(DOTS_COST),
        name="dots_block",
    )(*near([scaled, *mixed, mean, rstd]))


def terms_kernel(base, share, place_ref, x_ref, scaled_ref, rows_ref, mixed_ref, mean_ref, rstd_ref, dot_ref, *refs):
    keep_ref, give_ref, flow_ref, sums_ref, taps_ref, turn_x, turn_flow, cell_x, cell_flow = refs
    images, height, width = x_ref.shape[:3]
    channels = mixed_ref.shape[3]
    own_tiles = share // LANES
    member = place_ref[0]
    core = place_ref[1]
    first = base * share
    sums_ref[TAPS // 8 * 8 : TERM_ROW, :] = jnp.zeros((TERM_ROW - TAPS // 8 * 8, channels), F32)
    sums_ref[TERM_ROW:ROWS_PAD, :] = rows_ref[:, first : first + channels]

    if cells_fit(images, height, width, share):
        per_piece = share // (GROUP * LANES)

        @pl.loop(0, channels // (GROUP * LANES))
        def _(g):
            piece = base + g // per_piece
            start = ((member ^ piece) * per_piece + g % per_piece) * GROUP * LANES
            for c in range(GROUP):
                here = g * GROUP * LANES + c * LANES
                lanes = pl.ds(pl.multiple_of(here, LANES), LANES)
                wide = pl.ds(pl.multiple_of(first + here, LANES), LANES)
                source = pl.ds(pl.multiple_of(start + c * LANES, LANES), LANES)
                for i in range(images):
                    slot = (i * GROUP + c) * width
                    factor = scaled_ref[i : i + 1, wide]
                    for h in range(height):
                        centered = mixed_ref[i, h, :, lanes] - mean_ref[i, h]
                        flow = rstd_ref[i, h] * (factor - centered * dot_ref[i, h])
                        flow_ref[i, h, :, lanes] = flow
                        turn_flow[h, slot : slot + width, :] = flow
                        turn_x[h, slot : slot + width, :] = x_ref[i, h, :, source].astype(F32)
            load_cells(turn_flow, cell_flow)
            load_cells(turn_x, cell_x)
            bias = None
            for a in range(KER):
                totals = [None] * KER
                for h in range(max(0, REACH - a), min(height, height + REACH - a)):
                    flows = [cell_flow[h, w] for w in range(width)]
                    row = [cell_x[h + a - REACH, w] for w in range(width)]
                    for b in range(KER):
                        for w in range(max(0, REACH - b), min(width, width + REACH - b)):
                            term = flows[w] * row[w + b - REACH]
                            totals[b] = term if totals[b] is None else totals[b] + term
                    if a == REACH:
                        for w in range(width):
                            bias = flows[w] if bias is None else bias + flows[w]
                for b in range(KER):
                    tap = a * KER + b
                    taps_ref[tap * 8 : tap * 8 + 8, :] = totals[b]
            taps_ref[TAPS * 8 : TAPS * 8 + 8, :] = bias
            for c in range(GROUP):
                lanes = pl.ds(pl.multiple_of(g * GROUP * LANES + c * LANES, LANES), LANES)
                total = (
                    taps_ref[pl.ds(c, TAPS + 1, stride=8), :]
                    + taps_ref[pl.ds(GROUP + c, TAPS + 1, stride=8), :]
                )
                sums_ref[0:TAPS, lanes] = total[0:TAPS]
                sums_ref[TERM_ROW : TERM_ROW + 1, lanes] = total[TAPS : TAPS + 1]

    else:
        @pl.loop(0, channels // LANES)
        def _(t):
            lanes = lane_block(t, LANES)
            wide = lane_block(t + base * own_tiles, LANES)
            source = tile_of(base, t, member, share)
            flows = []
            for i in range(images):
                factor = scaled_ref[i : i + 1, wide]
                flow_rows = []
                for h in range(height):
                    centered = mixed_ref[i, h, :, lanes] - mean_ref[i, h]
                    flow = rstd_ref[i, h] * (factor - centered * dot_ref[i, h])
                    flow_ref[i, h, :, lanes] = flow
                    flow_rows.append(flow)
                flows.append(flow_rows)
            bias = flows[0][0]
            for i in range(images):
                for h in range(height):
                    if i or h:
                        bias = bias + flows[i][h]
            taps_ref[TAPS * width : TAPS * width + width, :] = bias
            for b in range(KER):
                totals = [None] * KER
                for i in range(images):
                    moved = [
                        shift_cols(x_ref[i, h, :, source].astype(F32), b - REACH)
                        for h in range(height)
                    ]
                    for a in range(KER):
                        for h in range(max(0, REACH - a), min(height, height + REACH - a)):
                            term = flows[i][h] * moved[h + a - REACH]
                            totals[a] = term if totals[a] is None else totals[a] + term
                for a in range(KER):
                    tap = a * KER + b
                    taps_ref[tap * width : tap * width + width, :] = totals[a]
            rows = TAPS + 1
            total = taps_ref[pl.ds(0, rows, stride=width), :]
            for s in range(1, width):
                total = total + taps_ref[pl.ds(s, rows, stride=width), :]
            sums_ref[0:TAPS, lanes] = total[0:TAPS]
            sums_ref[TERM_ROW : TERM_ROW + 1, lanes] = total[TAPS : TAPS + 1]

    for m in range(channels // share):
        lanes = slice(m * share, (m + 1) * share)
        keep_ref[m] = sums_ref[pl.ds(pl.multiple_of(core * HALF_PAD, HALF_PAD), HALF_PAD), lanes].astype(BF)
        give_ref[m] = sums_ref[pl.ds(pl.multiple_of((1 - core) * HALF_PAD, HALF_PAD), HALF_PAD), lanes].astype(BF)


def terms_block(base, share, place, order, x_here, scaled, rows, mixed, mean, rstd, dots):
    width = x_here.shape[2]
    channels = mixed.shape[3]
    half = SHAPE((channels // share, HALF_PAD, share), BF)
    return pl.pallas_call(
        lambda place_ref, order_ref, *refs: terms_kernel(base, share, place_ref, *refs),
        out_shape=[half, half, SHAPE(mixed.shape, F32)],
        in_specs=[SM, ANY] + [VM] * 7,
        out_specs=[VM] * 3,
        scratch_shapes=[
            pltpu.VMEM((ROWS_PAD, channels), F32),
            pltpu.VMEM(((TAPS + 1) * width, LANES), F32),
            pltpu.VMEM((8, 64, LANES), F32),
            pltpu.VMEM((8, 64, LANES), F32),
            pltpu.VMEM((8, 8, 8, LANES), F32),
            pltpu.VMEM((8, 8, 8, LANES), F32),
        ],
        compiler_params=params(24),
        name="terms_block",
    )(place, order, *near([x_here, scaled, rows, mixed, mean, rstd, dots]))


def images_kernel(image, base, place_ref, flow_own, flow_rest, weight_own, weight_rest, shared_ref, out_ref, token_ref):
    height = flow_own.shape[1]
    share = weight_own.shape[1]
    own_tiles = share // LANES
    step = pl.program_id(0) + base
    token_ref[...] = jnp.zeros_like(token_ref)

    def piece(flow_ref, weight_ref, first):
        @pl.loop(0, own_tiles)
        def _(t):
            lanes = lane_block(t, LANES)
            wide = lane_block(t + step * own_tiles, LANES)
            near_lanes = lane_block(t + (step - first) * own_tiles, LANES)
            rows = [flow_ref[image, h, :, near_lanes] for h in range(height)]
            sums = conv_rows(rows, lambda tap: weight_ref[tap : tap + 1, near_lanes], True)
            for h in range(height):
                out_ref[0, h, :, lanes] = (sums[h] + shared_ref[image : image + 1, wide]).astype(BF)

    if base == 0:

        @pl.when(step == 0)
        def _():
            piece(flow_own, weight_own, 0)

    @pl.when(step != 0)
    def _():
        piece(flow_rest, weight_rest, 1)


def image_block(image, base, count, place, flow, weights, shared, order, out):
    first = out is None
    share = weights[0].shape[1]
    operands = [place, *near([*flow, *weights, shared]), order] + ([] if first else [out])

    def kernel(*refs):
        images_kernel(image, base, *refs[:6], refs[-2], refs[-1])

    return pl.pallas_call(
        kernel,
        grid_spec=pltpu.PrefetchScalarGridSpec(
            num_scalar_prefetch=1,
            grid=(count,),
            in_specs=[VM] * 5 + [ANY] + ([] if first else [HB]),
            out_specs=[
                pl.BlockSpec(
                    (1,) + flow[0].shape[1:3] + (share,),
                    lambda step, place_ref: (image, 0, 0, place_ref[0] ^ (step + base)),
                ),
                pl.BlockSpec((8, LANES), lambda step, place_ref: (0, 0)),
            ],
        ),
        out_shape=[
            SHAPE(flow[0].shape[:3] + (shared.shape[1],), BF),
            SHAPE((8, LANES), F32),
        ],
        input_output_aliases={} if first else {7: 0},
        compiler_params=params(24),
        cost_estimate=cost(1.5),
        name="image_block",
    )(*operands)


def image_cells_kernel(base, place_ref, flow_own, flow_rest, weight_own, weight_rest, shared_ref, out_ref, token_ref, *scratch):
    turn_ref, _, spread_ref, _ = scratch
    own_groups = weight_own.shape[1] // (GROUP * LANES)
    group = pl.program_id(0) + base
    token_ref[...] = jnp.zeros_like(token_ref)

    def one(flow_ref, weight_ref, g):
        for c in range(GROUP):
            lanes = pl.ds(pl.multiple_of(g * GROUP * LANES + c * LANES, LANES), LANES)
            column = weight_ref[:, lanes]
            for i in range(2):
                slot = i * GROUP + c
                spread_ref[slot * WEIGHT_ROWS : (slot + 1) * WEIGHT_ROWS, :] = column
                for h in range(8):
                    turn_ref[h, slot * 8 : slot * 8 + 8, :] = flow_ref[i, h, :, lanes]
        conv_group(scratch, None, True)
        for c in range(GROUP):
            wide = pl.ds(pl.multiple_of(group * GROUP * LANES + c * LANES, LANES), LANES)
            for i in range(2):
                shared = shared_ref[i : i + 1, wide]
                for h in range(8):
                    value = turn_ref[h, pl.ds(i * GROUP + c, 8, stride=8), :]
                    out_ref[i, h, :, c * LANES : (c + 1) * LANES] = (value + shared).astype(BF)

    @pl.when(group < own_groups)
    def _():
        one(flow_own, weight_own, group)

    @pl.when(group >= own_groups)
    def _():
        one(flow_rest, weight_rest, group - own_groups)


def image_cells(base, count, place, flow, weights, shared, order, out):
    first = out is None
    groups = weights[0].shape[1] // (GROUP * LANES)
    images, height, width = flow[0].shape[:3]
    operands = [place, *near([*flow, *weights, shared]), order] + ([] if first else [out])

    def kernel(*refs):
        image_cells_kernel(base, *refs[:6], *refs[-6:])

    def index(step, place_ref):
        group = step + base
        return (0, 0, 0, (place_ref[0] ^ (group // groups)) * groups + group % groups)

    return pl.pallas_call(
        kernel,
        grid_spec=pltpu.PrefetchScalarGridSpec(
            num_scalar_prefetch=1,
            grid=(count,),
            in_specs=[VM] * 5 + [ANY] + ([] if first else [HB]),
            out_specs=[
                pl.BlockSpec((images, height, width, GROUP * LANES), index),
                pl.BlockSpec((8, LANES), lambda step, place_ref: (0, 0)),
            ],
            scratch_shapes=conv_scratch(),
        ),
        out_shape=[
            SHAPE((images, height, width, shared.shape[1]), BF),
            SHAPE((8, LANES), F32),
        ],
        input_output_aliases={} if first else {7: 0},
        compiler_params=params(24),
        cost_estimate=cost(1.5),
        name="image_cells",
    )(*operands)


def head_grads_kernel(block, packed_low, packed_high, text_ref, order_ref, head_ref, text_grad_ref, token_ref):
    share = packed_low.shape[1] - 2 * text_ref.shape[1]
    width = text_ref.shape[1]
    step = pl.program_id(0)
    lanes = lane_block(step, block)
    grads = slice(share, share + width)
    images = jnp.concatenate([packed_low[:, lanes], packed_high[:, lanes]], axis=0)
    grad = jnp.concatenate([packed_low[:, grads], packed_high[:, grads]], axis=0)
    head_ref[...] = lax.dot_general(
        images, grad, (((0,), (0,)), ((), ())), preferred_element_type=F32
    )

    @pl.when(step == 0)
    def _():
        token_ref[...] = jnp.zeros_like(token_ref)
        units = slice(share + width, share + 2 * width)
        unit_all = jnp.concatenate([packed_low[:, units], packed_high[:, units]], axis=0)
        raw = text_ref[...].astype(F32)
        inverse = inverse_norm(raw)
        unit = raw * inverse
        pairs = pair_weights(unit_all, unit.astype(BF))
        text_sum = LOGIT_SCALE * lax.dot_general(
            pairs, unit_all, (((0,), (0,)), ((), ())), preferred_element_type=F32
        )
        text_grad_ref[...] = unit_back(unit, inverse, text_sum)


def head_grads_block(packed, text_here, share, order):
    rows, width = text_here.shape
    block = 512 if share % 512 == 0 else LANES
    return pl.pallas_call(
        lambda *refs: head_grads_kernel(block, *refs),
        grid=(share // block,),
        out_shape=[
            SHAPE((share, width), F32),
            SHAPE((rows, width), F32),
            SHAPE((8, LANES), F32),
        ],
        in_specs=[VM, VM, VM, ANY],
        out_specs=[
            pl.BlockSpec((block, width), lambda step: (step, 0)),
            pl.BlockSpec((rows, width), lambda step: (0, 0)),
            pl.BlockSpec((8, LANES), lambda step: (0, 0)),
        ],
        compiler_params=params(24),
        name="head_grads_block",
    )(*near([*packed, text_here]), order)


def split_kernel(place_ref, own_ref, other_ref, kernel_ref, term_ref):
    core = place_ref[1]
    rest = TAPS - HALF_PAD
    terms = slice(TERM_ROW - HALF_PAD, TERM_ROW - HALF_PAD + 4)

    def write(low_ref, high_ref):
        kernel_ref[0:HALF_PAD, :] = low_ref[...].astype(F32)
        high = high_ref[...].astype(F32)
        kernel_ref[HALF_PAD:TAPS, :] = high[0:rest]
        term_ref[...] = high[terms]

    @pl.when(core == 0)
    def _():
        write(own_ref, other_ref)

    @pl.when(core != 0)
    def _():
        write(other_ref, own_ref)


def split_block(place, own, other):
    share = own.shape[1]
    return pl.pallas_call(
        split_kernel,
        out_shape=[SHAPE((TAPS, share), F32), SHAPE((4, share), F32)],
        in_specs=[SM, VM, VM],
        out_specs=[VM, VM],
        compiler_params=params(24),
        name="split_block",
    )(place, *near([own, other]))


def per_device(image_maps, dw_kernel, channel_terms, head_weight, text_feats):
    members = lax.axis_size("fsdp")
    member = lax.axis_index("fsdp")
    core = lax.axis_index("dp") % 2
    place = jnp.stack([member, core]).astype(jnp.int32)
    others = range(1, members)
    dp_masks = bits_up(lax.axis_size("dp"))
    down = dp_masks[::-1]
    share = head_weight.shape[0]

    kernels = [swap(dw_kernel, "fsdp", m) for m in others]
    text_core = swap(text_feats, "dp", 1)
    x_here, weight_own, text_here = load_block(image_maps, dw_kernel, channel_terms, text_feats)
    pack_own = pack_block(weight_own, text_here, text_core)
    packs = [swap(pack_own, "fsdp", m) for m in others]
    mixed_own, sum_own = own_block(place, x_here, weight_own)

    text_rows = text_stack(text_here, text_core, packs, sum_own)
    text_masks = down[:-1]
    pieces, head_here, weight_rest, mixed_rest, saved = forward_block(
        place, head_weight, x_here, (mixed_own, sum_own, weight_own), text_rows, kernels, packs
    )
    weights = (weight_own, weight_rest)
    far_rows = swap(text_rows, "dp", text_masks[0])
    pieces = [pieces[0]] + [swap(pieces[m], "fsdp", m) for m in others]
    group, partial = head_project(pieces, head_here)
    orders = [saved[4]] + [partial] * len(text_masks)
    for mask, order in zip(text_masks[1:], orders):
        text_rows = stack_rows(text_rows, far_rows, order)
        far_rows = swap(text_rows, "dp", mask)
    texts = (text_rows, far_rows)

    partials = [partial] + [swap(partial, "fsdp", m) for m in others]
    packed, grads = loss_block(members, embed_sum(partials), texts, group, head_here)
    grads = [grads[0]] + [swap(grads[m], "fsdp", m) for m in others]

    mean, rstd, hatsum, hat, hrstd = saved
    cells = image_maps.shape[1] * image_maps.shape[2]
    shared, scaled, term_rows = pool_grad_block(grads, cells, weights, hatsum, hat, hrstd)
    mixed = (mixed_own, mixed_rest)
    dots = dots_block(scaled, mixed, mean, rstd)
    gather_masks = [down[1], down[0]] + list(down[2:])
    moving = swap(packed, "dp", gather_masks.pop(0))

    def terms_part(base, mixed_part, order):
        return terms_block(
            base, share, place, order, x_here, scaled, term_rows, mixed_part, mean, rstd, dots
        )

    packed = stack_rows(packed, moving, dots)
    keep_rest, give_rest, flow_rest = terms_part(1, mixed_rest, packed)
    keep_own, give_own, flow_own = terms_part(0, mixed_own, keep_rest)
    flow = (flow_own, flow_rest)

    fits = cells_fit(*image_maps.shape[:3], share)
    image_grads = None
    if fits:
        groups = image_maps.shape[3] // (GROUP * LANES)
        edges = [0, groups // 6, groups // 2, groups]
        parts = [(low, high - low) for low, high in zip(edges, edges[1:]) if high > low]
    else:
        parts = [(image, base) for image in range(image_maps.shape[0]) for base in (0, members // 2)]

    def image_parts(count, order, image_grads):
        token = order
        for _ in range(min(count, len(parts))):
            first, second = parts.pop(0)
            if fits:
                image_grads, token = image_cells(
                    first, second, place, flow, weights, shared, order, image_grads
                )
            else:
                image_grads, token = image_block(
                    first, second, members // 2, place, flow, weights, shared, order, image_grads
                )
        return image_grads, token

    chip = chip_sums(keep_rest, swap(give_rest, "dp", 1), keep_own)
    chip_own = chip_sums(keep_own, swap(give_own, "dp", 1), chip[0])[0]
    image_grads, token = image_parts(1, chip[0], None)
    packed = hold(packed, token)
    moving = swap(packed, "dp", gather_masks.pop(0))
    sent = add_all([chip_own] + [swap(chip[m - 1], "fsdp", m) for m in others], token)
    ring_masks = dp_masks[1:]
    counts = [1] + [2] * len(ring_masks)
    for mask, count in zip(ring_masks[:-1], counts):
        image_grads, token = image_parts(count, sent, image_grads)
        if mask == ring_masks[0]:
            packed = stack_rows(packed, moving, token)
            moving = swap(packed, "dp", gather_masks.pop(0))
        sent = add_all([sent, swap(sent, "dp", mask)], token)
    image_grads, token = image_parts(len(parts), sent, image_grads)
    while gather_masks:
        packed = stack_rows(packed, moving, token)
        moving = swap(packed, "dp", gather_masks.pop(0))
    head_grads, text_grads, token = head_grads_block((packed, moving), text_here, share, sent)
    sent = add_all([sent, swap(sent, "dp", ring_masks[-1])], token)
    kernel_grads, term_grads = split_block(place, sent, swap(sent, "dp", 1))
    return (image_grads, kernel_grads, term_grads, head_grads, text_grads)


def solution(mesh):
    in_specs = (
        P(("dp", "fsdp"), None, None, None),
        P(None, "fsdp"),
        P(None, "fsdp"),
        P("fsdp", None),
        P(("dp", "fsdp"), None),
    )
    out_specs = (
        P(("dp", "fsdp"), None, None, None),
        P(None, "fsdp"),
        P(None, "fsdp"),
        P("fsdp", None),
        P(("dp", "fsdp"), None),
    )
    return jax.shard_map(
        per_device, mesh=mesh, in_specs=in_specs, out_specs=out_specs, check_vma=False
    )
```

```python
import jax
import jax.numpy as jnp
from jax import lax
from jax.experimental import pallas as pl
from jax.experimental.pallas import tpu as pltpu
from jax.sharding import PartitionSpec as P

EPS = 1e-06
LOGIT_SCALE = 10.0
LOGIT_BIAS = -2.0
KER = 7
REACH = KER // 2
TAPS = KER * KER
LANES = 128
ROWS_PAD = 64
HALF_PAD = ROWS_PAD // 2
TERM_ROW = 56
GAIN_ROW = TAPS
WEIGHT_ROWS = 56
GROUP = 4
DOTS_COST = 3.0
SUM_COST = 1.0
BF = jnp.bfloat16
F32 = jnp.float32


def swap(value, axis, mask):
    count = lax.axis_size(axis)
    return lax.ppermute(value, axis, [(source, source ^ mask) for source in range(count)])


def bits_up(count):
    masks = []
    mask = 1
    while mask < count:
        masks.append(mask)
        mask *= 2
    return masks


def params(mebibytes):
    return pltpu.CompilerParams(vmem_limit_bytes=mebibytes * 1024 * 1024)


def cost(micros):
    return pl.CostEstimate(flops=int(micros * 1.1e9), bytes_accessed=0, transcendentals=0)


def far(arrays):
    return [pltpu.with_memory_space_constraint(value, pltpu.HBM) for value in arrays]


def near(arrays):
    return [pltpu.with_memory_space_constraint(value, pltpu.VMEM) for value in arrays]


VM = pl.BlockSpec(memory_space=pltpu.VMEM)
SM = pl.BlockSpec(memory_space=pltpu.SMEM)
HB = pl.BlockSpec(memory_space=pltpu.HBM)
ANY = pl.BlockSpec(memory_space=pl.ANY)
SHAPE = jax.ShapeDtypeStruct


def lane_block(index, width):
    return pl.ds(pl.multiple_of(index * width, LANES), width)


def shift_cols(value, step):
    if step == 0:
        return value
    width = value.shape[0]
    rolled = pltpu.roll(value, (-step) % width, 0)
    col = lax.broadcasted_iota(jnp.int32, value.shape, 0)
    inside = (col < width - step) if step > 0 else (col >= -step)
    return jnp.where(inside, rolled, 0.0)


def conv_rows(rows, tap_row, flip):
    height = len(rows)
    sums = [None] * height
    for b in range(KER):
        moved = [shift_cols(row, b - REACH) for row in rows]
        for a in range(KER):
            tap = (KER - 1 - a) * KER + (KER - 1 - b) if flip else a * KER + b
            weight = tap_row(tap)
            for h in range(max(0, REACH - a), min(height, height + REACH - a)):
                term = moved[h + a - REACH] * weight
                sums[h] = term if sums[h] is None else sums[h] + term
    return sums


def stack_rows(low, high, order):
    def kernel(low_ref, high_ref, order_ref, out_ref):
        both = jnp.concatenate([low_ref[...].astype(F32), high_ref[...].astype(F32)], axis=0)
        out_ref[...] = both.astype(out_ref.dtype)

    rows, width = low.shape
    return pl.pallas_call(
        kernel,
        out_shape=SHAPE((2 * rows, width), low.dtype),
        in_specs=[VM, VM, ANY],
        out_specs=VM,
        compiler_params=params(24),
        name="stack_rows",
    )(low, high, order)


def add_all(values, order):
    def kernel(*refs):
        total = refs[0][...].astype(F32)
        for ref in refs[1:-2]:
            total = total + ref[...].astype(F32)
        refs[-1][...] = total.astype(BF)

    return pl.pallas_call(
        kernel,
        out_shape=SHAPE(values[0].shape, BF),
        in_specs=[VM] * len(values) + [ANY],
        out_specs=VM,
        compiler_params=params(24),
        name="add_all",
    )(*values, order)


def hold(value, order):
    def kernel(value_ref, order_ref, out_ref):
        out_ref[...] = value_ref[...]

    return pl.pallas_call(
        kernel,
        out_shape=SHAPE(value.shape, value.dtype),
        in_specs=[VM, ANY],
        out_specs=VM,
        compiler_params=params(24),
        name="hold",
    )(value, order)


def chip_sums(keep, give, order):
    members = keep.shape[0]

    def kernel(keep_ref, give_ref, order_ref, *out_refs):
        for m in range(members):
            out_refs[m][...] = (keep_ref[m].astype(F32) + give_ref[m].astype(F32)).astype(BF)

    return pl.pallas_call(
        kernel,
        out_shape=[SHAPE(keep.shape[1:], BF)] * members,
        in_specs=[VM, VM, ANY],
        out_specs=[VM] * members,
        compiler_params=params(24),
        name="chip_sums",
    )(keep, give, order)


def together(tiles):
    return GROUP if tiles % GROUP == 0 else 1


def tile_of(base_piece, t, member, share):
    per_piece = share // LANES
    piece = base_piece + t // per_piece
    return lane_block((member ^ piece) * per_piece + t % per_piece, LANES)


def cells_fit(images, height, width, share):
    return images == 2 and height == 8 and width == 8 and share % (GROUP * LANES) == 0


def conv_scratch():
    return [
        pltpu.VMEM((8, 64, LANES), F32),
        pltpu.VMEM((8, 8, 8, LANES), F32),
        pltpu.VMEM((8 * WEIGHT_ROWS, LANES), F32),
        pltpu.VMEM((TAPS, 8, LANES), F32),
    ]


def load_cells(turn_ref, cell_ref):
    for h in range(8):
        for w in range(8):
            cell_ref[h, w] = turn_ref[h, pl.ds(w, 8, stride=8), :]


def conv_group(scratch, start, flip):
    turn_ref, cell_ref, spread_ref, tap_ref = scratch
    for tap in range(TAPS):
        source = TAPS - 1 - tap if flip else tap
        tap_ref[tap] = spread_ref[pl.ds(source, 8, stride=WEIGHT_ROWS), :]
    load_cells(turn_ref, cell_ref)
    for h in range(8):
        sums = [start] * 8
        for a in range(max(0, REACH - h), min(KER, 8 + REACH - h)):
            row = [cell_ref[h + a - REACH, w] for w in range(8)]
            for b in range(KER):
                weight = tap_ref[a * KER + b]
                for w in range(max(0, REACH - b), min(8, 8 + REACH - b)):
                    term = row[w + b - REACH] * weight
                    sums[w] = term if sums[w] is None else sums[w] + term
        for w in range(8):
            turn_ref[h, w * 8 : w * 8 + 8, :] = sums[w]


def conv_cells(groups, base_piece, member, share, x_ref, weight_ref, mixed_ref, sum_ref, scratch):
    turn_ref, cell_ref, spread_ref, tap_ref = scratch
    per_piece = share // (GROUP * LANES)

    @pl.loop(0, groups)
    def _(g):
        piece = base_piece + g // per_piece
        start = ((member ^ piece) * per_piece + g % per_piece) * GROUP * LANES
        for c in range(GROUP):
            lanes = pl.ds(pl.multiple_of(g * GROUP * LANES + c * LANES, LANES), LANES)
            source = pl.ds(pl.multiple_of(start + c * LANES, LANES), LANES)
            column = weight_ref[:, lanes]
            for i in range(2):
                slot = i * GROUP + c
                spread_ref[slot * WEIGHT_ROWS : (slot + 1) * WEIGHT_ROWS, :] = column
                for h in range(8):
                    turn_ref[h, slot * 8 : slot * 8 + 8, :] = x_ref[i, h, :, source].astype(F32)
        bias = spread_ref[pl.ds(GAIN_ROW, 8, stride=WEIGHT_ROWS), :]
        conv_group(scratch, bias, False)
        for h in range(8):
            for i in range(2):
                total = None
                for c in range(GROUP):
                    lanes = pl.ds(pl.multiple_of(g * GROUP * LANES + c * LANES, LANES), LANES)
                    value = turn_ref[h, pl.ds(i * GROUP + c, 8, stride=8), :]
                    mixed_ref[i, h, :, lanes] = value
                    total = value if total is None else total + value
                sum_ref[i, h] += total


def conv_tiles(tiles, base_piece, member, share, x_ref, weight_ref, mixed_ref, sum_ref, scratch):
    images, height, width = x_ref.shape[:3]
    if cells_fit(images, height, width, share):
        conv_cells(
            tiles // GROUP, base_piece, member, share, x_ref, weight_ref, mixed_ref, sum_ref, scratch
        )
        return

    @pl.loop(0, tiles)
    def _(t):
        lanes = lane_block(t, LANES)
        source = tile_of(base_piece, t, member, share)
        bias = weight_ref[GAIN_ROW : GAIN_ROW + 1, lanes]
        for i in range(images):
            rows = [x_ref[i, h, :, source].astype(F32) for h in range(height)]
            sums = conv_rows(rows, lambda tap: weight_ref[tap : tap + 1, lanes], False)
            for h in range(height):
                value = sums[h] + bias
                mixed_ref[i, h, :, lanes] = value
                sum_ref[i, h] += value


def text_chunks(embed_width, share):
    return [
        (chunk, first, min(share, embed_width - first))
        for chunk, first in enumerate(range(0, embed_width, share))
    ]


def pack_rows(texts, embed_width, share):
    return (4 + texts * len(text_chunks(embed_width, share)) + 7) // 8 * 8


def load_kernel(x_hbm, kernel_hbm, term_hbm, text_hbm, x_ref, weight_ref, text_ref, kernel_ref, term_ref, sems):
    copies = [
        pltpu.make_async_copy(kernel_hbm, kernel_ref, sems.at[0]),
        pltpu.make_async_copy(term_hbm, term_ref, sems.at[1]),
        pltpu.make_async_copy(text_hbm, text_ref, sems.at[2]),
        pltpu.make_async_copy(x_hbm, x_ref, sems.at[3]),
    ]
    for copy in copies:
        copy.start()
    for copy in copies[:3]:
        copy.wait()
    weight_ref[0:TAPS, :] = kernel_ref[...].astype(F32)
    weight_ref[GAIN_ROW : GAIN_ROW + 4, :] = term_ref[...].astype(F32)
    copies[3].wait()


def load_block(image_maps, dw_kernel, channel_terms, text_feats):
    share = dw_kernel.shape[1]
    return pl.pallas_call(
        load_kernel,
        out_shape=[
            SHAPE(image_maps.shape, BF),
            SHAPE((WEIGHT_ROWS, share), F32),
            SHAPE(text_feats.shape, BF),
        ],
        in_specs=[HB, HB, HB, HB],
        out_specs=[VM] * 3,
        scratch_shapes=[
            pltpu.VMEM(dw_kernel.shape, BF),
            pltpu.VMEM(channel_terms.shape, BF),
            pltpu.SemaphoreType.DMA((4,)),
        ],
        compiler_params=params(24),
        name="load_block",
    )(*far([image_maps, dw_kernel, channel_terms, text_feats]))


def pack_block(weight_own, text_here, text_core):
    images, embed_width = text_here.shape
    share = weight_own.shape[1]
    texts = 2 * images
    rows = pack_rows(texts, embed_width, share)

    def kernel(weight_ref, here_ref, core_ref, packed_ref, rows_ref):
        rows_ref[...] = jnp.zeros_like(rows_ref)
        rows_ref[0:4, :] = weight_ref[GAIN_ROW : GAIN_ROW + 4, :]
        both = jnp.concatenate([here_ref[...].astype(F32), core_ref[...].astype(F32)], axis=0)
        for chunk, first, width in text_chunks(embed_width, share):
            row = 4 + chunk * texts
            rows_ref[row : row + texts, 0:width] = both[:, first : first + width]
        packed_ref[...] = rows_ref[...].astype(BF)

    return pl.pallas_call(
        kernel,
        out_shape=SHAPE((rows, share), BF),
        in_specs=[VM] * 3,
        out_specs=VM,
        scratch_shapes=[pltpu.VMEM((rows, share), F32)],
        compiler_params=params(24),
        name="pack_block",
    )(*near([weight_own, text_here, text_core]))


def text_stack(text_here, text_core, packs, order):
    images, embed_width = text_here.shape
    share = packs[0].shape[1]
    members = len(packs) + 1
    total = 2 * members * images

    def kernel(*refs):
        here_ref, core_ref, pack_refs, out_ref, rows_ref = refs[0], refs[1], refs[2 : members + 1], refs[-2], refs[-1]
        half = members * images
        rows_ref[0:images, :] = here_ref[...].astype(F32)
        rows_ref[half : half + images, :] = core_ref[...].astype(F32)
        for m in range(1, members):
            pack = pack_refs[m - 1][...].astype(F32)
            for chunk, first, width in text_chunks(embed_width, share):
                for core in range(2):
                    row = 4 + (chunk * 2 + core) * images
                    place = core * half + m * images
                    rows_ref[place : place + images, first : first + width] = pack[
                        row : row + images, 0:width
                    ]
        raw = rows_ref[...]
        out_ref[...] = (raw * inverse_norm(raw)).astype(BF)

    return pl.pallas_call(
        kernel,
        out_shape=SHAPE((total, embed_width), BF),
        in_specs=[VM] * (members + 1) + [ANY],
        out_specs=VM,
        scratch_shapes=[pltpu.VMEM((total, embed_width), F32)],
        compiler_params=params(24),
        name="text_stack",
    )(text_here, text_core, *packs, order)


def own_block(place, x_here, weight_own):
    images, height, width, channels = x_here.shape
    share = weight_own.shape[1]

    def kernel(place_ref, x_ref, weight_ref, mixed_ref, sum_ref, *scratch):
        sum_ref[...] = jnp.zeros_like(sum_ref)
        conv_tiles(
            share // LANES, 0, place_ref[0], share, x_ref, weight_ref, mixed_ref, sum_ref, scratch
        )

    return pl.pallas_call(
        kernel,
        out_shape=[
            SHAPE((images, height, width, share), F32),
            SHAPE((images, height, width, LANES), F32),
        ],
        in_specs=[SM, VM, VM],
        out_specs=[VM] * 2,
        scratch_shapes=conv_scratch(),
        compiler_params=params(24),
        name="own_block",
    )(place, *near([x_here, weight_own]))


def forward_kernel(members, place_ref, head_hbm, x_ref, mixed_own, sum_own, weight_own, order_ref, *refs):
    kernel_refs, refs = refs[: members - 1], refs[members - 1 :]
    pack_refs, refs = refs[: members - 1], refs[members - 1 :]
    piece_refs, refs = refs[:members], refs[members:]
    head_ref, weight_rest, mixed_rest, mean_ref, rstd_ref, hatsum_ref, hat_ref, hrstd_ref, sum_ref, pool_ref, sem = refs[:11]
    scratch = refs[11:]
    images, height, width, channels = x_ref.shape
    share = channels // members
    cells = height * width
    member = place_ref[0]
    head_copy = pltpu.make_async_copy(head_hbm, head_ref, sem)
    head_copy.start()
    for m in range(1, members):
        lanes = slice((m - 1) * share, m * share)
        weight_rest[0:TAPS, lanes] = kernel_refs[m - 1][...].astype(F32)
        weight_rest[GAIN_ROW : GAIN_ROW + 4, lanes] = pack_refs[m - 1][...].astype(F32)[0:4]
    sum_ref[...] = sum_own[...]
    own_tiles = share // LANES
    rest_tiles = (members - 1) * own_tiles
    conv_tiles(rest_tiles, 1, member, share, x_ref, weight_rest, mixed_rest, sum_ref, scratch)
    parts = [(0, own_tiles, mixed_own, weight_own), (1, rest_tiles, mixed_rest, weight_rest)]

    mean = jnp.sum(sum_ref[...], axis=-1, keepdims=True) * (1.0 / channels)
    mean_ref[...] = jnp.broadcast_to(mean, mean_ref.shape)
    sum_ref[...] = jnp.zeros_like(sum_ref)
    for base, tiles, mixed_ref, weight_ref in parts:

        @pl.loop(0, tiles // together(tiles))
        def _(t):
            for i in range(images):
                for h in range(height):
                    total = None
                    for k in range(together(tiles)):
                        lanes = lane_block(t * together(tiles) + k, LANES)
                        value = mixed_ref[i, h, :, lanes] - mean_ref[i, h]
                        total = value * value if total is None else total + value * value
                    sum_ref[i, h] += total

    var = jnp.sum(sum_ref[...], axis=-1, keepdims=True) * (1.0 / channels)
    rstd_ref[...] = jnp.broadcast_to(lax.rsqrt(var + EPS), rstd_ref.shape)
    for base, tiles, mixed_ref, weight_ref in parts:

        @pl.loop(0, tiles // together(tiles))
        def _(step):
            for k in range(together(tiles)):
                t = step * together(tiles) + k
                lanes = lane_block(t, LANES)
                wide = lane_block(t + base * own_tiles, LANES)
                source = tile_of(base, t, member, share)
                scale = (
                    weight_ref[GAIN_ROW + 1 : GAIN_ROW + 2, lanes]
                    * weight_ref[GAIN_ROW + 2 : GAIN_ROW + 3, lanes]
                )
                for i in range(images):
                    hats = jnp.zeros((width, LANES), F32)
                    plain = jnp.zeros((width, LANES), F32)
                    for h in range(height):
                        hats = hats + (mixed_ref[i, h, :, lanes] - mean_ref[i, h]) * rstd_ref[i, h]
                        plain = plain + x_ref[i, h, :, source].astype(F32)
                    hat_row = jnp.sum(hats, axis=0, keepdims=True)
                    hatsum_ref[i : i + 1, wide] = hat_row
                    pool_ref[i : i + 1, wide] = (
                        jnp.sum(plain, axis=0, keepdims=True) + scale * hat_row
                    ) * (1.0 / cells)

    pooled = pool_ref[...]
    centered = pooled - jnp.mean(pooled, axis=1, keepdims=True)
    head_rstd = lax.rsqrt(jnp.mean(centered * centered, axis=1, keepdims=True) + EPS)
    hat = centered * head_rstd
    hat_ref[...] = hat
    hrstd_ref[...] = jnp.broadcast_to(head_rstd, hrstd_ref.shape)
    for m in range(members):
        gain = (
            weight_own[GAIN_ROW + 3 : GAIN_ROW + 4, :]
            if m == 0
            else weight_rest[GAIN_ROW + 3 : GAIN_ROW + 4, (m - 1) * share : m * share]
        )
        piece_refs[m][...] = (hat[:, m * share : (m + 1) * share] * gain).astype(BF)
    head_copy.wait()


def forward_block(place, head_weight, x_here, own, order, kernels, packs):
    images, height, width, channels = x_here.shape
    members = len(packs) + 1
    share = channels // members
    cell = (images, height, width, LANES)
    outs = [SHAPE((images, share), BF)] * members + [
        SHAPE(head_weight.shape, BF),
        SHAPE((WEIGHT_ROWS, channels - share), F32),
        SHAPE((images, height, width, channels - share), F32),
        SHAPE(cell, F32),
        SHAPE(cell, F32),
        SHAPE((images, channels), F32),
        SHAPE((images, channels), F32),
        SHAPE((images, LANES), F32),
    ]
    result = pl.pallas_call(
        lambda *refs: forward_kernel(members, *refs),
        out_shape=outs,
        in_specs=[SM, HB, VM, VM, VM, VM, ANY] + [VM] * (2 * (members - 1)),
        out_specs=[VM] * len(outs),
        scratch_shapes=[
            pltpu.VMEM(cell, F32),
            pltpu.VMEM((images, channels), F32),
            pltpu.SemaphoreType.DMA,
        ]
        + conv_scratch(),
        compiler_params=params(24),
        name="forward_block",
    )(place, *far([head_weight]), *near([x_here, *own]), order, *near([*kernels, *packs]))
    return result[:members], result[members], result[members + 1], result[members + 2], result[members + 3 :]


def head_kernel(members, *refs):
    group = jnp.concatenate([ref[...].astype(F32) for ref in refs[:members]], axis=0).astype(BF)
    weight_ref, group_ref, out_ref = refs[members:]
    group_ref[...] = group
    out_ref[...] = jnp.dot(group, weight_ref[...], preferred_element_type=F32)


def head_project(pieces, head_weight):
    members = len(pieces)
    share, embed_width = head_weight.shape
    rows = members * pieces[0].shape[0]
    return pl.pallas_call(
        lambda *refs: head_kernel(members, *refs),
        out_shape=[SHAPE((rows, share), BF), SHAPE((rows, embed_width), F32)],
        in_specs=[VM] * (members + 1),
        out_specs=[VM, VM],
        compiler_params=params(24),
        cost_estimate=cost(0.5),
        name="head_project",
    )(*near([*pieces, head_weight]))


def inverse_norm(vectors):
    return lax.rsqrt(jnp.sum(vectors * vectors, axis=1, keepdims=True) + EPS)


def pair_weights(images, texts):
    logits = (
        LOGIT_SCALE
        * lax.dot_general(images, texts, (((1,), (1,)), ((), ())), preferred_element_type=F32)
        + LOGIT_BIAS
    )
    here = lax.broadcasted_iota(jnp.int32, logits.shape, 0)
    there = lax.broadcasted_iota(jnp.int32, logits.shape, 1)
    positive = jnp.where(here == there, 1.0, 0.0).astype(F32)
    return (jax.nn.sigmoid(logits) - positive).astype(BF)


def unit_back(unit, inverse, grad):
    return inverse * (grad - unit * jnp.sum(unit * grad, axis=1, keepdims=True))


def embed_sum_kernel(members, *refs):
    total_rows = refs[0].shape[0]
    rows = total_rows // members
    embed = refs[0][...]
    for m in range(1, members):
        embed = embed + jnp.concatenate(
            [refs[m][(k ^ m) * rows : (k ^ m) * rows + rows, :] for k in range(members)], axis=0
        )
    refs[members][...] = embed


def embed_sum(partials):
    members = len(partials)
    return pl.pallas_call(
        lambda *refs: embed_sum_kernel(members, *refs),
        out_shape=SHAPE(partials[0].shape, F32),
        in_specs=[VM] * members,
        out_specs=VM,
        compiler_params=params(24),
        cost_estimate=cost(SUM_COST),
        name="embed_sum",
    )(*near(partials))


def loss_kernel(members, embed_ref, text_low, text_high, group_ref, weight_ref, packed_ref, *piece_refs):
    total_rows, width = embed_ref.shape
    rows = total_rows // members
    share = group_ref.shape[1]
    embed = embed_ref[...]
    inverse = inverse_norm(embed)
    unit = embed * inverse
    unit_bf = unit.astype(BF)
    texts = jnp.concatenate([text_low[...], text_high[...]], axis=0)
    unit_grad = LOGIT_SCALE * jnp.dot(
        pair_weights(unit_bf, texts), texts, preferred_element_type=F32
    )
    embed_grad = unit_back(unit, inverse, unit_grad).astype(BF)
    packed_ref[:, 0:share] = group_ref[...]
    packed_ref[:, share : share + width] = embed_grad
    packed_ref[:, share + width : share + 2 * width] = unit_bf
    part = lax.dot_general(
        embed_grad, weight_ref[...], (((1,), (1,)), ((), ())), preferred_element_type=F32
    )
    for m in range(members):
        piece_refs[m][...] = part[m * rows : m * rows + rows]


def loss_block(members, embed, texts, group, head_weight):
    total_rows, embed_width = embed.shape
    share = head_weight.shape[0]
    result = pl.pallas_call(
        lambda *refs: loss_kernel(members, *refs),
        out_shape=[SHAPE((total_rows, share + 2 * embed_width), BF)]
        + [SHAPE((total_rows // members, share), F32)] * members,
        in_specs=[VM] * 5,
        out_specs=[VM] * (members + 1),
        compiler_params=params(24),
        name="loss_block",
    )(*near([embed, *texts, group, head_weight]))
    return result[0], result[1:]


def pool_grad_kernel(members, cells, *refs):
    grad_refs, refs = refs[:members], refs[members:]
    weight_own, weight_rest, hatsum_ref, hat_ref, hrstd_ref, shared_ref, scaled_ref, rows_ref = refs

    def term_row(row):
        return jnp.concatenate(
            [weight_own[GAIN_ROW + row : GAIN_ROW + row + 1, :], weight_rest[GAIN_ROW + row : GAIN_ROW + row + 1, :]],
            axis=1,
        )

    grad = jnp.concatenate([ref[...] for ref in grad_refs], axis=1)
    hat = hat_ref[...]
    inner = grad * term_row(3)
    shared = (
        hrstd_ref[:, 0:1]
        * (
            inner
            - jnp.mean(inner, axis=1, keepdims=True)
            - hat * jnp.mean(inner * hat, axis=1, keepdims=True)
        )
        * (1.0 / cells)
    )
    shared_ref[...] = shared
    gain = term_row(1)
    scale = term_row(2)
    hat_total = jnp.sum(shared * hatsum_ref[...], axis=0, keepdims=True)
    rows_ref[...] = jnp.zeros_like(rows_ref)
    rows_ref[1:2, :] = hat_total * scale
    rows_ref[2:3, :] = hat_total * gain
    rows_ref[3:4, :] = jnp.sum(grad * hat, axis=0, keepdims=True)
    scaled = shared * (gain * scale)
    scaled_ref[...] = scaled - jnp.mean(scaled, axis=1, keepdims=True)


def pool_grad_block(grads, cells, weights, hatsum, hat, hrstd):
    members = len(grads)
    images, channels = hat.shape
    return pl.pallas_call(
        lambda *refs: pool_grad_kernel(members, cells, *refs),
        out_shape=[
            SHAPE((images, channels), F32),
            SHAPE((images, channels), F32),
            SHAPE((8, channels), F32),
        ],
        in_specs=[VM] * (members + 5),
        out_specs=[VM] * 3,
        compiler_params=params(24),
        cost_estimate=cost(0.4),
        name="pool_grad_block",
    )(*near([*grads, *weights, hatsum, hat, hrstd]))


def dots_kernel(scaled_ref, mixed_own, mixed_rest, mean_ref, rstd_ref, dot_ref):
    images, height = dot_ref.shape[:2]
    channels = scaled_ref.shape[1]
    own_tiles = mixed_own.shape[3] // LANES
    rest_tiles = mixed_rest.shape[3] // LANES
    dot_ref[...] = jnp.zeros_like(dot_ref)
    for first, tiles, mixed_ref in [(0, own_tiles, mixed_own), (own_tiles, rest_tiles, mixed_rest)]:

        @pl.loop(0, tiles // together(tiles))
        def _(t):
            for i in range(images):
                for h in range(height):
                    total = None
                    for k in range(together(tiles)):
                        tile = t * together(tiles) + k
                        factor = scaled_ref[i : i + 1, lane_block(tile + first, LANES)]
                        term = factor * (mixed_ref[i, h, :, lane_block(tile, LANES)] - mean_ref[i, h])
                        total = term if total is None else total + term
                    dot_ref[i, h] += total

    dots = jnp.sum(dot_ref[...], axis=-1, keepdims=True) * (1.0 / channels)
    dot_ref[...] = jnp.broadcast_to(dots, dot_ref.shape) * rstd_ref[...] * rstd_ref[...]


def dots_block(scaled, mixed, mean, rstd):
    return pl.pallas_call(
        dots_kernel,
        out_shape=SHAPE(mean.shape, F32),
        in_specs=[VM] * 5,
        out_specs=VM,
        compiler_params=params(24),
        cost_estimate=cost(DOTS_COST),
        name="dots_block",
    )(*near([scaled, *mixed, mean, rstd]))


def terms_kernel(base, share, place_ref, x_ref, scaled_ref, rows_ref, mixed_ref, mean_ref, rstd_ref, dot_ref, *refs):
    keep_ref, give_ref, flow_ref, sums_ref, taps_ref, turn_x, turn_flow, cell_x, cell_flow = refs
    images, height, width = x_ref.shape[:3]
    channels = mixed_ref.shape[3]
    own_tiles = share // LANES
    member = place_ref[0]
    core = place_ref[1]
    first = base * share
    sums_ref[TAPS // 8 * 8 : TERM_ROW, :] = jnp.zeros((TERM_ROW - TAPS // 8 * 8, channels), F32)
    sums_ref[TERM_ROW:ROWS_PAD, :] = rows_ref[:, first : first + channels]

    if cells_fit(images, height, width, share):
        per_piece = share // (GROUP * LANES)

        @pl.loop(0, channels // (GROUP * LANES))
        def _(g):
            piece = base + g // per_piece
            start = ((member ^ piece) * per_piece + g % per_piece) * GROUP * LANES
            for c in range(GROUP):
                here = g * GROUP * LANES + c * LANES
                lanes = pl.ds(pl.multiple_of(here, LANES), LANES)
                wide = pl.ds(pl.multiple_of(first + here, LANES), LANES)
                source = pl.ds(pl.multiple_of(start + c * LANES, LANES), LANES)
                for i in range(images):
                    slot = (i * GROUP + c) * width
                    factor = scaled_ref[i : i + 1, wide]
                    for h in range(height):
                        centered = mixed_ref[i, h, :, lanes] - mean_ref[i, h]
                        flow = rstd_ref[i, h] * (factor - centered * dot_ref[i, h])
                        flow_ref[i, h, :, lanes] = flow
                        turn_flow[h, slot : slot + width, :] = flow
                        turn_x[h, slot : slot + width, :] = x_ref[i, h, :, source].astype(F32)
            load_cells(turn_flow, cell_flow)
            load_cells(turn_x, cell_x)
            bias = None
            for a in range(KER):
                totals = [None] * KER
                for h in range(max(0, REACH - a), min(height, height + REACH - a)):
                    flows = [cell_flow[h, w] for w in range(width)]
                    row = [cell_x[h + a - REACH, w] for w in range(width)]
                    for b in range(KER):
                        for w in range(max(0, REACH - b), min(width, width + REACH - b)):
                            term = flows[w] * row[w + b - REACH]
                            totals[b] = term if totals[b] is None else totals[b] + term
                    if a == REACH:
                        for w in range(width):
                            bias = flows[w] if bias is None else bias + flows[w]
                for b in range(KER):
                    tap = a * KER + b
                    taps_ref[tap * 8 : tap * 8 + 8, :] = totals[b]
            taps_ref[TAPS * 8 : TAPS * 8 + 8, :] = bias
            for c in range(GROUP):
                lanes = pl.ds(pl.multiple_of(g * GROUP * LANES + c * LANES, LANES), LANES)
                total = (
                    taps_ref[pl.ds(c, TAPS + 1, stride=8), :]
                    + taps_ref[pl.ds(GROUP + c, TAPS + 1, stride=8), :]
                )
                sums_ref[0:TAPS, lanes] = total[0:TAPS]
                sums_ref[TERM_ROW : TERM_ROW + 1, lanes] = total[TAPS : TAPS + 1]

    else:
        @pl.loop(0, channels // LANES)
        def _(t):
            lanes = lane_block(t, LANES)
            wide = lane_block(t + base * own_tiles, LANES)
            source = tile_of(base, t, member, share)
            flows = []
            for i in range(images):
                factor = scaled_ref[i : i + 1, wide]
                flow_rows = []
                for h in range(height):
                    centered = mixed_ref[i, h, :, lanes] - mean_ref[i, h]
                    flow = rstd_ref[i, h] * (factor - centered * dot_ref[i, h])
                    flow_ref[i, h, :, lanes] = flow
                    flow_rows.append(flow)
                flows.append(flow_rows)
            bias = flows[0][0]
            for i in range(images):
                for h in range(height):
                    if i or h:
                        bias = bias + flows[i][h]
            taps_ref[TAPS * width : TAPS * width + width, :] = bias
            for b in range(KER):
                totals = [None] * KER
                for i in range(images):
                    moved = [
                        shift_cols(x_ref[i, h, :, source].astype(F32), b - REACH)
                        for h in range(height)
                    ]
                    for a in range(KER):
                        for h in range(max(0, REACH - a), min(height, height + REACH - a)):
                            term = flows[i][h] * moved[h + a - REACH]
                            totals[a] = term if totals[a] is None else totals[a] + term
                for a in range(KER):
                    tap = a * KER + b
                    taps_ref[tap * width : tap * width + width, :] = totals[a]
            rows = TAPS + 1
            total = taps_ref[pl.ds(0, rows, stride=width), :]
            for s in range(1, width):
                total = total + taps_ref[pl.ds(s, rows, stride=width), :]
            sums_ref[0:TAPS, lanes] = total[0:TAPS]
            sums_ref[TERM_ROW : TERM_ROW + 1, lanes] = total[TAPS : TAPS + 1]

    for m in range(channels // share):
        lanes = slice(m * share, (m + 1) * share)
        keep_ref[m] = sums_ref[pl.ds(pl.multiple_of(core * HALF_PAD, HALF_PAD), HALF_PAD), lanes].astype(BF)
        give_ref[m] = sums_ref[pl.ds(pl.multiple_of((1 - core) * HALF_PAD, HALF_PAD), HALF_PAD), lanes].astype(BF)


def terms_block(base, share, place, order, x_here, scaled, rows, mixed, mean, rstd, dots):
    width = x_here.shape[2]
    channels = mixed.shape[3]
    half = SHAPE((channels // share, HALF_PAD, share), BF)
    return pl.pallas_call(
        lambda place_ref, order_ref, *refs: terms_kernel(base, share, place_ref, *refs),
        out_shape=[half, half, SHAPE(mixed.shape, F32)],
        in_specs=[SM, ANY] + [VM] * 7,
        out_specs=[VM] * 3,
        scratch_shapes=[
            pltpu.VMEM((ROWS_PAD, channels), F32),
            pltpu.VMEM(((TAPS + 1) * width, LANES), F32),
            pltpu.VMEM((8, 64, LANES), F32),
            pltpu.VMEM((8, 64, LANES), F32),
            pltpu.VMEM((8, 8, 8, LANES), F32),
            pltpu.VMEM((8, 8, 8, LANES), F32),
        ],
        compiler_params=params(24),
        name="terms_block",
    )(place, order, *near([x_here, scaled, rows, mixed, mean, rstd, dots]))


def images_kernel(image, base, place_ref, flow_own, flow_rest, weight_own, weight_rest, shared_ref, out_ref, token_ref):
    height = flow_own.shape[1]
    share = weight_own.shape[1]
    own_tiles = share // LANES
    step = pl.program_id(0) + base
    token_ref[...] = jnp.zeros_like(token_ref)

    def piece(flow_ref, weight_ref, first):
        @pl.loop(0, own_tiles)
        def _(t):
            lanes = lane_block(t, LANES)
            wide = lane_block(t + step * own_tiles, LANES)
            near_lanes = lane_block(t + (step - first) * own_tiles, LANES)
            rows = [flow_ref[image, h, :, near_lanes] for h in range(height)]
            sums = conv_rows(rows, lambda tap: weight_ref[tap : tap + 1, near_lanes], True)
            for h in range(height):
                out_ref[0, h, :, lanes] = (sums[h] + shared_ref[image : image + 1, wide]).astype(BF)

    if base == 0:

        @pl.when(step == 0)
        def _():
            piece(flow_own, weight_own, 0)

    @pl.when(step != 0)
    def _():
        piece(flow_rest, weight_rest, 1)


def image_block(image, base, count, place, flow, weights, shared, order, out):
    first = out is None
    share = weights[0].shape[1]
    operands = [place, *near([*flow, *weights, shared]), order] + ([] if first else [out])

    def kernel(*refs):
        images_kernel(image, base, *refs[:6], refs[-2], refs[-1])

    return pl.pallas_call(
        kernel,
        grid_spec=pltpu.PrefetchScalarGridSpec(
            num_scalar_prefetch=1,
            grid=(count,),
            in_specs=[VM] * 5 + [ANY] + ([] if first else [HB]),
            out_specs=[
                pl.BlockSpec(
                    (1,) + flow[0].shape[1:3] + (share,),
                    lambda step, place_ref: (image, 0, 0, place_ref[0] ^ (step + base)),
                ),
                pl.BlockSpec((8, LANES), lambda step, place_ref: (0, 0)),
            ],
        ),
        out_shape=[
            SHAPE(flow[0].shape[:3] + (shared.shape[1],), BF),
            SHAPE((8, LANES), F32),
        ],
        input_output_aliases={} if first else {7: 0},
        compiler_params=params(24),
        cost_estimate=cost(1.5),
        name="image_block",
    )(*operands)


def image_cells_kernel(base, place_ref, flow_own, flow_rest, weight_own, weight_rest, shared_ref, out_ref, token_ref, *scratch):
    turn_ref, _, spread_ref, _ = scratch
    own_groups = weight_own.shape[1] // (GROUP * LANES)
    group = pl.program_id(0) + base
    token_ref[...] = jnp.zeros_like(token_ref)

    def one(flow_ref, weight_ref, g):
        for c in range(GROUP):
            lanes = pl.ds(pl.multiple_of(g * GROUP * LANES + c * LANES, LANES), LANES)
            column = weight_ref[:, lanes]
            for i in range(2):
                slot = i * GROUP + c
                spread_ref[slot * WEIGHT_ROWS : (slot + 1) * WEIGHT_ROWS, :] = column
                for h in range(8):
                    turn_ref[h, slot * 8 : slot * 8 + 8, :] = flow_ref[i, h, :, lanes]
        conv_group(scratch, None, True)
        for c in range(GROUP):
            wide = pl.ds(pl.multiple_of(group * GROUP * LANES + c * LANES, LANES), LANES)
            for i in range(2):
                shared = shared_ref[i : i + 1, wide]
                for h in range(8):
                    value = turn_ref[h, pl.ds(i * GROUP + c, 8, stride=8), :]
                    out_ref[i, h, :, c * LANES : (c + 1) * LANES] = (value + shared).astype(BF)

    @pl.when(group < own_groups)
    def _():
        one(flow_own, weight_own, group)

    @pl.when(group >= own_groups)
    def _():
        one(flow_rest, weight_rest, group - own_groups)


def image_cells(base, count, place, flow, weights, shared, order, out):
    first = out is None
    groups = weights[0].shape[1] // (GROUP * LANES)
    images, height, width = flow[0].shape[:3]
    operands = [place, *near([*flow, *weights, shared]), order] + ([] if first else [out])

    def kernel(*refs):
        image_cells_kernel(base, *refs[:6], *refs[-6:])

    def index(step, place_ref):
        group = step + base
        return (0, 0, 0, (place_ref[0] ^ (group // groups)) * groups + group % groups)

    return pl.pallas_call(
        kernel,
        grid_spec=pltpu.PrefetchScalarGridSpec(
            num_scalar_prefetch=1,
            grid=(count,),
            in_specs=[VM] * 5 + [ANY] + ([] if first else [HB]),
            out_specs=[
                pl.BlockSpec((images, height, width, GROUP * LANES), index),
                pl.BlockSpec((8, LANES), lambda step, place_ref: (0, 0)),
            ],
            scratch_shapes=conv_scratch(),
        ),
        out_shape=[
            SHAPE((images, height, width, shared.shape[1]), BF),
            SHAPE((8, LANES), F32),
        ],
        input_output_aliases={} if first else {7: 0},
        compiler_params=params(24),
        cost_estimate=cost(1.5),
        name="image_cells",
    )(*operands)


def head_grads_kernel(block, packed_low, packed_high, text_ref, order_ref, head_ref, text_grad_ref, token_ref):
    share = packed_low.shape[1] - 2 * text_ref.shape[1]
    width = text_ref.shape[1]
    step = pl.program_id(0)
    lanes = lane_block(step, block)
    grads = slice(share, share + width)
    images = jnp.concatenate([packed_low[:, lanes], packed_high[:, lanes]], axis=0)
    grad = jnp.concatenate([packed_low[:, grads], packed_high[:, grads]], axis=0)
    head_ref[...] = lax.dot_general(
        images, grad, (((0,), (0,)), ((), ())), preferred_element_type=F32
    )

    @pl.when(step == 0)
    def _():
        token_ref[...] = jnp.zeros_like(token_ref)
        units = slice(share + width, share + 2 * width)
        unit_all = jnp.concatenate([packed_low[:, units], packed_high[:, units]], axis=0)
        raw = text_ref[...].astype(F32)
        inverse = inverse_norm(raw)
        unit = raw * inverse
        pairs = pair_weights(unit_all, unit.astype(BF))
        text_sum = LOGIT_SCALE * lax.dot_general(
            pairs, unit_all, (((0,), (0,)), ((), ())), preferred_element_type=F32
        )
        text_grad_ref[...] = unit_back(unit, inverse, text_sum)


def head_grads_block(packed, text_here, share, order):
    rows, width = text_here.shape
    block = 768 if share % 768 == 0 else LANES
    return pl.pallas_call(
        lambda *refs: head_grads_kernel(block, *refs),
        grid=(share // block,),
        out_shape=[
            SHAPE((share, width), F32),
            SHAPE((rows, width), F32),
            SHAPE((8, LANES), F32),
        ],
        in_specs=[VM, VM, VM, ANY],
        out_specs=[
            pl.BlockSpec((block, width), lambda step: (step, 0)),
            pl.BlockSpec((rows, width), lambda step: (0, 0)),
            pl.BlockSpec((8, LANES), lambda step: (0, 0)),
        ],
        compiler_params=params(24),
        name="head_grads_block",
    )(*near([*packed, text_here]), order)


def split_kernel(place_ref, own_ref, other_ref, kernel_ref, term_ref):
    core = place_ref[1]
    rest = TAPS - HALF_PAD
    terms = slice(TERM_ROW - HALF_PAD, TERM_ROW - HALF_PAD + 4)

    def write(low_ref, high_ref):
        kernel_ref[0:HALF_PAD, :] = low_ref[...].astype(F32)
        high = high_ref[...].astype(F32)
        kernel_ref[HALF_PAD:TAPS, :] = high[0:rest]
        term_ref[...] = high[terms]

    @pl.when(core == 0)
    def _():
        write(own_ref, other_ref)

    @pl.when(core != 0)
    def _():
        write(other_ref, own_ref)


def split_block(place, own, other):
    share = own.shape[1]
    return pl.pallas_call(
        split_kernel,
        out_shape=[SHAPE((TAPS, share), F32), SHAPE((4, share), F32)],
        in_specs=[SM, VM, VM],
        out_specs=[VM, VM],
        compiler_params=params(24),
        name="split_block",
    )(place, *near([own, other]))


def per_device(image_maps, dw_kernel, channel_terms, head_weight, text_feats):
    members = lax.axis_size("fsdp")
    member = lax.axis_index("fsdp")
    core = lax.axis_index("dp") % 2
    place = jnp.stack([member, core]).astype(jnp.int32)
    others = range(1, members)
    dp_masks = bits_up(lax.axis_size("dp"))
    down = dp_masks[::-1]
    share = head_weight.shape[0]

    kernels = [swap(dw_kernel, "fsdp", m) for m in others]
    text_core = swap(text_feats, "dp", 1)
    x_here, weight_own, text_here = load_block(image_maps, dw_kernel, channel_terms, text_feats)
    pack_own = pack_block(weight_own, text_here, text_core)
    packs = [swap(pack_own, "fsdp", m) for m in others]
    mixed_own, sum_own = own_block(place, x_here, weight_own)

    text_rows = text_stack(text_here, text_core, packs, sum_own)
    text_masks = down[:-1]
    pieces, head_here, weight_rest, mixed_rest, saved = forward_block(
        place, head_weight, x_here, (mixed_own, sum_own, weight_own), text_rows, kernels, packs
    )
    weights = (weight_own, weight_rest)
    far_rows = swap(text_rows, "dp", text_masks[0])
    pieces = [pieces[0]] + [swap(pieces[m], "fsdp", m) for m in others]
    group, partial = head_project(pieces, head_here)
    orders = [saved[4]] + [partial] * len(text_masks)
    for mask, order in zip(text_masks[1:], orders):
        text_rows = stack_rows(text_rows, far_rows, order)
        far_rows = swap(text_rows, "dp", mask)
    texts = (text_rows, far_rows)

    partials = [partial] + [swap(partial, "fsdp", m) for m in others]
    packed, grads = loss_block(members, embed_sum(partials), texts, group, head_here)
    grads = [grads[0]] + [swap(grads[m], "fsdp", m) for m in others]

    mean, rstd, hatsum, hat, hrstd = saved
    cells = image_maps.shape[1] * image_maps.shape[2]
    shared, scaled, term_rows = pool_grad_block(grads, cells, weights, hatsum, hat, hrstd)
    mixed = (mixed_own, mixed_rest)
    dots = dots_block(scaled, mixed, mean, rstd)
    gather_masks = [down[1], down[0]] + list(down[2:])
    moving = swap(packed, "dp", gather_masks.pop(0))

    def terms_part(base, mixed_part, order):
        return terms_block(
            base, share, place, order, x_here, scaled, term_rows, mixed_part, mean, rstd, dots
        )

    packed = stack_rows(packed, moving, dots)
    keep_rest, give_rest, flow_rest = terms_part(1, mixed_rest, packed)
    keep_own, give_own, flow_own = terms_part(0, mixed_own, keep_rest)
    flow = (flow_own, flow_rest)

    fits = cells_fit(*image_maps.shape[:3], share)
    image_grads = None
    if fits:
        groups = image_maps.shape[3] // (GROUP * LANES)
        edges = [0, groups // 6, groups // 2, groups]
        parts = [(low, high - low) for low, high in zip(edges, edges[1:]) if high > low]
    else:
        parts = [(image, base) for image in range(image_maps.shape[0]) for base in (0, members // 2)]

    def image_parts(count, order, image_grads):
        token = order
        for _ in range(min(count, len(parts))):
            first, second = parts.pop(0)
            if fits:
                image_grads, token = image_cells(
                    first, second, place, flow, weights, shared, order, image_grads
                )
            else:
                image_grads, token = image_block(
                    first, second, members // 2, place, flow, weights, shared, order, image_grads
                )
        return image_grads, token

    chip = chip_sums(keep_rest, swap(give_rest, "dp", 1), keep_own)
    chip_own = chip_sums(keep_own, swap(give_own, "dp", 1), chip[0])[0]
    image_grads, token = image_parts(1, chip[0], None)
    packed = hold(packed, token)
    moving = swap(packed, "dp", gather_masks.pop(0))
    sent = add_all([chip_own] + [swap(chip[m - 1], "fsdp", m) for m in others], token)
    ring_masks = dp_masks[1:]
    counts = [1] + [2] * len(ring_masks)
    for mask, count in zip(ring_masks[:-1], counts):
        image_grads, token = image_parts(count, sent, image_grads)
        if mask == ring_masks[0]:
            packed = stack_rows(packed, moving, token)
            moving = swap(packed, "dp", gather_masks.pop(0))
        sent = add_all([sent, swap(sent, "dp", mask)], token)
    image_grads, token = image_parts(len(parts), sent, image_grads)
    while gather_masks:
        packed = stack_rows(packed, moving, token)
        moving = swap(packed, "dp", gather_masks.pop(0))
    head_grads, text_grads, token = head_grads_block((packed, moving), text_here, share, sent)
    sent = add_all([sent, swap(sent, "dp", ring_masks[-1])], token)
    kernel_grads, term_grads = split_block(place, sent, swap(sent, "dp", 1))
    return (image_grads, kernel_grads, term_grads, head_grads, text_grads)


def solution(mesh):
    in_specs = (
        P(("dp", "fsdp"), None, None, None),
        P(None, "fsdp"),
        P(None, "fsdp"),
        P("fsdp", None),
        P(("dp", "fsdp"), None),
    )
    out_specs = (
        P(("dp", "fsdp"), None, None, None),
        P(None, "fsdp"),
        P(None, "fsdp"),
        P("fsdp", None),
        P(("dp", "fsdp"), None),
    )
    return jax.shard_map(
        per_device, mesh=mesh, in_specs=in_specs, out_specs=out_specs, check_vma=False
    )
```
